32 devices in a mesh: batch: 8 (over y, x, core), head: 4 (over z).
Axes of the slice: x: 2, y: 2, z: 4, core: 2. Of those that a mesh axis runs over, the one named last changes fastest.
Arguments:
- tokens: bfloat16 [16384, 1152], P('batch'), may hold values from -6 to 6
- segments: int32 [16384], P('batch'), may hold values from 0 to 39, as said below
- item_cond: int32 [40], replicated, may hold values from 0 to 63
- condition: bfloat16 [64, 1152], replicated, may hold values from -6 to 6
- ada_weight: bfloat16 [1152, 6912], P(None, 'head'), may hold values from -0.1875 to 0.1875
- ada_bias: bfloat16 [6912], P('head'), may hold values from -3 to 3
- qkv_weight: bfloat16 [1152, 3456], P(None, 'head'), may hold values from -0.1875 to 0.1875
- qv_bias: bfloat16 [2304], P('head'), may hold values from -2 to 2
- proj_weight: bfloat16 [1152, 1152], P('head'), may hold values from -1.5 to 1.5
- proj_bias: bfloat16 [1152], replicated, may hold values from -2 to 2
- in_weight: bfloat16 [1152, 4608], P(None, 'head'), may hold values from -0.1875 to 0.1875
- in_bias: bfloat16 [4608], P('head'), may hold values from -2 to 2
- out_weight: bfloat16 [4608, 1152], P('head'), may hold values from -0.09375 to 0.09375
- out_bias: bfloat16 [1152], replicated, may hold values from -3 to 3
- cotangent: bfloat16 [16384, 1152], P('batch'), may hold values from -6 to 6
Outputs:
- block_out: bfloat16 [16384, 1152], P('batch', 'head')
- tokens_grad: bfloat16 [16384, 1152], P('batch', 'head')
- condition_grad: float32 [64, 1152], replicated
- ada_weight_grad: float32 [1152, 6912], P(None, 'head')
- ada_bias_grad: float32 [6912], P('head')
- qkv_weight_grad: float32 [1152, 3456], P(None, 'head')
- qv_bias_grad: float32 [2304], P('head')
- proj_weight_grad: float32 [1152, 1152], P('head')
- proj_bias_grad: float32 [1152], replicated
- in_weight_grad: float32 [1152, 4608], P(None, 'head')
- in_bias_grad: float32 [4608], P('head')
- out_weight_grad: float32 [4608, 1152], P('head')
- out_bias_grad: float32 [1152], replicated
The draws below stay inside these ranges and needn't reach their ends.
Inputs may be any that keep to these rules, and one draw needn't show every extreme that they name: Tokens come in packed rows of 1024; each row holds either one segment or four segments of 256 tokens, and the 2 rows of each batch index hold 1 of each kind. Segment numbers never fall along the tokens and every number occurs.
All inputs are finite; a program needn't handle non-finite values.
Results may differ from the reference program's by a relative error of at most 0.02.
Values may be sent and summed in bfloat16 or wider, within the bound.
No kernel may reach another device: no remote copies, remote signals or barrier semaphores. Data moves between devices by JAX's collectives and lax.ppermute only.
A program may use at most 256 MiB of HBM per device.

```python
import math
import jax
import jax.numpy as jnp
from jax import lax

D = 1152
HEAD_DIM = 72
FF = 4608
SEQ = 1024
ROWS_DEV = 2
CONDS = 64
TOKENS = 16384
SEGS = 40
N_HEAD = 4


def draw_segments(key, part):
    group_count = TOKENS // (ROWS_DEV * SEQ)
    group_keys = jax.random.split(key, group_count)

    def row_order(one_key):
        return jax.random.permutation(one_key, ROWS_DEV)
    orders = jax.vmap(row_order)(group_keys)
    split_rows = (orders < ROWS_DEV // 2).astype(jnp.int32).reshape(-1)
    row_counts = 1 + 3 * split_rows
    row_starts = jnp.cumsum(row_counts) - row_counts
    position = jnp.arange(SEQ, dtype=jnp.int32)
    local_index = position[None, :] // (SEQ // 4) * split_rows[:, None]
    return (row_starts[:, None] + local_index).reshape(-1).astype(jnp.int32)


def set_ends(array, own_key, least, largest):
    longest = array.shape.index(max(array.shape))
    spots = []
    for shift in (0, 1):
        where = [jax.random.randint(jax.random.fold_in(own_key, axis), (), 0, length) for axis, length in enumerate(array.shape)]
        where[longest] = (where[longest] + shift) % array.shape[longest]
        spots.append(tuple(where))
    return array.at[spots[0]].set(least).at[spots[1]].set(largest)


def block_levels(own_key, extent, shards, least, high):
    def one(axis_at, blocks):
        draws = jax.random.uniform(jax.random.fold_in(jax.random.fold_in(own_key, 6), axis_at), (blocks,), jnp.float32, least / len(shards), high / len(shards))
        return jnp.repeat(jnp.exp(draws), extent[axis_at] // blocks).reshape((-1,) + (1,) * (len(extent) - axis_at - 1))

    gain = one(*shards[0])
    for cut in shards[1:]:
        gain = gain * one(*cut)
    return gain


def scatter_about(stream_key, shape, deviation, limit, cuts=(), held_as=jnp.bfloat16):
    drawn = jax.random.normal(stream_key, shape, jnp.float32) * deviation
    if len(cuts) > 0:
        drawn = block_levels(stream_key, shape, cuts, -0.22, 0.18) * drawn
    return jnp.clip(drawn, min=-limit, max=limit).astype(held_as)


def setup_inputs(seed: int = 0) -> dict:
    key_of = jax.random.split(jax.random.key(seed), 16)
    return {
        "tokens": scatter_about(key_of[0], (TOKENS, D), 1.0, 6.0, ((0, 8),)),
        "segments": draw_segments(jax.random.fold_in(key_of[15], 71), 0),
        "item_cond": set_ends(jax.random.randint(key_of[2], (SEGS,), 0, CONDS), jax.random.fold_in(key_of[2], 1), 0, CONDS - 1).astype(jnp.int32),
        "condition": scatter_about(key_of[3], (CONDS, D), 1.0, 6.0),
        "ada_weight": scatter_about(key_of[4], (D, 6 * D), D ** -0.5, 0.1875, ((1, 4),)),
        "ada_bias": scatter_about(key_of[5], (6 * D,), 0.5, 3.0, ((0, 4),)),
        "qkv_weight": scatter_about(key_of[6], (D, 3 * D), D ** -0.5, 0.1875, ((1, 4),)),
        "qv_bias": scatter_about(key_of[7], (2 * D,), 0.3, 2.0, ((0, 4),)),
        "proj_weight": scatter_about(key_of[8], (D, D), (D // 64) ** -0.5, 1.5, ((0, 4),)),
        "proj_bias": scatter_about(key_of[9], (D,), 0.3, 2.0),
        "in_weight": scatter_about(key_of[10], (D, FF), D ** -0.5, 0.1875, ((1, 4),)),
        "in_bias": scatter_about(key_of[11], (FF,), 0.3, 2.0, ((0, 4),)),
        "out_weight": scatter_about(key_of[12], (FF, D), FF ** -0.5, 0.09375, ((0, 4),)),
        "out_bias": scatter_about(key_of[13], (D,), 0.5, 3.0),
        "cotangent": scatter_about(key_of[14], (TOKENS, D), 1.0, 6.0, ((0, 8),)),
    }


@jax.custom_vjp
def low(v):
    return lax.optimization_barrier(v.astype(jnp.bfloat16)).astype(jnp.float32)

@jax.custom_vjp
def low_back(v):
    return v

def low_keep(v):
    return (low(v), None)

def low_pass(kept, grad):
    return (grad,)

def back_keep(v):
    return (v, None)

def back_low(kept, grad):
    return (low(grad),)
low.defvjp(low_keep, low_pass)
low_back.defvjp(back_keep, back_low)
norm_eps = 1e-06
neg_large = -1e+30
gelu_coeff = 0.7978845608028654

def matmul(left_side, right_side):
    return jnp.dot(left_side, right_side, precision=lax.Precision.HIGHEST, preferred_element_type=jnp.float32)

def grouped_product(left_side, right_side):
    groups = N_HEAD
    left_groups = left_side.reshape(left_side.shape[0], groups, -1)
    right_groups = right_side.reshape(groups, -1, right_side.shape[1])
    terms = jnp.einsum('tgf,gfd->gtd', left_groups, right_groups, precision=lax.Precision.HIGHEST)
    return lax.optimization_barrier(jnp.sum(low(terms), axis=0))

def row_norm(values):
    center = lax.optimization_barrier(jnp.mean(values, axis=-1, keepdims=True))
    shifted = values - center
    spread = lax.optimization_barrier(jnp.mean(shifted * shifted, axis=-1, keepdims=True))
    return shifted * lax.rsqrt(spread + norm_eps)

def gelu_tanh(values):
    inner = gelu_coeff * (values + 0.044715 * values * values * values)
    return 0.5 * values * (1.0 + jnp.tanh(inner))

def silu_act(values):
    return values / (1.0 + jnp.exp(-values))

def attend(block_data):
    queries, key_rows, value_rows, seg_row = block_data
    same_segment = seg_row[:, None] == seg_row[None, :]
    raw_scores = jnp.einsum('qhd,khd->hqk', queries, key_rows, precision=lax.Precision.HIGHEST)
    scores = jnp.where(same_segment[None], low_back(raw_scores) * (1.0 / math.sqrt(HEAD_DIM)), neg_large)
    row_peak = lax.optimization_barrier(jnp.max(scores, axis=-1, keepdims=True))
    exp_scores = jnp.exp(scores - row_peak)
    probs = exp_scores / lax.optimization_barrier(jnp.sum(exp_scores, axis=-1, keepdims=True))
    mixed_heads = jnp.einsum('hqk,khd->qhd', low(probs), value_rows, precision=lax.Precision.HIGHEST)
    return mixed_heads.reshape(mixed_heads.shape[0], -1)

def block_fn(params, mod_table, tokens_f, token_class, seg_rows):
    qkv_weight, qv_bias, proj_weight, proj_bias, in_weight, in_bias, out_weight, out_bias = params
    feature_width = tokens_f.shape[1]
    all_mods = jnp.take(mod_table, token_class, axis=0)
    shift_one = all_mods[:, 0:feature_width]
    scale_one = all_mods[:, feature_width:2 * feature_width]
    gate_one = all_mods[:, 2 * feature_width:3 * feature_width]
    shift_two = all_mods[:, 3 * feature_width:4 * feature_width]
    scale_two = all_mods[:, 4 * feature_width:5 * feature_width]
    gate_two = all_mods[:, 5 * feature_width:6 * feature_width]
    normed_one = row_norm(tokens_f)
    attn_in = low(normed_one * (1.0 + scale_one) + shift_one)
    heads_here = qv_bias.shape[0] // (2 * HEAD_DIM)
    bias_pairs = qv_bias.reshape(heads_here, 2, HEAD_DIM)
    zero_keys = jnp.zeros((heads_here, 1, HEAD_DIM), jnp.float32)
    full_bias = jnp.concatenate([bias_pairs[:, :1], zero_keys, bias_pairs[:, 1:]], axis=1).reshape(-1)
    projected = low(low_back(matmul(attn_in, qkv_weight) + full_bias))
    packed_rows = seg_rows.shape[0]
    grouped = projected.reshape(packed_rows, SEQ, heads_here, 3, HEAD_DIM)
    mixed_rows = lax.map(jax.checkpoint(attend), (grouped[:, :, :, 0], grouped[:, :, :, 1], grouped[:, :, :, 2], seg_rows))
    mixed = low(low_back(mixed_rows.reshape(tokens_f.shape[0], feature_width)))
    attn = low_back(grouped_product(mixed, proj_weight) + proj_bias)
    stream = tokens_f + low_back(gate_one * attn)
    normed_two = row_norm(low(stream))
    mlp_in = low(normed_two * (1.0 + scale_two) + shift_two)
    hidden = low(gelu_tanh(low_back(matmul(mlp_in, in_weight) + in_bias)))
    mlp_out = low_back(grouped_product(hidden, out_weight) + out_bias)
    return stream + gate_two * mlp_out

def table_fn(cond_in, ada_w, ada_b):
    return low_back(matmul(low(silu_act(cond_in)), ada_w) + ada_b)

def reference(tokens, segments, item_cond, condition, ada_weight, ada_bias, qkv_weight, qv_bias, proj_weight, proj_bias, in_weight, in_bias, out_weight, out_bias, cotangent):
    mod_table, table_back = jax.vjp(table_fn, condition.astype(jnp.float32), ada_weight.astype(jnp.float32), ada_bias.astype(jnp.float32))
    params = (qkv_weight.astype(jnp.float32), qv_bias.astype(jnp.float32), proj_weight.astype(jnp.float32), proj_bias.astype(jnp.float32), in_weight.astype(jnp.float32), in_bias.astype(jnp.float32), out_weight.astype(jnp.float32), out_bias.astype(jnp.float32))
    token_class = jnp.take(item_cond, segments, axis=0).astype(jnp.int32)
    step_rows = 2
    block_count = tokens.shape[0] // (step_rows * SEQ)
    feature_width = tokens.shape[1]
    token_blocks = tokens.astype(jnp.float32).reshape(block_count, step_rows * SEQ, feature_width)
    grad_blocks = cotangent.astype(jnp.float32).reshape(block_count, step_rows * SEQ, feature_width)
    class_blocks = token_class.reshape(block_count, step_rows * SEQ)
    seg_blocks = segments.reshape(block_count, step_rows, SEQ)

    def advance(carry, block_data):
        param_grads, table_grad = carry
        token_part, grad_part, class_part, seg_part = block_data

        def apply_block(prm, table_in, tok_in):
            return block_fn(prm, table_in, tok_in, class_part, seg_part)
        out_part, pullback = jax.vjp(apply_block, params, mod_table, token_part)
        grad_params, grad_table, grad_tokens = pullback(grad_part)
        new_grads = jax.tree.map(jnp.add, param_grads, grad_params)
        return ((new_grads, table_grad + grad_table), (out_part.astype(jnp.bfloat16), grad_tokens.astype(jnp.bfloat16)))
    start_grads = (jax.tree.map(jnp.zeros_like, params), jnp.zeros_like(mod_table))
    final_grads, outputs = lax.scan(advance, start_grads, (token_blocks, grad_blocks, class_blocks, seg_blocks))
    param_grads, table_grad = final_grads
    block_out = outputs[0].reshape(tokens.shape[0], feature_width)
    tokens_grad = outputs[1].reshape(tokens.shape[0], feature_width)
    condition_grad, ada_weight_grad, ada_bias_grad = table_back(table_grad)
    return (block_out, tokens_grad, condition_grad, ada_weight_grad, ada_bias_grad, param_grads[0], param_grads[1], param_grads[2], param_grads[3], param_grads[4], param_grads[5], param_grads[6], param_grads[7])
```

```python
import functools
import math

import jax
import jax.numpy as jnp
from jax import lax
from jax.experimental import pallas as pl
from jax.experimental.pallas import tpu as pltpu
from jax.sharding import PartitionSpec as P

HEAD_DIM = 72
SEQ = 1024
LOG2E = 1.4426950408889634
KEY_SCALE = 1.0 / math.sqrt(HEAD_DIM)


def nt(a, b):
    return lax.dot_general(a, b, (((1,), (1,)), ((), ())), preferred_element_type=jnp.float32)


def nn(a, b):
    return lax.dot_general(a, b, (((1,), (0,)), ((), ())), preferred_element_type=jnp.float32)


def attend_kernel(heads, chunk, groups, split, proj_ref, mixed_ref, lse_ref):
    seq = proj_ref.shape[1]
    home = seq // groups
    group = lax.axis_index("head")
    width = 3 * HEAD_DIM
    key_count = chunk if split else seq

    def part(head, start):
        at = head * width
        rows = pl.ds(start, chunk)
        keys = pl.ds(start if split else 0, key_count)
        queries = proj_ref[0, rows, at : at + HEAD_DIM]
        key_rows = proj_ref[0, keys, at + HEAD_DIM : at + 2 * HEAD_DIM]
        value_rows = proj_ref[0, keys, at + 2 * HEAD_DIM : at + 3 * HEAD_DIM]
        scores = nt(key_rows, queries)
        peak = jnp.max(scores, axis=0, keepdims=True)
        weights = jnp.exp2((scores - peak) * (KEY_SCALE * LOG2E))
        total = jnp.sum(weights, axis=0, keepdims=True)
        mixed_t = nn(value_rows.T, weights.astype(jnp.bfloat16)) / total
        lse_ref[0, head : head + 1, rows] = peak * (KEY_SCALE * LOG2E) + jnp.log2(total)
        return mixed_t.T

    def step(index, _):
        start = pl.multiple_of(index * chunk, chunk)
        outs = [part(head, start) for head in range(heads)]
        outs = jnp.concatenate(outs, axis=1).astype(jnp.bfloat16)
        for spot in range(chunk // home):
            target = index * (chunk // home) + spot
            mixed_ref[(group - target + groups) % groups, 0] = outs[spot * home : (spot + 1) * home]
        return 0

    lax.fori_loop(0, seq // chunk, step, 0)


def attend(projected, row, heads, chunk, groups, order):
    seq, width = projected.shape[1:]
    split = row == 0
    return call(
        functools.partial(attend_kernel, heads, chunk, groups, split),
        [
            shape_of((groups, 1, seq // groups, heads * HEAD_DIM), jnp.bfloat16),
            shape_of((1, heads, seq), jnp.float32),
        ],
        [pl.BlockSpec((1, seq, width), lambda i: (row, 0, 0))],
        [
            pl.BlockSpec((groups, 1, seq // groups, heads * HEAD_DIM), lambda i: (0, 0, 0, 0)),
            pl.BlockSpec((1, heads, seq), lambda i: (0, 0, 0)),
        ],
        grid=(1,),
        name="attend_split" if split else "attend_whole",
        micros=6 if split else 16,
        order=order,
    )(projected)


def attend_back_kernel(heads, chunk, groups, split, proj_ref, lse_ref, pieces_ref, out_ref, dk_ref, dv_ref, grad_ref):
    seq = proj_ref.shape[1]
    home = seq // groups
    group = lax.axis_index("head")
    width = 3 * HEAD_DIM
    key_count = chunk if split else seq
    for spot in range(groups):
        grad_ref[spot * home : (spot + 1) * home, :] = pieces_ref[(group - spot + groups) % groups, 0]

    def part(head, start):
        at = head * width
        rows = pl.ds(start, chunk)
        keys = pl.ds(start if split else 0, key_count)
        queries = proj_ref[0, rows, at : at + HEAD_DIM]
        key_rows = proj_ref[0, keys, at + HEAD_DIM : at + 2 * HEAD_DIM]
        value_rows = proj_ref[0, keys, at + 2 * HEAD_DIM : at + 3 * HEAD_DIM]
        grads = grad_ref[rows, head * HEAD_DIM : (head + 1) * HEAD_DIM]
        scores = nt(key_rows, queries)
        probs = jnp.exp2(scores * (KEY_SCALE * LOG2E) - lse_ref[0, head : head + 1, rows])
        grad_probs = nt(value_rows, grads)
        inner = jnp.sum(probs * grad_probs, axis=0, keepdims=True)
        grad_raw = (probs * (grad_probs - inner) * KEY_SCALE).astype(jnp.bfloat16)
        grad_values = nn(probs.astype(jnp.bfloat16), grads)
        grad_keys = nn(grad_raw, queries)
        grad_queries = nn(key_rows.T, grad_raw).T
        return grad_queries, grad_keys, grad_values

    if not split:
        for head in range(heads):
            at = head * width
            dk_ref[...] = jnp.zeros_like(dk_ref)
            dv_ref[...] = jnp.zeros_like(dv_ref)

            def step(index, _):
                start = pl.multiple_of(index * chunk, chunk)
                dq, dk, dv = part(head, start)
                out_ref[0, pl.ds(start, chunk), at : at + HEAD_DIM] = dq.astype(jnp.bfloat16)
                dk_ref[...] += dk
                dv_ref[...] += dv
                return 0

            lax.fori_loop(0, seq // chunk, step, 0)
            both = jnp.concatenate([dk_ref[...], dv_ref[...]], axis=1).astype(jnp.bfloat16)
            out_ref[0, :, at + HEAD_DIM : at + 3 * HEAD_DIM] = both
    else:

        def step(index, _):
            start = pl.multiple_of(index * chunk, chunk)
            outs = [t for head in range(heads) for t in part(head, start)]
            out_ref[0, pl.ds(start, chunk), :] = jnp.concatenate(outs, axis=1).astype(jnp.bfloat16)
            return 0

        lax.fori_loop(0, seq // chunk, step, 0)


def attend_back(projected, row, lse, grads, heads, chunk, groups, order):
    seq, width = projected.shape[1:]
    split = row == 0

    return call(
        functools.partial(attend_back_kernel, heads, chunk, groups, split),
        shape_of((1, seq, width), jnp.bfloat16),
        [
            pl.BlockSpec((1, seq, width), lambda i: (row, 0, 0)),
            pl.BlockSpec((1, heads, seq), lambda i: (0, 0, 0)),
            pl.BlockSpec((groups, 1, seq // groups, heads * HEAD_DIM), lambda i: (0, 0, 0, 0)),
        ],
        pl.BlockSpec((1, seq, width), lambda i: (0, 0, 0)),
        grid=(1,),
        scratch=[pltpu.VMEM((seq, HEAD_DIM), jnp.float32)] * 2
        + [pltpu.VMEM((seq, heads * HEAD_DIM), jnp.bfloat16)],
        name="attend_back_split" if split else "attend_back_whole",
        micros=8 if split else 24,
        order=order,
    )(projected, lse, grads)


norm_eps = 1e-06
gelu_coeff = 0.7978845608028654
VMEM_BYTES = 58 * 1024 * 1024
UNIT_TILE = 384


def tn(left_side, right_side):
    return lax.dot_general(
        left_side, right_side, (((0,), (0,)), ((), ())), preferred_element_type=jnp.float32
    )


def row_norm(values):
    center = jnp.mean(values, axis=-1, keepdims=True)
    shifted = values - center
    spread = jnp.mean(shifted * shifted, axis=-1, keepdims=True)
    inverse = lax.rsqrt(spread + norm_eps)
    return (shifted * inverse, inverse)


def norm_back(normed, inverse, grad_normed):
    first_mean = jnp.mean(grad_normed, axis=-1, keepdims=True)
    second_mean = jnp.mean(grad_normed * normed, axis=-1, keepdims=True)
    return inverse * (grad_normed - first_mean - normed * second_mean)


def silu_act(values):
    return values / (1.0 + jnp.exp(-values))


def weight_of(micros):
    return pl.CostEstimate(flops=0, bytes_accessed=int(micros * 3.3e6), transcendentals=0)


def call(kernel, out_shape, in_specs, out_specs, grid=(), prefetch=0, scratch=(), name=None, micros=1, order=()):
    first = prefetch + len(in_specs)

    def ordered(*refs):
        kernel(*refs[:first], *refs[first + len(order) :])

    run = pl.pallas_call(
        ordered if order else kernel,
        grid_spec=pltpu.PrefetchScalarGridSpec(
            num_scalar_prefetch=prefetch,
            grid=grid,
            in_specs=list(in_specs) + [pl.BlockSpec(memory_space=pl.ANY)] * len(order),
            out_specs=out_specs,
            scratch_shapes=scratch,
        ),
        out_shape=out_shape,
        compiler_params=pltpu.CompilerParams(vmem_limit_bytes=VMEM_BYTES),
        cost_estimate=weight_of(micros),
        name=name,
    )
    return lambda *arrays: run(*arrays, *order)


def hold(values, *order):
    run = pl.pallas_call(
        lambda *refs: None,
        in_specs=[pl.BlockSpec(memory_space=pl.ANY)] * (1 + len(order)),
        out_specs=pl.BlockSpec(memory_space=pl.ANY),
        out_shape=shape_of(values.shape, values.dtype),
        input_output_aliases={0: 0},
        name="hold",
    )
    return run(values, *order)


def whole(shape):
    return pl.BlockSpec(shape, lambda *_: (0,) * len(shape))


SCALARS = pl.BlockSpec(memory_space=pltpu.SMEM)
shape_of = jax.ShapeDtypeStruct


class Links:
    def __init__(self, heads, batches):
        self.heads = heads
        self.batches = batches
        bits = batches.bit_length() - 1
        self.levels = bits - 1
        first = list(range(bits - 1, 0, -1))
        self.orders = (first, first[1:] + first[:1])

    def fetch(self, values, distance):
        count = self.heads
        return lax.ppermute(values, "head", [((i + distance) % count, i) for i in range(count)])

    def send(self, values, distance):
        count = self.heads
        return lax.ppermute(values, "head", [(i, (i + distance) % count) for i in range(count)])

    def core_swap(self, values):
        return lax.ppermute(values, "batch", [(i, i ^ 1) for i in range(self.batches)])

    def link_swap(self, values, level):
        pairs = [(i, i ^ (1 << self.orders[i & 1][level])) for i in range(self.batches)]
        return lax.ppermute(values, "batch", pairs)

    def owner(self, spot):
        batch = lax.axis_index("batch")
        half = spot >> self.levels
        masks = [
            sum(1 << order[level] for level in range(self.levels) if spot >> level & 1)
            for order in self.orders
        ]
        mask = jnp.where(batch % 2 == half, masks[0], masks[1])
        return (batch ^ half) ^ mask

    def place(self, index):
        batch = lax.axis_index("batch")
        way = batch ^ index
        half = way & 1
        spots = [
            sum(((way >> order[level]) & 1) << level for level in range(self.levels))
            for order in self.orders
        ]
        return (half << self.levels) + jnp.where((batch & 1) == half, spots[0], spots[1])

    def gather_levels(self, values, order=()):
        pieces = [values]
        for level in range(self.levels):
            joined = pieces[0] if level == 0 else jnp.concatenate(pieces, axis=0)
            more = self.link_swap(joined, level)
            if level == 0 and order:
                more = hold(more, *order)
            pieces = [joined, more]
        return pieces

    def gather_batch(self, values):
        own = jnp.concatenate(self.gather_levels(values), axis=0)
        return jnp.concatenate([own, self.core_swap(own)], axis=0)

    def reduce_levels(self, kept, orders=()):
        low = jnp.bfloat16
        steps = []
        for level in reversed(range(self.levels)):
            more = self.link_swap(kept[1], level)
            if len(orders) > len(steps):
                more = hold(more, orders[len(steps)])
            total = (kept[0].astype(jnp.float32) + more.astype(jnp.float32)).astype(low)
            half = total.shape[0] // 2
            kept = [total[:half], total[half:]]
            steps.append(total)
        return steps

    def by_owner(self, values):
        return jnp.concatenate(
            [lax.dynamic_index_in_dim(values, self.owner(i), 0) for i in range(self.batches)]
        )

    def by_index(self, values):
        return jnp.concatenate(
            [lax.dynamic_index_in_dim(values, self.place(i), 0) for i in range(self.batches)]
        )

    def at_head(self, distance):
        return (lax.axis_index("head") + distance) % self.heads


def mod_kernel(quarter, units_here, seg_ref, item_ref, cond_ref, ada_ref, bias_ref, in_bias_ref, table_ref, info_ref):
    starts = [[seg_ref[row * SEQ + spot * quarter] for spot in range(4)] for row in range(2)]
    first_splits = starts[0][0] != starts[0][3]
    ids = [jnp.where(first_splits, starts[1][0], starts[0][0])] + [
        jnp.where(first_splits, starts[0][spot], starts[1][spot]) for spot in range(4)
    ]
    classes = [item_ref[one] for one in ids]
    info_ref[0] = jnp.where(first_splits, 0, 1)
    info_ref[1] = lax.axis_index("head")
    info_ref[2] = 0
    for spot in range(5):
        info_ref[3 + spot] = classes[spot]
    cond_low = silu_act(cond_ref[...].astype(jnp.float32)).astype(jnp.bfloat16)
    count = cond_low.shape[0]
    row_spot = lax.broadcasted_iota(jnp.int32, (8, count), 0)
    wanted = jnp.full((8, count), count, jnp.int32)
    for spot in range(5):
        wanted = jnp.where(row_spot == spot, classes[spot], wanted)
    hits = (lax.broadcasted_iota(jnp.int32, (8, count), 1) == wanted).astype(jnp.float32)
    rows = nn(hits.astype(jnp.bfloat16), cond_low).astype(jnp.bfloat16)
    table_ref[...] = nt(rows, ada_ref[...]) + bias_ref[...]
    table_ref[5:6, :units_here] = in_bias_ref[...]


def project_kernel(heads, quarter, info_ref, table_rel_ref, tokens_ref, weight_ref, bias_ref, attn_in_ref, projected_ref, table_ref):
    block = pl.program_id(0)
    width = tokens_ref.shape[1]
    columns = table_rel_ref.shape[2]

    @pl.when(block == 0)
    def _():
        for head in range(heads):
            spot = (head - lax.axis_index("head") + heads) % heads
            table_ref[:, head * columns : (head + 1) * columns] = table_rel_ref[spot]

    row = jnp.where(block < 4, 1 + block % 4, 0)
    normed, _ = row_norm(tokens_ref[...].astype(jnp.float32))
    shift = table_ref[pl.ds(row, 1), :width]
    scale = table_ref[pl.ds(row, 1), width : 2 * width]
    attn_in = (normed * (1.0 + scale) + shift).astype(jnp.bfloat16)
    attn_in_ref[...] = attn_in
    projected_ref[...] = (nt(attn_in, weight_ref[...]) + bias_ref[...]).astype(jnp.bfloat16)


def home_row(info_ref, row, home, quarter):
    return jnp.where(row == 0, 1 + info_ref[1] * home // quarter, 0)


def enter_kernel(link, quarter, info_ref, table_ref, split_ref, single_ref, proj_ref, tokens_ref, grad_ref, bias_ref,
                 attn_ref, stream_ref, mlp_in_ref, grad_mlp_ref, mixed_home_ref, proj_true_ref, grad_sum_ref):
    row = pl.program_id(0)
    heads = link.heads
    home, width = tokens_ref.shape[1:]
    share = width // heads
    slice_rows = proj_ref.shape[2]
    head = lax.axis_index("head")

    @pl.when(row == 0)
    def _():
        grad_sum_ref[...] = jnp.zeros_like(grad_sum_ref)
        for index in range(link.batches):
            first = index * slice_rows
            count = min(slice_rows, share - first)
            if count > 0:
                place = link.place(index)
                for spot in range(heads):
                    piece = proj_ref[place, (spot - head + heads) % heads]
                    at = spot * share + first
                    proj_true_ref[at : at + count, :] = piece[:count]

    for at_row, mixed_ref in enumerate((split_ref, single_ref)):

        @pl.when(row == at_row)
        def _(mixed_ref=mixed_ref):
            for spot in range(heads):
                piece = mixed_ref[(spot - head + heads) % heads, 0]
                mixed_home_ref[0, :, spot * share : (spot + 1) * share] = piece

    spot = home_row(info_ref, row, home, quarter)

    def mod(group):
        return table_ref[pl.ds(spot, 1), group * width : (group + 1) * width]

    attn = nn(mixed_home_ref[0], proj_true_ref[...]) + bias_ref[...]
    attn_ref[0] = attn
    stream = tokens_ref[0].astype(jnp.float32) + mod(2) * attn
    stream_ref[0] = stream
    normed, _ = row_norm(stream.astype(jnp.bfloat16).astype(jnp.float32))
    mlp_in_ref[0] = (normed * (1.0 + mod(4)) + mod(3)).astype(jnp.bfloat16)
    grad_mlp = (grad_ref[0].astype(jnp.float32) * mod(5)).astype(jnp.bfloat16)
    grad_mlp_ref[0] = grad_mlp
    grad_sum_ref[...] += jnp.sum(grad_mlp.astype(jnp.float32), axis=0, keepdims=True)


def expand_kernel(steps, mlp_in_ref, bias_ref, *refs):
    pieces, (hidden_ref, slope_ref) = refs[:-2], refs[-2:]
    step = pl.program_id(0)
    for spot, piece_ref in enumerate(pieces):

        @pl.when(step // steps == spot)
        def _(piece_ref=piece_ref):
            pre = nt(mlp_in_ref[...], piece_ref[...]) + bias_ref[...]
            square = pre * pre
            bent = jnp.tanh(gelu_coeff * (pre + 0.044715 * square * pre))
            half = 0.5 * (1.0 + bent)
            hidden_ref[...] = (pre * half).astype(jnp.bfloat16)
            inner = gelu_coeff * (1.0 + (3.0 * 0.044715) * square)
            slope_ref[...] = (half + 0.5 * pre * (1.0 - bent * bent) * inner).astype(jnp.bfloat16)


def contract_kernel(link, quarter, steps, info_ref, table_ref, grad_mlp_ref, hidden_ref, slope_ref, out_bias_ref,
                    tokens_grad_ref, stream_ref, attn_ref, proj_ref, *refs):
    count = 4
    ins, outs = refs[:count], refs[count : 2 * count]
    (grad_pre_ref, pre_sum_ref, block_ref, stream_grad_ref, grad_attn_ref, split_ref, single_ref, sums_ref, attn_sum_ref,
     mlp_acc, grad_acc) = refs[2 * count :]
    grad_mixed_refs = (split_ref, single_ref)
    step = pl.program_id(0)
    heads = link.heads
    rows, home, width = stream_ref.shape
    share = width // heads

    @pl.when(step == 0)
    def _():
        mlp_acc[...] = jnp.zeros_like(mlp_acc)
        grad_acc[...] = jnp.zeros_like(grad_acc)

    for spot in range(count):

        @pl.when(step // steps == spot)
        def _(in_ref=ins[spot], out_ref=outs[spot]):
            grad_pre = (nt(grad_mlp_ref[...], out_ref[...]) * slope_ref[...].astype(jnp.float32)).astype(jnp.bfloat16)
            grad_pre_ref[...] = grad_pre
            pre_sum_ref[...] = jnp.sum(grad_pre.astype(jnp.float32), axis=0, keepdims=True)
            grad_acc[...] += nn(grad_pre, in_ref[...])
            mlp_acc[...] += nn(hidden_ref[...], out_ref[...])

    @pl.when(step == count * steps - 1)
    def _():
        head = lax.axis_index("head")
        attn_sum = jnp.zeros((1, width), jnp.float32)
        for row in range(rows):
            spot = home_row(info_ref, row, home, quarter)

            def mod(group):
                return table_ref[pl.ds(spot, 1), group * width : (group + 1) * width]

            here = slice(row * home, (row + 1) * home)
            grad_out = tokens_grad_ref[row_at(row, info_ref)].astype(jnp.float32)
            stream = stream_ref[row]
            mlp = mlp_acc[here, :] + out_bias_ref[...]
            block = (stream + mod(5) * mlp).astype(jnp.bfloat16)
            for other in range(heads):
                block_ref[(other - head + heads) % heads, row] = block[:, other * share : (other + 1) * share]
            normed, inverse = row_norm(stream.astype(jnp.bfloat16).astype(jnp.float32))
            grad_in = grad_acc[here, :]
            sums_ref[row, 1:2] = jnp.sum(grad_in, axis=0, keepdims=True)
            sums_ref[row, 2:3] = jnp.sum(grad_in * normed, axis=0, keepdims=True)
            sums_ref[row, 3:4] = jnp.sum(grad_out * mlp, axis=0, keepdims=True)
            stream_grad = grad_out + norm_back(normed, inverse, grad_in * (1.0 + mod(4)))
            stream_grad_ref[row] = stream_grad
            rounded = stream_grad.astype(jnp.bfloat16).astype(jnp.float32)
            sums_ref[row, 0:1] = jnp.sum(rounded * attn_ref[row], axis=0, keepdims=True)
            grad_attn = (rounded * mod(2)).astype(jnp.bfloat16)
            grad_attn_ref[row] = grad_attn
            attn_sum += jnp.sum(grad_attn.astype(jnp.float32), axis=0, keepdims=True)
            grad_mixed = nt(grad_attn, proj_ref[...]).astype(jnp.bfloat16)
            for other in range(heads):
                grad_mixed_refs[row][(other - head + heads) % heads, 0] = grad_mixed[:, other * share : (other + 1) * share]
        attn_sum_ref[...] = attn_sum


def row_at(spot, info_ref):
    return jnp.where(spot == 0, info_ref[0], 1 - info_ref[0])


def leave_kernel(link, quarter, at_row, info_ref, table_ref, grad_ref, weight_ref, tokens_ref, stream_grad_ref,
                 shares_ref, sums_ref, term_ref):
    block = pl.program_id(0)
    heads = link.heads
    width = tokens_ref.shape[1]
    share = width // heads
    home = stream_grad_ref.shape[1]
    spot = 1 + block if at_row == 0 else 0
    scale = table_ref[pl.ds(spot, 1), width : 2 * width]
    grad_in = nn(grad_ref[...], weight_ref[...])
    normed, inverse = row_norm(tokens_ref[...].astype(jnp.float32))
    sums_ref[0, 0:1] = jnp.sum(grad_in, axis=0, keepdims=True)
    sums_ref[0, 1:2] = jnp.sum(grad_in * normed, axis=0, keepdims=True)
    term_ref[...] = norm_back(normed, inverse, grad_in * (1.0 + scale))
    start = info_ref[1] * home

    @pl.when(start // quarter == block)
    def _():
        rows = pl.ds(pl.multiple_of(start % quarter, 8), home)
        term_ref[rows, :] += stream_grad_ref[0]

    low = term_ref[...].astype(jnp.bfloat16)
    for head in range(heads):
        shares_ref[head] = low[:, head * share : (head + 1) * share]


def unit_grads_kernel(steps, left_ref, right_ref, *refs):
    more, outs = refs[:2], refs[2:]
    for spot in range(2):

        @pl.when(pl.program_id(0) // steps == spot)
        def _(spot=spot):
            total = tn(left_ref[...], right_ref[...])
            total = total + more[spot][...].astype(jnp.float32)
            outs[spot][...] = total.astype(jnp.bfloat16)


def unit_grads(left, right, half, more=(), order=()):
    count, total = left.shape
    width = right.shape[1]
    piece = total // 4
    steps = piece // UNIT_TILE

    def spec(spot):
        return pl.BlockSpec((UNIT_TILE, width), lambda i: (jnp.clip(i - spot * steps, 0, steps - 1), 0))

    kernel = functools.partial(unit_grads_kernel, steps)
    if not more:
        kernel = lambda l, r, *outs: unit_grads_plain(steps, l, r, *outs)
    return call(
        kernel,
        [shape_of((piece, width), jnp.bfloat16)] * 2,
        [pl.BlockSpec((count, UNIT_TILE), lambda i: (0, i + half * 2 * steps)), whole((count, width))]
        + [spec(i) for i in range(len(more))],
        [spec(0), spec(1)],
        grid=(2 * steps,),
        name="unit_grads", micros=6,
        order=order,
    )(left, right, *more)


def unit_grads_plain(steps, left_ref, right_ref, *outs):
    for spot in range(2):

        @pl.when(pl.program_id(0) // steps == spot)
        def _(spot=spot):
            outs[spot][...] = tn(left_ref[...], right_ref[...]).astype(jnp.bfloat16)


def place_rows_kernel(link, slices_ref, out_ref):
    rows = slices_ref.shape[1]
    for index in range(link.batches):
        count = min(rows, out_ref.shape[0] - index * rows)
        if count > 0:
            piece = slices_ref[link.place(index)].astype(jnp.float32)
            out_ref[index * rows : index * rows + count, :] = piece[:count]


def place_rows(link, slices, rows):
    width = slices.shape[2]
    tile = 384
    return call(
        functools.partial(place_rows_kernel, link),
        shape_of((rows, width), jnp.float32),
        [pl.BlockSpec(slices.shape[:2] + (tile,), lambda i: (0, 0, i))],
        pl.BlockSpec((rows, tile), lambda i: (0, i)),
        grid=(width // tile,),
        name="place_rows", micros=4,
    )(slices)


def place_columns_kernel(link, slices_ref, out_ref, rows_ref):
    rows = slices_ref.shape[1]
    for index in range(link.batches):
        rows_ref[index * rows : (index + 1) * rows, :] = slices_ref[link.place(index)].astype(jnp.float32)
    out_ref[...] = rows_ref[...].T


def place_columns(link, slices):
    batches, rows, width = slices.shape
    tile = 128
    return call(
        functools.partial(place_columns_kernel, link),
        shape_of((width, batches * rows), jnp.float32),
        [pl.BlockSpec((batches, rows, tile), lambda i: (0, 0, i))],
        pl.BlockSpec((tile, batches * rows), lambda i: (i, 0)),
        grid=(width // tile,),
        scratch=[pltpu.VMEM((batches * rows, tile), jnp.float32)],
        name="place_columns", micros=8,
    )(slices)


def lay_home_kernel(heads, info_ref, blocks_ref, out_ref):
    home = blocks_ref.shape[2]
    head = lax.axis_index("head")
    for spot in range(heads):
        for row in range(2):
            out_ref[row_at(row, info_ref), spot * home : (spot + 1) * home, :] = blocks_ref[(head - spot + heads) % heads, row]


def shards(
    tokens,
    segments,
    item_cond,
    condition,
    ada_weight,
    ada_bias,
    qkv_weight,
    qv_bias,
    proj_weight,
    proj_bias,
    in_weight,
    in_bias,
    out_weight,
    out_bias,
    cotangent,
):
    low = jnp.bfloat16
    full = jnp.float32
    heads, batches = lax.axis_size("head"), lax.axis_size("batch")
    link = Links(heads, batches)
    batch = lax.axis_index("batch")
    token_count, width = tokens.shape
    rows = token_count // SEQ
    quarter = SEQ // 4
    home = SEQ // heads
    home_count = rows * home
    share = width // heads
    heads_here = qv_bias.shape[0] // (2 * HEAD_DIM)
    qkv_here = 3 * heads_here * HEAD_DIM
    units_here = in_weight.shape[1]
    units = units_here // batches
    ada_here = ada_weight.shape[1]
    cond_count = condition.shape[0]

    ada_t = ada_weight.T
    qkv_t = qkv_weight.T
    table_part, info = call(
        functools.partial(mod_kernel, quarter, units_here),
        [shape_of((8, ada_here), full), shape_of((8,), jnp.int32)],
        [SCALARS, SCALARS] + [whole(s) for s in ((cond_count, width), (ada_here, width), (1, ada_here), (1, units_here))],
        [whole((8, ada_here)), SCALARS],
        name="modulation", micros=5,
    )(segments, item_cond, condition, ada_t, ada_bias.astype(full)[None], in_bias.astype(full)[None])
    table_rel = jnp.stack([table_part] + [link.fetch(table_part, j) for j in range(1, heads)])

    slice_rows = -(-share // (8 * batches)) * 8
    proj_pad = jnp.pad(proj_weight, ((0, slice_rows * batches - share), (0, 0)))
    proj_slice = lax.dynamic_slice_in_dim(proj_pad, batch * slice_rows, slice_rows, 0)
    in_slice = lax.dynamic_slice_in_dim(in_weight, batch * units, units, 1).T
    out_slice = lax.dynamic_slice_in_dim(out_weight, batch * units, units, 0)
    proj_rel = jnp.stack([proj_slice] + [link.fetch(proj_slice, j) for j in range(1, heads)])
    in_gathered = lax.all_gather(in_slice, "head", axis=0, tiled=True)
    out_gathered = lax.all_gather(out_slice, "head", axis=0, tiled=True)
    def tokens_block(i, info_ref):
        return (4 * row_at(i // 4, info_ref) + i % 4, 0)

    bias_pairs = qv_bias.astype(full).reshape(heads_here, 2, HEAD_DIM)
    full_bias = jnp.concatenate(
        [bias_pairs[:, :1], jnp.zeros((heads_here, 1, HEAD_DIM), full), bias_pairs[:, 1:]], axis=1
    ).reshape(1, -1)
    attn_in, projected, table = call(
        functools.partial(project_kernel, heads, quarter),
        [
            shape_of((token_count, width), low),
            shape_of((token_count, qkv_here), low),
            shape_of((8, 6 * width), full),
        ],
        [
            whole((heads, 8, ada_here)),
            pl.BlockSpec((quarter, width), tokens_block),
            whole((qkv_here, width)),
            whole((1, qkv_here)),
        ],
        [
            pl.BlockSpec((quarter, width), lambda i, _: (i, 0)),
            pl.BlockSpec((quarter, qkv_here), lambda i, _: (i, 0)),
            whole((8, 6 * width)),
        ],
        grid=(4 * rows,),
        prefetch=1,
        name="project", micros=13,
        order=[proj_rel],
    )(info, table_rel, tokens, qkv_t, full_bias)
    projected = projected.reshape(rows, SEQ, qkv_here)
    mixed_rows = []
    mixed_here_rows = []
    log_totals = []
    proj_own = jnp.concatenate(link.gather_levels(proj_rel[None]), axis=0)
    orders = [[proj_own]]
    for row in range(rows):
        mixed, log_total = attend(projected, row, heads_here, quarter, heads, orders[row])
        mixed_rows.append(jnp.stack([mixed[0]] + [link.fetch(mixed[j], j) for j in range(1, heads)]))
        mixed_here_rows.append(mixed)
        if row == 0:
            in_gathered = hold(in_gathered, mixed)
            orders.append([in_gathered])
        log_totals.append(log_total)

    proj_all = jnp.concatenate([proj_own, link.core_swap(proj_own)], axis=0)
    in_held = link.gather_levels(in_gathered, [mixed_here_rows[1]])
    out_held = link.gather_levels(out_gathered)
    out_pieces = out_held + [link.core_swap(piece) for piece in out_held]
    tokens_rows = tokens.reshape(rows, SEQ, width)
    grad_rows = cotangent.reshape(rows, SEQ, width)
    home_spec = pl.BlockSpec((1, home, width), lambda i, info_ref: (row_at(i, info_ref), info_ref[1], 0))
    row_spec = pl.BlockSpec((1, home, width), lambda i, _: (i, 0, 0))
    attn, stream, mlp_in, grad_mlp, mixed_home, proj_true, grad_sum = call(
        functools.partial(enter_kernel, link, quarter),
        [
            shape_of((rows, home, width), full),
            shape_of((rows, home, width), full),
            shape_of((rows, home, width), low),
            shape_of((rows, home, width), low),
            shape_of((rows, home, width), low),
            shape_of((width, width), low),
            shape_of((1, width), full),
        ],
        [
            whole((8, 6 * width)),
            whole((heads, 1, home, share)),
            whole((heads, 1, home, share)),
            whole(proj_all.shape),
            home_spec,
            home_spec,
            whole((1, width)),
        ],
        [row_spec] * 5 + [whole((width, width)), whole((1, width))],
        grid=(rows,),
        prefetch=1,
        name="enter", micros=9,
        order=[in_held[0], out_gathered],
    )(info, table, *mixed_rows, proj_all, tokens_rows, grad_rows, proj_bias.astype(full)[None])

    in_held[1] = hold(in_held[1], mlp_in)
    in_pieces = in_held + [link.core_swap(piece) for piece in in_held]
    mlp_in = mlp_in.reshape(home_count, width)
    grad_mlp = grad_mlp.reshape(home_count, width)
    in_bias_all = table[5].reshape(heads, -1)[:, :units_here]
    in_bias_all = in_bias_all.reshape(heads, batches, units)
    in_bias_all = link.by_owner(in_bias_all.transpose(1, 0, 2)).reshape(1, -1)
    piece_rows = in_pieces[0].shape[0]
    unit_count = 4 * piece_rows
    steps = piece_rows // UNIT_TILE

    def piece_spec(spot):
        return pl.BlockSpec((UNIT_TILE, width), lambda i, *_: (jnp.clip(i - spot * steps, 0, steps - 1), 0))

    tile_spec = pl.BlockSpec((home_count, UNIT_TILE), lambda i, *_: (0, i))
    bias_spec = pl.BlockSpec((1, UNIT_TILE), lambda i, *_: (0, i))
    hidden, slope = call(
        functools.partial(expand_kernel, steps),
        [shape_of((home_count, unit_count), low)] * 2,
        [whole((home_count, width)), bias_spec] + [piece_spec(spot) for spot in range(4)],
        [tile_spec, tile_spec],
        grid=(4 * steps,),
        name="expand", micros=20,
        order=[out_held[0]],
    )(mlp_in, in_bias_all, *in_pieces)

    out_far = unit_grads(hidden, grad_mlp, 1)
    out_near = unit_grads(hidden, grad_mlp, 0, [link.core_swap(piece) for piece in out_far])

    stay = pl.BlockSpec((rows, home, width), lambda *_: (0, 0, 0))
    by_head = whole((heads, rows, home, share))
    one_row = whole((heads, 1, home, share))
    grad_pre, pre_sum, block_home, stream_grad, grad_attn, mixed_split, mixed_single, home_sums, attn_sum = call(
        functools.partial(contract_kernel, link, quarter, steps),
        [
            shape_of((home_count, unit_count), low),
            shape_of((1, unit_count), full),
            shape_of((heads, rows, home, share), low),
            shape_of((rows, home, width), full),
            shape_of((rows, home, width), low),
            shape_of((heads, 1, home, share), low),
            shape_of((heads, 1, home, share), low),
            shape_of((rows, 4, width), full),
            shape_of((1, width), full),
        ],
        [
            whole((8, 6 * width)),
            whole((home_count, width)),
            tile_spec,
            tile_spec,
            whole((1, width)),
            pl.BlockSpec((rows, home, width), lambda i, info_ref: (0, info_ref[1], 0)),
            stay,
            stay,
            whole((width, width)),
        ]
        + [piece_spec(spot) for spot in range(4)] * 2,
        [tile_spec, bias_spec, by_head, stay, stay, one_row, one_row, whole((rows, 4, width)), whole((1, width))],
        grid=(4 * steps,),
        prefetch=1,
        scratch=[pltpu.VMEM((home_count, width), full)] * 2,
        name="contract", micros=44,
        order=list(out_near),
    )(info, table, grad_mlp, hidden, slope, out_bias.astype(full)[None], grad_rows, stream, attn, proj_true,
      *in_pieces, *out_pieces)
    grad_mixed_rows = [
        jnp.stack([piece[0]] + [link.send(piece[j], j) for j in range(1, heads)])
        for piece in (mixed_split, mixed_single)
    ]
    out_sums = link.reduce_levels(list(out_near))
    in_far = unit_grads(grad_pre, mlp_in, 1, order=[out_sums[0]])
    in_near = unit_grads(
        grad_pre, mlp_in, 0, [link.core_swap(piece) for piece in in_far], order=[grad_mixed_rows[0]]
    )
    proj_grad = tn(mixed_home.reshape(home_count, width), grad_attn.reshape(home_count, width)).astype(low)

    grad_rows_low = []
    block_sums = []
    shares = []
    for row in range(rows):
        grad_row = attend_back(
            projected, row, log_totals[row], grad_mixed_rows[row], heads_here, quarter, heads,
            [in_near[0], out_sums[-1]] if row == 0 else [sums_row],
        )[0]
        share_row, sums_row = call(
            functools.partial(leave_kernel, link, quarter, row),
            [shape_of((heads, SEQ, share), low), shape_of((4, 2, width), full)],
            [
                whole((8, 6 * width)),
                pl.BlockSpec((quarter, qkv_here), lambda i, _: (i, 0)),
                whole((qkv_here, width)),
                pl.BlockSpec((quarter, width), lambda i, info_ref, row=row: tokens_block(i + 4 * row, info_ref)),
                pl.BlockSpec((1, home, width), lambda i, _, row=row: (row, 0, 0)),
            ],
            [
                pl.BlockSpec((heads, quarter, share), lambda i, _: (0, i, 0)),
                pl.BlockSpec((1, 2, width), lambda i, _: (i, 0, 0)),
            ],
            grid=(4,),
            prefetch=1,
            scratch=[pltpu.VMEM((quarter, width), full)],
            name="leave", micros=9,
            order=shares,
        )(info, table, grad_row, qkv_t, tokens, stream_grad)
        grad_rows_low.append(grad_row)
        block_sums.append(sums_row)
        shares.append(lax.psum_scatter(share_row, "head", scatter_dimension=0, tiled=True)[0] if row == 0 else share_row)
    grad_projected = jnp.concatenate(grad_rows_low, axis=0)
    in_sums = link.reduce_levels(list(in_near), [grad_rows_low[1], shares[1]])

    def head_sum(values):
        return lax.psum_scatter(values, "head", scatter_dimension=0, tiled=True)

    out_slice_sum = head_sum(out_sums[-1])
    in_slice_sum = head_sum(hold(in_sums[-1], shares[0]))
    shares[1] = head_sum(hold(shares[1], in_slice_sum))[0]
    tokens_grad = jnp.where(
        info[0] == 0, jnp.concatenate(shares, axis=0), jnp.concatenate(shares[::-1], axis=0)
    )

    block_home = jnp.stack([block_home[0]] + [link.send(block_home[j], j) for j in range(1, heads)])
    block_out = call(
        functools.partial(lay_home_kernel, heads),
        shape_of((rows, SEQ, share), low),
        [whole((heads, rows, home, share))],
        whole((rows, SEQ, share)),
        prefetch=1,
        name="lay_home", micros=3,
        order=[grad_rows_low[1]],
    )(info, block_home).reshape(token_count, share)

    home_quarter = lax.axis_index("head") * home // quarter
    seg_spots = lax.broadcasted_iota(jnp.int32, (5, 1), 0)

    def seg_home(sums):
        placed = jnp.where(seg_spots == 1 + home_quarter, sums[0][None, :], 0.0)
        return jnp.where(seg_spots == 0, sums[1][None, :], placed)

    seg_blocks = jnp.concatenate([jnp.sum(block_sums[1], axis=0, keepdims=True), block_sums[0]], axis=0)
    seg_grads = jnp.concatenate(
        [seg_blocks[:, 0], seg_blocks[:, 1]] + [seg_home(home_sums[:, i]) for i in range(4)], axis=1
    )
    in_bias_part = link.by_index(pre_sum.reshape(batches, heads, units)).transpose(1, 0, 2)
    bias_grads = jnp.concatenate(
        [
            in_bias_part.reshape(heads, -1),
            grad_sum.reshape(heads, -1),
            attn_sum.reshape(heads, -1),
        ],
        axis=1,
    ).reshape(1, -1)
    sent = jnp.concatenate([seg_grads, bias_grads, jnp.zeros((2, 6 * width), full)], axis=0)
    sent = sent.reshape(8, heads, ada_here)

    def sent_block(distance):
        return lax.dynamic_index_in_dim(sent, link.at_head(distance), 1, keepdims=False)

    held = sent_block(0)
    for j in range(1, heads):
        held = held + link.send(sent_block(j), j)
    column_sums = jnp.sum(grad_projected.astype(full), axis=0).reshape(heads_here, 3, HEAD_DIM)
    qv_bias_part = jnp.concatenate([column_sums[:, :1], column_sums[:, 2:]], axis=1).reshape(-1)
    held = jnp.concatenate(
        [
            held[:6],
            jnp.pad(qv_bias_part, (0, ada_here - qv_bias_part.shape[0]))[None],
            jnp.pad(info[3:].astype(full), (0, ada_here - 5))[None],
        ],
        axis=0,
    )
    all_held = link.gather_batch(held[None])
    all_classes = (all_held[:, 7, :5] + 0.5).astype(jnp.int32).reshape(-1)
    class_hits = (
        lax.broadcasted_iota(jnp.int32, (cond_count, 1), 0) == all_classes[None, :]
    ).astype(full)
    mod_low = jnp.dot(
        class_hits,
        all_held[:, :5].reshape(-1, ada_here),
        precision=lax.Precision.HIGHEST,
        preferred_element_type=full,
    ).astype(low)
    bias_total = jnp.sum(all_held[:, 5], axis=0)
    qv_bias_grad = jnp.sum(all_held[:, 6, : qv_bias.shape[0]], axis=0)
    in_bias_grad = bias_total[:units_here]
    cond_f = condition.astype(full)
    ada_weight_grad = tn(mod_low, silu_act(cond_f).astype(low)).T
    ada_bias_grad = jnp.sum(mod_low.astype(full), axis=0)
    cond_part = nn(mod_low, ada_t)
    shared = jnp.pad(bias_total[units_here:], (0, width - 2 * share))
    last = jnp.concatenate([cond_part, shared[None], jnp.zeros((7, width), full)]).astype(low)
    last = jnp.stack([last] + [link.fetch(last, j) for j in range(1, heads)]).astype(full)
    cond_total = jnp.sum(last[:, :cond_count], axis=0)
    condition_grad = jax.vjp(silu_act, cond_f)[1](cond_total)[0]
    shared = last[:, cond_count]
    head = lax.axis_index("head")
    shared = jnp.concatenate(
        [lax.dynamic_index_in_dim(shared, (j - head + heads) % heads, 0) for j in range(heads)]
    )
    out_bias_grad = shared[:, :share].reshape(-1)
    proj_bias_grad = shared[:, share : 2 * share].reshape(-1)

    out_weight_grad = place_rows(link, link.gather_batch(out_slice_sum[None]), units_here)
    in_weight_grad = place_columns(link, link.gather_batch(in_slice_sum[None]))

    qkv_rows = -(-qkv_here // (16 * batches)) * 16
    qkv_grad = tn(grad_projected, attn_in.reshape(token_count, width)).astype(low)
    qkv_grad = jnp.pad(qkv_grad, ((0, qkv_rows * batches - qkv_here), (0, 0))).reshape(batches, qkv_rows, width)
    proj_grad = jnp.pad(
        proj_grad.reshape(heads, share, width), ((0, 0), (0, slice_rows * batches - share), (0, 0))
    ).reshape(heads, batches, slice_rows, width)
    proj_grad = proj_grad.transpose(1, 0, 2, 3).reshape(batches, heads * slice_rows, width)
    both = link.by_owner(jnp.concatenate([qkv_grad, proj_grad], axis=1))
    both = both.reshape(2, 2, -1, width)
    got = [link.core_swap(piece) for piece in both[1]]
    both = [(mine.astype(full) + more.astype(full)).astype(low) for mine, more in zip(both[0], got)]
    both = link.reduce_levels(both)[-1]
    proj_blocks = both[qkv_rows:].reshape(heads, slice_rows, width)

    def proj_block(distance):
        return lax.dynamic_index_in_dim(proj_blocks, link.at_head(distance), 0, keepdims=False)

    proj_sum = proj_block(0).astype(full)
    for j in range(1, heads):
        proj_sum = proj_sum + link.send(proj_block(j), j).astype(full)
    both = jnp.concatenate([both[:qkv_rows], proj_sum.astype(low)], axis=0)
    both = link.gather_batch(both[None])
    qkv_weight_grad = place_rows(link, both[:, :qkv_rows], qkv_here).T
    proj_weight_grad = place_rows(link, both[:, qkv_rows:], share)

    return (
        block_out,
        tokens_grad,
        condition_grad,
        ada_weight_grad,
        ada_bias_grad,
        qkv_weight_grad,
        qv_bias_grad,
        proj_weight_grad,
        proj_bias_grad,
        in_weight_grad,
        in_bias_grad,
        out_weight_grad,
        out_bias_grad,
    )


def solution(mesh):
    in_specs = (
        P("batch", None),
        P("batch"),
        P(),
        P(),
        P(None, "head"),
        P("head"),
        P(None, "head"),
        P("head"),
        P("head", None),
        P(),
        P(None, "head"),
        P("head"),
        P("head", None),
        P(),
        P("batch", None),
    )
    out_specs = (
        P("batch", "head"),
        P("batch", "head"),
        P(),
        P(None, "head"),
        P("head"),
        P(None, "head"),
        P("head"),
        P("head", None),
        P(),
        P(None, "head"),
        P("head"),
        P("head", None),
        P(),
    )
    return jax.shard_map(shards, mesh=mesh, in_specs=in_specs, out_specs=out_specs, check_vma=False)
```

```python
import functools
import math

import jax
import jax.numpy as jnp
from jax import lax
from jax.experimental import pallas as pl
from jax.experimental.pallas import tpu as pltpu
from jax.sharding import PartitionSpec as P

HEAD_DIM = 72
SEQ = 1024
LOG2E = 1.4426950408889634
KEY_SCALE = 1.0 / math.sqrt(HEAD_DIM)


def nt(a, b):
    return lax.dot_general(a, b, (((1,), (1,)), ((), ())), preferred_element_type=jnp.float32)


def nn(a, b):
    return lax.dot_general(a, b, (((1,), (0,)), ((), ())), preferred_element_type=jnp.float32)


def attend_kernel(heads, chunk, groups, split, proj_ref, mixed_ref, lse_ref):
    seq = proj_ref.shape[1]
    home = seq // groups
    group = lax.axis_index("head")
    width = 3 * HEAD_DIM
    key_count = chunk if split else seq

    def part(head, start):
        at = head * width
        rows = pl.ds(start, chunk)
        keys = pl.ds(start if split else 0, key_count)
        queries = proj_ref[0, rows, at : at + HEAD_DIM]
        key_rows = proj_ref[0, keys, at + HEAD_DIM : at + 2 * HEAD_DIM]
        value_rows = proj_ref[0, keys, at + 2 * HEAD_DIM : at + 3 * HEAD_DIM]
        scores = nt(key_rows, queries)
        peak = jnp.max(scores, axis=0, keepdims=True)
        weights = jnp.exp2((scores - peak) * (KEY_SCALE * LOG2E))
        total = jnp.sum(weights, axis=0, keepdims=True)
        mixed_t = nn(value_rows.T, weights.astype(jnp.bfloat16)) / total
        lse_ref[0, head : head + 1, rows] = peak * (KEY_SCALE * LOG2E) + jnp.log2(total)
        return mixed_t.T

    def step(index, _):
        start = pl.multiple_of(index * chunk, chunk)
        outs = [part(head, start) for head in range(heads)]
        outs = jnp.concatenate(outs, axis=1).astype(jnp.bfloat16)
        for spot in range(chunk // home):
            target = index * (chunk // home) + spot
            mixed_ref[(group - target + groups) % groups, 0] = outs[spot * home : (spot + 1) * home]
        return 0

    lax.fori_loop(0, seq // chunk, step, 0)


def attend(projected, row, mixed, heads, chunk, groups, order):
    seq, width = projected.shape[1:]
    split = row == 0
    kernel = functools.partial(attend_kernel, heads, chunk, groups, split)
    earlier = [] if mixed is None else [mixed]
    return call(
        kernel if mixed is None else lambda p, _, *refs: kernel(p, *refs),
        [
            shape_of((groups, 2, seq // groups, heads * HEAD_DIM), jnp.bfloat16),
            shape_of((1, heads, seq), jnp.float32),
        ],
        [pl.BlockSpec((1, seq, width), lambda i: (row, 0, 0))] + [pl.BlockSpec(memory_space=pl.ANY)] * len(earlier),
        [
            pl.BlockSpec((groups, 1, seq // groups, heads * HEAD_DIM), lambda i: (0, row, 0, 0)),
            pl.BlockSpec((1, heads, seq), lambda i: (0, 0, 0)),
        ],
        grid=(1,),
        name="attend_split" if split else "attend_whole",
        micros=6 if split else 16,
        order=order,
        aliases={} if mixed is None else {1: 0},
    )(projected, *earlier)


def attend_back_kernel(heads, chunk, groups, split, proj_ref, lse_ref, pieces_ref, out_ref, dk_ref, dv_ref, grad_ref):
    seq = proj_ref.shape[1]
    home = seq // groups
    group = lax.axis_index("head")
    width = 3 * HEAD_DIM
    key_count = chunk if split else seq
    for spot in range(groups):
        grad_ref[spot * home : (spot + 1) * home, :] = pieces_ref[(group - spot + groups) % groups, 0]

    def part(head, start):
        at = head * width
        rows = pl.ds(start, chunk)
        keys = pl.ds(start if split else 0, key_count)
        queries = proj_ref[0, rows, at : at + HEAD_DIM]
        key_rows = proj_ref[0, keys, at + HEAD_DIM : at + 2 * HEAD_DIM]
        value_rows = proj_ref[0, keys, at + 2 * HEAD_DIM : at + 3 * HEAD_DIM]
        grads = grad_ref[rows, head * HEAD_DIM : (head + 1) * HEAD_DIM]
        scores = nt(key_rows, queries)
        probs = jnp.exp2(scores * (KEY_SCALE * LOG2E) - lse_ref[0, head : head + 1, rows])
        grad_probs = nt(value_rows, grads)
        inner = jnp.sum(probs * grad_probs, axis=0, keepdims=True)
        grad_raw = (probs * (grad_probs - inner) * KEY_SCALE).astype(jnp.bfloat16)
        grad_values = nn(probs.astype(jnp.bfloat16), grads)
        grad_keys = nn(grad_raw, queries)
        grad_queries = nn(key_rows.T, grad_raw).T
        return grad_queries, grad_keys, grad_values

    if not split:
        for head in range(heads):
            at = head * width
            dk_ref[...] = jnp.zeros_like(dk_ref)
            dv_ref[...] = jnp.zeros_like(dv_ref)

            def step(index, _):
                start = pl.multiple_of(index * chunk, chunk)
                dq, dk, dv = part(head, start)
                out_ref[0, pl.ds(start, chunk), at : at + HEAD_DIM] = dq.astype(jnp.bfloat16)
                dk_ref[...] += dk
                dv_ref[...] += dv
                return 0

            lax.fori_loop(0, seq // chunk, step, 0)
            both = jnp.concatenate([dk_ref[...], dv_ref[...]], axis=1).astype(jnp.bfloat16)
            out_ref[0, :, at + HEAD_DIM : at + 3 * HEAD_DIM] = both
    else:

        def step(index, _):
            start = pl.multiple_of(index * chunk, chunk)
            outs = [t for head in range(heads) for t in part(head, start)]
            out_ref[0, pl.ds(start, chunk), :] = jnp.concatenate(outs, axis=1).astype(jnp.bfloat16)
            return 0

        lax.fori_loop(0, seq // chunk, step, 0)


def attend_back(projected, row, lse, grads, heads, chunk, groups, order):
    seq, width = projected.shape[1:]
    split = row == 0

    return call(
        functools.partial(attend_back_kernel, heads, chunk, groups, split),
        shape_of((1, seq, width), jnp.bfloat16),
        [
            pl.BlockSpec((1, seq, width), lambda i: (row, 0, 0)),
            pl.BlockSpec((1, heads, seq), lambda i: (0, 0, 0)),
            pl.BlockSpec((groups, 1, seq // groups, heads * HEAD_DIM), lambda i: (0, row, 0, 0)),
        ],
        pl.BlockSpec((1, seq, width), lambda i: (0, 0, 0)),
        grid=(1,),
        scratch=[pltpu.VMEM((seq, HEAD_DIM), jnp.float32)] * 2
        + [pltpu.VMEM((seq, heads * HEAD_DIM), jnp.bfloat16)],
        name="attend_back_split" if split else "attend_back_whole",
        micros=8 if split else 24,
        order=order,
    )(projected, lse, grads)


norm_eps = 1e-06
gelu_coeff = 0.7978845608028654
VMEM_BYTES = 58 * 1024 * 1024
UNIT_TILE = 384


def tn(left_side, right_side):
    return lax.dot_general(
        left_side, right_side, (((0,), (0,)), ((), ())), preferred_element_type=jnp.float32
    )


def row_norm(values):
    center = jnp.mean(values, axis=-1, keepdims=True)
    shifted = values - center
    spread = jnp.mean(shifted * shifted, axis=-1, keepdims=True)
    inverse = lax.rsqrt(spread + norm_eps)
    return (shifted * inverse, inverse)


def norm_back(normed, inverse, grad_normed):
    first_mean = jnp.mean(grad_normed, axis=-1, keepdims=True)
    second_mean = jnp.mean(grad_normed * normed, axis=-1, keepdims=True)
    return inverse * (grad_normed - first_mean - normed * second_mean)


def silu_act(values):
    return values / (1.0 + jnp.exp(-values))


def weight_of(micros):
    return pl.CostEstimate(flops=int(micros * 2.2e10), bytes_accessed=int(micros * 6.6e7), transcendentals=0)


def call(kernel, out_shape, in_specs, out_specs, grid=(), prefetch=0, scratch=(), name=None, micros=1, order=(), aliases={}):
    first = prefetch + len(in_specs)

    def ordered(*refs):
        kernel(*refs[:first], *refs[first + len(order) :])

    run = pl.pallas_call(
        ordered if order else kernel,
        grid_spec=pltpu.PrefetchScalarGridSpec(
            num_scalar_prefetch=prefetch,
            grid=grid,
            in_specs=list(in_specs) + [pl.BlockSpec(memory_space=pl.ANY)] * len(order),
            out_specs=out_specs,
            scratch_shapes=scratch,
        ),
        out_shape=out_shape,
        input_output_aliases=aliases,
        compiler_params=pltpu.CompilerParams(vmem_limit_bytes=VMEM_BYTES),
        cost_estimate=weight_of(micros),
        name=name,
    )
    return lambda *arrays: run(*arrays, *order)


def hold(values, *order, micros=0):
    run = pl.pallas_call(
        lambda *refs: None,
        in_specs=[pl.BlockSpec(memory_space=pl.ANY)] * (1 + len(order)),
        out_specs=pl.BlockSpec(memory_space=pl.ANY),
        out_shape=shape_of(values.shape, values.dtype),
        input_output_aliases={0: 0},
        cost_estimate=weight_of(micros),
        name="hold",
    )
    return run(values, *order)


def whole(shape):
    return pl.BlockSpec(shape, lambda *_: (0,) * len(shape))


SCALARS = pl.BlockSpec(memory_space=pltpu.SMEM)
shape_of = jax.ShapeDtypeStruct


class Links:
    def __init__(self, heads, batches):
        self.heads = heads
        self.batches = batches
        bits = batches.bit_length() - 1
        self.levels = bits - 1
        first = list(range(bits - 1, 0, -1))
        self.orders = (first, first[1:] + first[:1])

    def fetch(self, values, distance):
        count = self.heads
        return lax.ppermute(values, "head", [((i + distance) % count, i) for i in range(count)])

    def send(self, values, distance):
        count = self.heads
        return lax.ppermute(values, "head", [(i, (i + distance) % count) for i in range(count)])

    def head_swap(self, values, bit):
        return lax.ppermute(values, "head", [(i, i ^ (1 << bit)) for i in range(self.heads)])

    def head_cube(self, values, orders):
        for bit in range(self.heads.bit_length() - 1):
            more = self.head_swap(values, bit)
            if bit < len(orders):
                more = hold(more, orders[bit])
            values = jnp.concatenate([values, more], axis=0)
        return values

    def head_gather(self, values):
        return [values] + [self.fetch(values, distance) for distance in range(1, self.heads)]

    def by_head(self, pieces):
        values = pieces[0]
        rows = values.shape[0]
        held = jnp.zeros((self.heads * rows,) + values.shape[1:], values.dtype)
        for distance in range(self.heads):
            held = lax.dynamic_update_slice_in_dim(held, pieces[distance], self.at_head(distance) * rows, 0)
        return held

    def core_swap(self, values):
        return lax.ppermute(values, "batch", [(i, i ^ 1) for i in range(self.batches)])

    def link_swap(self, values, level):
        pairs = [(i, i ^ (1 << self.orders[i & 1][level])) for i in range(self.batches)]
        return lax.ppermute(values, "batch", pairs)

    def owner(self, spot):
        batch = lax.axis_index("batch")
        half = spot >> self.levels
        masks = [
            sum(1 << order[level] for level in range(self.levels) if spot >> level & 1)
            for order in self.orders
        ]
        mask = jnp.where(batch % 2 == half, masks[0], masks[1])
        return (batch ^ half) ^ mask

    def place(self, index):
        batch = lax.axis_index("batch")
        way = batch ^ index
        half = way & 1
        spots = [
            sum(((way >> order[level]) & 1) << level for level in range(self.levels))
            for order in self.orders
        ]
        return (half << self.levels) + jnp.where((batch & 1) == half, spots[0], spots[1])

    def gather_levels(self, values, order=()):
        pieces = [values]
        for level in range(self.levels):
            joined = pieces[0] if level == 0 else jnp.concatenate(pieces, axis=0)
            more = self.link_swap(joined, level)
            if level == 0 and order:
                more = hold(more, *order)
            pieces = [joined, more]
        return pieces

    def gather_batch(self, values):
        own = jnp.concatenate(self.gather_levels(values), axis=0)
        return jnp.concatenate([own, self.core_swap(own)], axis=0)

    def reduce_cores(self, pieces, *order):
        sums = []
        for mine, other in zip(pieces[:2], pieces[2:]):
            more = self.core_swap(other)
            if order:
                more = hold(more, *order)
            sums.append((mine.astype(jnp.float32) + more.astype(jnp.float32)).astype(jnp.bfloat16))
        return sums

    def reduce_first(self, kept, *order):
        more = self.link_swap(kept[1], self.levels - 1)
        if order:
            more = hold(more, *order)
        return (kept[0].astype(jnp.float32) + more.astype(jnp.float32)).astype(jnp.bfloat16)

    def reduce_rest(self, total, *order):
        for level in reversed(range(self.levels - 1)):
            half = total.shape[0] // 2
            more = self.link_swap(total[half:], level)
            if order:
                more = hold(more, *order)
                order = ()
            total = (total[:half].astype(jnp.float32) + more.astype(jnp.float32)).astype(jnp.bfloat16)
        return total

    def by_owner(self, values):
        return jnp.concatenate(
            [lax.dynamic_index_in_dim(values, self.owner(i), 0) for i in range(self.batches)]
        )

    def by_index(self, values):
        return jnp.concatenate(
            [lax.dynamic_index_in_dim(values, self.place(i), 0) for i in range(self.batches)]
        )

    def at_head(self, distance):
        return (lax.axis_index("head") + distance) % self.heads


def mod_kernel(quarter, units_here, seg_ref, item_ref, cond_ref, ada_ref, bias_ref, in_bias_ref, table_ref, info_ref):
    starts = [[seg_ref[row * SEQ + spot * quarter] for spot in range(4)] for row in range(2)]
    first_splits = starts[0][0] != starts[0][3]
    ids = [jnp.where(first_splits, starts[1][0], starts[0][0])] + [
        jnp.where(first_splits, starts[0][spot], starts[1][spot]) for spot in range(4)
    ]
    classes = [item_ref[one] for one in ids]
    info_ref[0] = jnp.where(first_splits, 0, 1)
    info_ref[1] = lax.axis_index("head")
    info_ref[2] = 0
    for spot in range(5):
        info_ref[3 + spot] = classes[spot]
    cond_low = silu_act(cond_ref[...].astype(jnp.float32)).astype(jnp.bfloat16)
    count = cond_low.shape[0]
    row_spot = lax.broadcasted_iota(jnp.int32, (8, count), 0)
    wanted = jnp.full((8, count), count, jnp.int32)
    for spot in range(5):
        wanted = jnp.where(row_spot == spot, classes[spot], wanted)
    hits = (lax.broadcasted_iota(jnp.int32, (8, count), 1) == wanted).astype(jnp.float32)
    rows = nn(hits.astype(jnp.bfloat16), cond_low).astype(jnp.bfloat16)
    table_ref[...] = nt(rows, ada_ref[...]) + bias_ref[...]
    table_ref[5:6, :units_here] = in_bias_ref[...]


def project_kernel(heads, quarter, info_ref, table_rel_ref, tokens_ref, weight_ref, bias_ref, attn_in_ref, projected_ref, table_ref):
    block = pl.program_id(0)
    width = tokens_ref.shape[1]
    columns = table_rel_ref.shape[2]

    @pl.when(block == 0)
    def _():
        for head in range(heads):
            spot = (head - lax.axis_index("head") + heads) % heads
            table_ref[:, head * columns : (head + 1) * columns] = table_rel_ref[spot]

    row = jnp.where(block < 4, 1 + block % 4, 0)
    normed, _ = row_norm(tokens_ref[...].astype(jnp.float32))
    shift = table_ref[pl.ds(row, 1), :width]
    scale = table_ref[pl.ds(row, 1), width : 2 * width]
    attn_in = (normed * (1.0 + scale) + shift).astype(jnp.bfloat16)
    attn_in_ref[...] = attn_in
    projected_ref[...] = (nt(attn_in, weight_ref[...]) + bias_ref[...]).astype(jnp.bfloat16)


def home_row(info_ref, row, home, quarter):
    return jnp.where(row == 0, 1 + info_ref[1] * home // quarter, 0)


def enter_kernel(link, quarter, info_ref, table_ref, mixed_ref, proj_ref, tokens_ref, grad_ref, bias_ref,
                 attn_ref, stream_ref, mlp_in_ref, grad_mlp_ref, mixed_home_ref, proj_true_ref, grad_sum_ref):
    row = pl.program_id(0)
    heads = link.heads
    home, width = tokens_ref.shape[1:]
    share = width // heads
    slice_rows = proj_ref.shape[2]
    head = lax.axis_index("head")

    @pl.when(row == 0)
    def _():
        grad_sum_ref[...] = jnp.zeros_like(grad_sum_ref)
        for index in range(link.batches):
            first = index * slice_rows
            count = min(slice_rows, share - first)
            if count > 0:
                place = link.place(index)
                for spot in range(heads):
                    piece = proj_ref[place, (spot - head + heads) % heads]
                    at = spot * share + first
                    proj_true_ref[at : at + count, :] = piece[:count]

    for spot in range(heads):
        piece = mixed_ref[(spot - head + heads) % heads, 0]
        mixed_home_ref[0, :, spot * share : (spot + 1) * share] = piece
    spot = home_row(info_ref, row, home, quarter)

    def mod(group):
        return table_ref[pl.ds(spot, 1), group * width : (group + 1) * width]

    attn = nn(mixed_home_ref[0], proj_true_ref[...]) + bias_ref[...]
    attn_ref[0] = attn
    stream = tokens_ref[0].astype(jnp.float32) + mod(2) * attn
    stream_ref[0] = stream
    normed, _ = row_norm(stream.astype(jnp.bfloat16).astype(jnp.float32))
    mlp_in_ref[0] = (normed * (1.0 + mod(4)) + mod(3)).astype(jnp.bfloat16)
    grad_mlp = (grad_ref[0].astype(jnp.float32) * mod(5)).astype(jnp.bfloat16)
    grad_mlp_ref[0] = grad_mlp
    grad_sum_ref[...] += jnp.sum(grad_mlp.astype(jnp.float32), axis=0, keepdims=True)


def expand_kernel(steps, mlp_in_ref, bias_ref, *refs):
    pieces, (hidden_ref, slope_ref) = refs[:-2], refs[-2:]
    step = pl.program_id(0)
    for spot, piece_ref in enumerate(pieces):

        @pl.when(step // steps == spot)
        def _(piece_ref=piece_ref):
            pre = nt(mlp_in_ref[...], piece_ref[...]) + bias_ref[...]
            square = pre * pre
            bent = jnp.tanh(gelu_coeff * (pre + 0.044715 * square * pre))
            half = 0.5 * (1.0 + bent)
            hidden_ref[...] = (pre * half).astype(jnp.bfloat16)
            inner = gelu_coeff * (1.0 + (3.0 * 0.044715) * square)
            slope_ref[...] = (half + 0.5 * pre * (1.0 - bent * bent) * inner).astype(jnp.bfloat16)


def contract_kernel(link, quarter, steps, info_ref, table_ref, grad_mlp_ref, hidden_ref, slope_ref, out_bias_ref,
                    tokens_grad_ref, stream_ref, attn_ref, proj_ref, *refs):
    count = 4
    ins, outs = refs[:count], refs[count : 2 * count]
    (grad_pre_ref, pre_sum_ref, block_ref, stream_grad_ref, grad_attn_ref, grad_mixed_ref, sums_ref, attn_sum_ref,
     mlp_acc, grad_acc) = refs[2 * count :]
    step = pl.program_id(0)
    heads = link.heads
    rows, home, width = stream_ref.shape
    share = width // heads

    @pl.when(step == 0)
    def _():
        mlp_acc[...] = jnp.zeros_like(mlp_acc)
        grad_acc[...] = jnp.zeros_like(grad_acc)

    for spot in range(count):

        @pl.when(step // steps == spot)
        def _(in_ref=ins[spot], out_ref=outs[spot]):
            grad_pre = (nt(grad_mlp_ref[...], out_ref[...]) * slope_ref[...].astype(jnp.float32)).astype(jnp.bfloat16)
            grad_pre_ref[...] = grad_pre
            pre_sum_ref[...] = jnp.sum(grad_pre.astype(jnp.float32), axis=0, keepdims=True)
            grad_acc[...] += nn(grad_pre, in_ref[...])
            mlp_acc[...] += nn(hidden_ref[...], out_ref[...])

    @pl.when(step == count * steps - 1)
    def _():
        head = lax.axis_index("head")
        attn_sum = jnp.zeros((1, width), jnp.float32)
        for row in range(rows):
            spot = home_row(info_ref, row, home, quarter)

            def mod(group):
                return table_ref[pl.ds(spot, 1), group * width : (group + 1) * width]

            here = slice(row * home, (row + 1) * home)
            grad_out = tokens_grad_ref[row_at(row, info_ref)].astype(jnp.float32)
            stream = stream_ref[row]
            mlp = mlp_acc[here, :] + out_bias_ref[...]
            block = (stream + mod(5) * mlp).astype(jnp.bfloat16)
            for other in range(heads):
                block_ref[(other - head + heads) % heads, row] = block[:, other * share : (other + 1) * share]
            normed, inverse = row_norm(stream.astype(jnp.bfloat16).astype(jnp.float32))
            grad_in = grad_acc[here, :]
            sums_ref[row, 1:2] = jnp.sum(grad_in, axis=0, keepdims=True)
            sums_ref[row, 2:3] = jnp.sum(grad_in * normed, axis=0, keepdims=True)
            sums_ref[row, 3:4] = jnp.sum(grad_out * mlp, axis=0, keepdims=True)
            stream_grad = grad_out + norm_back(normed, inverse, grad_in * (1.0 + mod(4)))
            stream_grad_ref[row] = stream_grad
            rounded = stream_grad.astype(jnp.bfloat16).astype(jnp.float32)
            sums_ref[row, 0:1] = jnp.sum(rounded * attn_ref[row], axis=0, keepdims=True)
            grad_attn = (rounded * mod(2)).astype(jnp.bfloat16)
            grad_attn_ref[row] = grad_attn
            attn_sum += jnp.sum(grad_attn.astype(jnp.float32), axis=0, keepdims=True)
            grad_mixed = nt(grad_attn, proj_ref[...]).astype(jnp.bfloat16)
            for other in range(heads):
                grad_mixed_ref[(other - head + heads) % heads, row] = grad_mixed[:, other * share : (other + 1) * share]
        attn_sum_ref[...] = attn_sum


def row_at(spot, info_ref):
    return jnp.where(spot == 0, info_ref[0], 1 - info_ref[0])


def leave_kernel(link, quarter, at_row, info_ref, table_ref, grad_ref, weight_ref, tokens_ref, stream_grad_ref,
                 shares_ref, sums_ref, term_ref):
    block = pl.program_id(0)
    heads = link.heads
    width = tokens_ref.shape[1]
    share = width // heads
    home = stream_grad_ref.shape[1]
    spot = 1 + block if at_row == 0 else 0
    scale = table_ref[pl.ds(spot, 1), width : 2 * width]
    grad_in = nn(grad_ref[...], weight_ref[...])
    normed, inverse = row_norm(tokens_ref[...].astype(jnp.float32))
    sums_ref[0, 0:1] = jnp.sum(grad_in, axis=0, keepdims=True)
    sums_ref[0, 1:2] = jnp.sum(grad_in * normed, axis=0, keepdims=True)
    term_ref[...] = norm_back(normed, inverse, grad_in * (1.0 + scale))
    start = info_ref[1] * home

    @pl.when(start // quarter == block)
    def _():
        rows = pl.ds(pl.multiple_of(start % quarter, 8), home)
        term_ref[rows, :] += stream_grad_ref[0]

    low = term_ref[...].astype(jnp.bfloat16)
    for head in range(heads):
        shares_ref[head] = low[:, head * share : (head + 1) * share]


def unit_grads_kernel(steps, left_ref, right_ref, *outs):
    for spot in range(4):

        @pl.when(pl.program_id(0) // steps == spot)
        def _(spot=spot):
            outs[spot][...] = tn(left_ref[...], right_ref[...]).astype(jnp.bfloat16)


def unit_grads(left, right, order=()):
    count, total = left.shape
    width = right.shape[1]
    piece = total // 4
    steps = piece // UNIT_TILE

    def spec(spot):
        return pl.BlockSpec((UNIT_TILE, width), lambda i: (jnp.clip(i - spot * steps, 0, steps - 1), 0))

    return call(
        functools.partial(unit_grads_kernel, steps),
        [shape_of((piece, width), jnp.bfloat16)] * 4,
        [pl.BlockSpec((count, UNIT_TILE), lambda i: (0, i)), whole((count, width))],
        [spec(i) for i in range(4)],
        grid=(4 * steps,),
        name="unit_grads", micros=14,
        order=order,
    )(left, right)


def place_rows_kernel(link, slices_ref, out_ref):
    rows = slices_ref.shape[1]
    for index in range(link.batches):
        count = min(rows, out_ref.shape[0] - index * rows)
        if count > 0:
            piece = slices_ref[link.place(index)].astype(jnp.float32)
            out_ref[index * rows : index * rows + count, :] = piece[:count]


def place_rows(link, slices, rows):
    width = slices.shape[2]
    tile = 384
    return call(
        functools.partial(place_rows_kernel, link),
        shape_of((rows, width), jnp.float32),
        [pl.BlockSpec(slices.shape[:2] + (tile,), lambda i: (0, 0, i))],
        pl.BlockSpec((rows, tile), lambda i: (0, i)),
        grid=(width // tile,),
        name="place_rows", micros=0,
    )(slices)


def place_columns_kernel(link, slices_ref, out_ref, rows_ref):
    rows = slices_ref.shape[1]
    for index in range(link.batches):
        rows_ref[index * rows : (index + 1) * rows, :] = slices_ref[link.place(index)].astype(jnp.float32)
    out_ref[...] = rows_ref[...].T


def place_columns(link, slices):
    batches, rows, width = slices.shape
    tile = 128
    return call(
        functools.partial(place_columns_kernel, link),
        shape_of((width, batches * rows), jnp.float32),
        [pl.BlockSpec((batches, rows, tile), lambda i: (0, 0, i))],
        pl.BlockSpec((tile, batches * rows), lambda i: (i, 0)),
        grid=(width // tile,),
        scratch=[pltpu.VMEM((batches * rows, tile), jnp.float32)],
        name="place_columns", micros=0,
    )(slices)


def lay_home_kernel(heads, info_ref, blocks_ref, out_ref):
    home = blocks_ref.shape[2]
    head = lax.axis_index("head")
    for spot in range(heads):
        for row in range(2):
            out_ref[row_at(row, info_ref), spot * home : (spot + 1) * home, :] = blocks_ref[(head - spot + heads) % heads, row]


def shards(
    tokens,
    segments,
    item_cond,
    condition,
    ada_weight,
    ada_bias,
    qkv_weight,
    qv_bias,
    proj_weight,
    proj_bias,
    in_weight,
    in_bias,
    out_weight,
    out_bias,
    cotangent,
):
    low = jnp.bfloat16
    full = jnp.float32
    heads, batches = lax.axis_size("head"), lax.axis_size("batch")
    link = Links(heads, batches)
    batch = lax.axis_index("batch")
    token_count, width = tokens.shape
    rows = token_count // SEQ
    quarter = SEQ // 4
    home = SEQ // heads
    home_count = rows * home
    share = width // heads
    heads_here = qv_bias.shape[0] // (2 * HEAD_DIM)
    qkv_here = 3 * heads_here * HEAD_DIM
    units_here = in_weight.shape[1]
    units = units_here // batches
    ada_here = ada_weight.shape[1]
    cond_count = condition.shape[0]

    ada_t = ada_weight.T
    qkv_t = qkv_weight.T
    table_part, info = call(
        functools.partial(mod_kernel, quarter, units_here),
        [shape_of((8, ada_here), full), shape_of((8,), jnp.int32)],
        [SCALARS, SCALARS] + [whole(s) for s in ((cond_count, width), (ada_here, width), (1, ada_here), (1, units_here))],
        [whole((8, ada_here)), SCALARS],
        name="modulation", micros=5,
    )(segments, item_cond, condition, ada_t, ada_bias.astype(full)[None], in_bias.astype(full)[None])
    table_rel = jnp.stack([table_part] + [link.fetch(table_part, j) for j in range(1, heads)])

    slice_rows = -(-share // (8 * batches)) * 8
    proj_pad = jnp.pad(proj_weight, ((0, slice_rows * batches - share), (0, 0)))
    in_slice = lax.dynamic_slice_in_dim(in_weight, batch * units, units, 1).T
    out_slice = lax.dynamic_slice_in_dim(out_weight, batch * units, units, 0)
    in_gathered = lax.all_gather(in_slice, "head", axis=0, tiled=True)
    out_gathered = lax.all_gather(out_slice, "head", axis=0, tiled=True)
    def tokens_block(i, info_ref):
        return (4 * row_at(i // 4, info_ref) + i % 4, 0)

    bias_pairs = qv_bias.astype(full).reshape(heads_here, 2, HEAD_DIM)
    full_bias = jnp.concatenate(
        [bias_pairs[:, :1], jnp.zeros((heads_here, 1, HEAD_DIM), full), bias_pairs[:, 1:]], axis=1
    ).reshape(1, -1)
    attn_in, projected, table = call(
        functools.partial(project_kernel, heads, quarter),
        [
            shape_of((token_count, width), low),
            shape_of((token_count, qkv_here), low),
            shape_of((8, 6 * width), full),
        ],
        [
            whole((heads, 8, ada_here)),
            pl.BlockSpec((quarter, width), tokens_block),
            whole((qkv_here, width)),
            whole((1, qkv_here)),
        ],
        [
            pl.BlockSpec((quarter, width), lambda i, _: (i, 0)),
            pl.BlockSpec((quarter, qkv_here), lambda i, _: (i, 0)),
            whole((8, 6 * width)),
        ],
        grid=(4 * rows,),
        prefetch=1,
        name="project", micros=13,
    )(info, table_rel, tokens, qkv_t, full_bias)
    projected = projected.reshape(rows, SEQ, qkv_here)
    proj_slice = hold(lax.dynamic_slice_in_dim(proj_pad, batch * slice_rows, slice_rows, 0), table_rel)
    proj_rel = jnp.stack(
        [proj_slice] + [hold(link.fetch(proj_slice, j), projected) for j in range(1, heads)]
    )[None]
    mixed = None
    log_totals = []
    for row in range(rows):
        order = [in_gathered] if row == 1 else []
        mixed, log_total = attend(projected, row, mixed, heads_here, quarter, heads, order)
        log_totals.append(log_total)
        if row < link.levels:
            proj_rel = jnp.concatenate([proj_rel, hold(link.link_swap(proj_rel, row), log_total)], axis=0)
        if row == 0:
            in_gathered = hold(in_gathered, log_total)
    in_held = link.gather_levels(in_gathered, [log_totals[1]])
    for level in range(rows, link.levels):
        proj_rel = jnp.concatenate([proj_rel, link.link_swap(proj_rel, level)], axis=0)
    proj_all = jnp.concatenate([proj_rel, link.core_swap(proj_rel)], axis=0)
    out_gathered = hold(out_gathered, in_held[0])
    mixed = hold(mixed, out_gathered, proj_all, micros=20)
    mixed_all = jnp.stack([mixed[0]] + [link.fetch(mixed[j], j) for j in range(1, heads)])

    out_held = link.gather_levels(out_gathered)
    out_pieces = out_held + [link.core_swap(piece) for piece in out_held]
    tokens_rows = tokens.reshape(rows, SEQ, width)
    grad_rows = cotangent.reshape(rows, SEQ, width)
    home_spec = pl.BlockSpec((1, home, width), lambda i, info_ref: (row_at(i, info_ref), info_ref[1], 0))
    row_spec = pl.BlockSpec((1, home, width), lambda i, _: (i, 0, 0))
    attn, stream, mlp_in, grad_mlp, mixed_home, proj_true, grad_sum = call(
        functools.partial(enter_kernel, link, quarter),
        [
            shape_of((rows, home, width), full),
            shape_of((rows, home, width), full),
            shape_of((rows, home, width), low),
            shape_of((rows, home, width), low),
            shape_of((rows, home, width), low),
            shape_of((width, width), low),
            shape_of((1, width), full),
        ],
        [
            whole((8, 6 * width)),
            pl.BlockSpec((heads, 1, home, share), lambda i, _: (0, i, 0, 0)),
            whole(proj_all.shape),
            home_spec,
            home_spec,
            whole((1, width)),
        ],
        [row_spec] * 5 + [whole((width, width)), whole((1, width))],
        grid=(rows,),
        prefetch=1,
        name="enter", micros=9,
        order=[out_held[0]],
    )(info, table, mixed_all, proj_all, tokens_rows, grad_rows, proj_bias.astype(full)[None])

    in_held[1] = hold(in_held[1], mlp_in)
    in_pieces = in_held + [link.core_swap(piece) for piece in in_held]
    mlp_in = mlp_in.reshape(home_count, width)
    grad_mlp = grad_mlp.reshape(home_count, width)
    in_bias_all = table[5].reshape(heads, -1)[:, :units_here]
    in_bias_all = in_bias_all.reshape(heads, batches, units)
    in_bias_all = link.by_owner(in_bias_all.transpose(1, 0, 2)).reshape(1, -1)
    piece_rows = in_pieces[0].shape[0]
    unit_count = 4 * piece_rows
    steps = piece_rows // UNIT_TILE

    def piece_spec(spot):
        return pl.BlockSpec((UNIT_TILE, width), lambda i, *_: (jnp.clip(i - spot * steps, 0, steps - 1), 0))

    tile_spec = pl.BlockSpec((home_count, UNIT_TILE), lambda i, *_: (0, i))
    bias_spec = pl.BlockSpec((1, UNIT_TILE), lambda i, *_: (0, i))
    hidden, slope = call(
        functools.partial(expand_kernel, steps),
        [shape_of((home_count, unit_count), low)] * 2,
        [whole((home_count, width)), bias_spec] + [piece_spec(spot) for spot in range(4)],
        [tile_spec, tile_spec],
        grid=(4 * steps,),
        name="expand", micros=20,
        order=[out_held[0]],
    )(mlp_in, in_bias_all, *in_pieces)

    out_parts = unit_grads(hidden, grad_mlp, order=[out_pieces[2]])

    stay = pl.BlockSpec((rows, home, width), lambda *_: (0, 0, 0))
    by_head = whole((heads, rows, home, share))
    grad_pre, pre_sum, block_home, stream_grad, grad_attn, grad_mixed, home_sums, attn_sum = call(
        functools.partial(contract_kernel, link, quarter, steps),
        [
            shape_of((home_count, unit_count), low),
            shape_of((1, unit_count), full),
            shape_of((heads, rows, home, share), low),
            shape_of((rows, home, width), full),
            shape_of((rows, home, width), low),
            shape_of((heads, rows, home, share), low),
            shape_of((rows, 4, width), full),
            shape_of((1, width), full),
        ],
        [
            whole((8, 6 * width)),
            whole((home_count, width)),
            tile_spec,
            tile_spec,
            whole((1, width)),
            pl.BlockSpec((rows, home, width), lambda i, info_ref: (0, info_ref[1], 0)),
            stay,
            stay,
            whole((width, width)),
        ]
        + [piece_spec(spot) for spot in range(4)] * 2,
        [tile_spec, bias_spec, by_head, stay, stay, by_head, whole((rows, 4, width)), whole((1, width))],
        grid=(4 * steps,),
        prefetch=1,
        scratch=[pltpu.VMEM((home_count, width), full)] * 2,
        name="contract", micros=44,
        order=[out_parts[0]],
    )(info, table, grad_mlp, hidden, slope, out_bias.astype(full)[None], grad_rows, stream, attn, proj_true,
      *in_pieces, *out_pieces)
    mixed_sends = [link.send(grad_mixed[j], j) for j in range(1, heads)]
    out_near = link.reduce_cores(out_parts, grad_pre)
    out_sum = link.reduce_first(out_near)
    in_parts = unit_grads(grad_pre, mlp_in, order=[out_near[1]])
    grad_mixed = jnp.stack([grad_mixed[0]] + [hold(piece, in_parts[0]) for piece in mixed_sends])
    out_slice = link.reduce_rest(out_sum)
    in_near = link.reduce_cores(in_parts, grad_mixed)
    proj_grad = tn(mixed_home.reshape(home_count, width), grad_attn.reshape(home_count, width)).astype(low)

    def head_sum(values):
        return lax.psum_scatter(values, "head", scatter_dimension=0, tiled=True)

    out_blocks = out_slice.reshape(heads, units, width)

    def out_block(distance):
        return lax.dynamic_index_in_dim(out_blocks, link.at_head(distance), 0, keepdims=False)

    out_more = [link.send(out_block(j), j) for j in range(1, heads)]
    grad_rows_low = []
    block_sums = []
    shares = None
    for row in range(rows):
        grad_row = attend_back(
            projected, row, log_totals[row], grad_mixed, heads_here, quarter, heads,
            [] if row == 0 else [sums_row, out_slice],
        )[0]
        order = list(in_near) + [out_sum]
        if row == 1:
            in_sum = link.reduce_first(in_near, grad_row)
            order = [in_sum]
        earlier = [] if shares is None else [shares]
        kernel = functools.partial(leave_kernel, link, quarter, row)
        shares, sums_row = call(
            kernel if row == 0 else lambda *refs: kernel(*refs[:6], *refs[7:]),
            [shape_of((heads, token_count, share), low), shape_of((4, 2, width), full)],
            [
                whole((8, 6 * width)),
                pl.BlockSpec((quarter, qkv_here), lambda i, _: (i, 0)),
                whole((qkv_here, width)),
                pl.BlockSpec((quarter, width), lambda i, info_ref, row=row: tokens_block(i + 4 * row, info_ref)),
                pl.BlockSpec((1, home, width), lambda i, _, row=row: (row, 0, 0)),
            ]
            + [pl.BlockSpec(memory_space=pl.ANY)] * len(earlier),
            [
                pl.BlockSpec((heads, quarter, share), lambda i, _, row=row: (0, i + 4 * row, 0)),
                pl.BlockSpec((1, 2, width), lambda i, _: (i, 0, 0)),
            ],
            grid=(4,),
            prefetch=1,
            scratch=[pltpu.VMEM((quarter, width), full)],
            name="leave", micros=9,
            aliases={6: 0} if earlier else {},
            order=order,
        )(info, table, grad_row, qkv_t, tokens, stream_grad, *earlier)
        grad_rows_low.append(grad_row)
        block_sums.append(sums_row)
    in_slice = link.reduce_rest(in_sum, sums_row)
    out_slice_sum = out_block(0).astype(full)
    for more in out_more:
        out_slice_sum = out_slice_sum + hold(more, grad_rows_low[1]).astype(full)
    out_slice_sum = out_slice_sum.astype(low)
    grad_projected = hold(jnp.concatenate(grad_rows_low, axis=0), in_slice)

    in_slice_sum = head_sum(in_slice)
    shares = head_sum(hold(shares, in_slice_sum))[0]
    tokens_grad = jnp.where(
        info[0] == 0, shares, jnp.concatenate([shares[SEQ:], shares[:SEQ]], axis=0)
    )

    block_home = hold(block_home, grad_mixed)
    block_home = jnp.stack(
        [block_home[0]] + [hold(link.send(block_home[j], j), sums_row) for j in range(1, heads)]
    )
    block_out = call(
        functools.partial(lay_home_kernel, heads),
        shape_of((rows, SEQ, share), low),
        [whole((heads, rows, home, share))],
        whole((rows, SEQ, share)),
        prefetch=1,
        name="lay_home", micros=0,
        order=[sums_row],
    )(info, block_home).reshape(token_count, share)

    home_quarter = lax.axis_index("head") * home // quarter
    seg_spots = lax.broadcasted_iota(jnp.int32, (5, 1), 0)

    def seg_home(sums):
        placed = jnp.where(seg_spots == 1 + home_quarter, sums[0][None, :], 0.0)
        return jnp.where(seg_spots == 0, sums[1][None, :], placed)

    seg_blocks = jnp.concatenate([jnp.sum(block_sums[1], axis=0, keepdims=True), block_sums[0]], axis=0)
    seg_grads = jnp.concatenate(
        [seg_blocks[:, 0], seg_blocks[:, 1]] + [seg_home(home_sums[:, i]) for i in range(4)], axis=1
    )
    in_bias_part = link.by_index(pre_sum.reshape(batches, heads, units)).transpose(1, 0, 2)
    bias_grads = jnp.concatenate(
        [
            in_bias_part.reshape(heads, -1),
            grad_sum.reshape(heads, -1),
            attn_sum.reshape(heads, -1),
        ],
        axis=1,
    ).reshape(1, -1)
    sent = jnp.concatenate([seg_grads, bias_grads, jnp.zeros((2, 6 * width), full)], axis=0)
    sent = hold(sent, in_slice).reshape(8, heads, ada_here)

    def sent_block(distance):
        return lax.dynamic_index_in_dim(sent, link.at_head(distance), 1, keepdims=False)

    held = sent_block(0)
    for j in range(1, heads):
        held = held + link.send(sent_block(j), j)
    column_sums = jnp.sum(grad_projected.astype(full), axis=0).reshape(heads_here, 3, HEAD_DIM)
    qv_bias_part = jnp.concatenate([column_sums[:, :1], column_sums[:, 2:]], axis=1).reshape(-1)
    held = jnp.concatenate(
        [
            held[:6],
            jnp.pad(qv_bias_part, (0, ada_here - qv_bias_part.shape[0]))[None],
            jnp.pad(info[3:].astype(full), (0, ada_here - 5))[None],
        ],
        axis=0,
    )
    all_held = hold(link.gather_batch(held[None]), in_slice_sum)
    all_classes = (all_held[:, 7, :5] + 0.5).astype(jnp.int32).reshape(-1)
    class_hits = (
        lax.broadcasted_iota(jnp.int32, (cond_count, 1), 0) == all_classes[None, :]
    ).astype(full)
    mod_low = jnp.dot(
        class_hits,
        all_held[:, :5].reshape(-1, ada_here),
        precision=lax.Precision.HIGHEST,
        preferred_element_type=full,
    ).astype(low)
    bias_total = jnp.sum(all_held[:, 5], axis=0)
    qv_bias_grad = jnp.sum(all_held[:, 6, : qv_bias.shape[0]], axis=0)
    in_bias_grad = bias_total[:units_here]
    cond_f = condition.astype(full)
    ada_weight_grad = tn(mod_low, silu_act(cond_f).astype(low)).T
    ada_bias_grad = jnp.sum(mod_low.astype(full), axis=0)
    cond_part = nn(mod_low, ada_t)
    shared = jnp.pad(bias_total[units_here:], (0, width - 2 * share))
    last = jnp.concatenate([cond_part, shared[None], jnp.zeros((7, width), full)]).astype(low)
    last = jnp.stack([last] + [link.fetch(last, j) for j in range(1, heads)]).astype(full)
    cond_total = jnp.sum(last[:, :cond_count], axis=0)
    condition_grad = jax.vjp(silu_act, cond_f)[1](cond_total)[0]
    shared = last[:, cond_count]
    head = lax.axis_index("head")
    shared = jnp.concatenate(
        [lax.dynamic_index_in_dim(shared, (j - head + heads) % heads, 0) for j in range(heads)]
    )
    out_bias_grad = shared[:, :share].reshape(-1)
    proj_bias_grad = shared[:, share : 2 * share].reshape(-1)

    out_weight_grad = place_rows(link, link.gather_batch(out_slice_sum[None]), units_here)
    in_weight_grad = place_columns(link, link.gather_batch(in_slice_sum[None]))

    qkv_rows = -(-qkv_here // (16 * batches)) * 16
    qkv_grad = tn(grad_projected, attn_in.reshape(token_count, width)).astype(low)
    qkv_grad = jnp.pad(qkv_grad, ((0, qkv_rows * batches - qkv_here), (0, 0))).reshape(batches, qkv_rows, width)
    proj_grad = jnp.pad(
        proj_grad.reshape(heads, share, width), ((0, 0), (0, slice_rows * batches - share), (0, 0))
    ).reshape(heads, batches, slice_rows, width)
    proj_grad = proj_grad.transpose(1, 0, 2, 3).reshape(batches, heads * slice_rows, width)
    both = link.by_owner(jnp.concatenate([qkv_grad, proj_grad], axis=1))
    both = both.reshape(2, 2, -1, width)
    got = [link.core_swap(piece) for piece in both[1]]
    both = [(mine.astype(full) + more.astype(full)).astype(low) for mine, more in zip(both[0], got)]
    both = link.reduce_rest(link.reduce_first(both))
    proj_blocks = both[qkv_rows:].reshape(heads, slice_rows, width)

    def proj_block(distance):
        return lax.dynamic_index_in_dim(proj_blocks, link.at_head(distance), 0, keepdims=False)

    proj_sum = proj_block(0).astype(full)
    for j in range(1, heads):
        proj_sum = proj_sum + link.send(proj_block(j), j).astype(full)
    both = jnp.concatenate([both[:qkv_rows], proj_sum.astype(low)], axis=0)
    both = link.gather_batch(both[None])
    qkv_weight_grad = place_rows(link, both[:, :qkv_rows], qkv_here).T
    proj_weight_grad = place_rows(link, both[:, qkv_rows:], share)

    return (
        block_out,
        tokens_grad,
        condition_grad,
        ada_weight_grad,
        ada_bias_grad,
        qkv_weight_grad,
        qv_bias_grad,
        proj_weight_grad,
        proj_bias_grad,
        in_weight_grad,
        in_bias_grad,
        out_weight_grad,
        out_bias_grad,
    )


def solution(mesh):
    in_specs = (
        P("batch", None),
        P("batch"),
        P(),
        P(),
        P(None, "head"),
        P("head"),
        P(None, "head"),
        P("head"),
        P("head", None),
        P(),
        P(None, "head"),
        P("head"),
        P("head", None),
        P(),
        P("batch", None),
    )
    out_specs = (
        P("batch", "head"),
        P("batch", "head"),
        P(),
        P(None, "head"),
        P("head"),
        P(None, "head"),
        P("head"),
        P("head", None),
        P(),
        P(None, "head"),
        P("head"),
        P("head", None),
        P(),
    )
    return jax.shard_map(shards, mesh=mesh, in_specs=in_specs, out_specs=out_specs, check_vma=False)
```

```python
import functools
import math

import jax
import jax.numpy as jnp
from jax import lax
from jax.experimental import pallas as pl
from jax.experimental.pallas import tpu as pltpu
from jax.sharding import PartitionSpec as P

HEAD_DIM = 72
SEQ = 1024
LOG2E = 1.4426950408889634
KEY_SCALE = 1.0 / math.sqrt(HEAD_DIM)


def nt(a, b):
    return lax.dot_general(a, b, (((1,), (1,)), ((), ())), preferred_element_type=jnp.float32)


def nn(a, b):
    return lax.dot_general(a, b, (((1,), (0,)), ((), ())), preferred_element_type=jnp.float32)


def attend_kernel(heads, chunk, groups, split, proj_ref, mixed_ref, lse_ref):
    seq = proj_ref.shape[1]
    home = seq // groups
    group = lax.axis_index("head")
    width = 3 * HEAD_DIM
    key_count = chunk if split else seq

    def part(head, start):
        at = head * width
        rows = pl.ds(start, chunk)
        keys = pl.ds(start if split else 0, key_count)
        queries = proj_ref[0, rows, at : at + HEAD_DIM]
        key_rows = proj_ref[0, keys, at + HEAD_DIM : at + 2 * HEAD_DIM]
        value_rows = proj_ref[0, keys, at + 2 * HEAD_DIM : at + 3 * HEAD_DIM]
        scores = nt(key_rows, queries)
        peak = jnp.max(scores, axis=0, keepdims=True)
        weights = jnp.exp2((scores - peak) * (KEY_SCALE * LOG2E))
        total = jnp.sum(weights, axis=0, keepdims=True)
        mixed_t = nn(value_rows.T, weights.astype(jnp.bfloat16)) / total
        lse_ref[0, head : head + 1, rows] = peak * (KEY_SCALE * LOG2E) + jnp.log2(total)
        return mixed_t.T

    def step(index, _):
        start = pl.multiple_of(index * chunk, chunk)
        outs = [part(head, start) for head in range(heads)]
        outs = jnp.concatenate(outs, axis=1).astype(jnp.bfloat16)
        for spot in range(chunk // home):
            target = index * (chunk // home) + spot
            mixed_ref[(group - target + groups) % groups, 0] = outs[spot * home : (spot + 1) * home]
        return 0

    lax.fori_loop(0, seq // chunk, step, 0, unroll=True)


def attend(projected, row, mixed, heads, chunk, groups, order):
    seq, width = projected.shape[1:]
    split = row == 0
    kernel = functools.partial(attend_kernel, heads, chunk, groups, split)
    earlier = [] if mixed is None else [mixed]
    return call(
        kernel if mixed is None else lambda p, _, *refs: kernel(p, *refs),
        [
            shape_of((groups, 2, seq // groups, heads * HEAD_DIM), jnp.bfloat16),
            shape_of((1, heads, seq), jnp.float32),
        ],
        [pl.BlockSpec((1, seq, width), lambda i: (row, 0, 0))] + [pl.BlockSpec(memory_space=pl.ANY)] * len(earlier),
        [
            pl.BlockSpec((groups, 1, seq // groups, heads * HEAD_DIM), lambda i: (0, row, 0, 0)),
            pl.BlockSpec((1, heads, seq), lambda i: (0, 0, 0)),
        ],
        grid=(1,),
        name="attend_split" if split else "attend_whole",
        micros=6 if split else 16,
        order=order,
        aliases={} if mixed is None else {1: 0},
    )(projected, *earlier)


def attend_back_kernel(heads, chunk, groups, split, proj_ref, lse_ref, pieces_ref, out_ref, dk_ref, dv_ref, grad_ref):
    seq = proj_ref.shape[1]
    home = seq // groups
    group = lax.axis_index("head")
    width = 3 * HEAD_DIM
    key_count = chunk if split else seq
    for spot in range(groups):
        grad_ref[spot * home : (spot + 1) * home, :] = pieces_ref[(group - spot + groups) % groups, 0]

    def part(head, start, key_turned=None):
        at = head * width
        rows = pl.ds(start, chunk)
        keys = pl.ds(start if split else 0, key_count)
        queries = proj_ref[0, rows, at : at + HEAD_DIM]
        key_rows = proj_ref[0, keys, at + HEAD_DIM : at + 2 * HEAD_DIM]
        value_rows = proj_ref[0, keys, at + 2 * HEAD_DIM : at + 3 * HEAD_DIM]
        key_turned = key_rows.T if key_turned is None else key_turned
        grads = grad_ref[rows, head * HEAD_DIM : (head + 1) * HEAD_DIM]
        scores = nt(key_rows, queries)
        probs = jnp.exp2(scores * (KEY_SCALE * LOG2E) - lse_ref[0, head : head + 1, rows])
        grad_probs = nt(value_rows, grads)
        inner = jnp.sum(probs * grad_probs, axis=0, keepdims=True)
        grad_raw = (probs * (grad_probs - inner) * KEY_SCALE).astype(jnp.bfloat16)
        grad_values = nn(probs.astype(jnp.bfloat16), grads)
        grad_keys = nn(grad_raw, queries)
        grad_queries = nn(key_turned, grad_raw).T
        return grad_queries, grad_keys, grad_values

    if not split:
        for head in range(heads):
            at = head * width
            dk_ref[...] = jnp.zeros_like(dk_ref)
            dv_ref[...] = jnp.zeros_like(dv_ref)
            key_turned = proj_ref[0, :, at + HEAD_DIM : at + 2 * HEAD_DIM].T

            def step(index, _, head=head, at=at, key_turned=key_turned):
                start = pl.multiple_of(index * chunk, chunk)
                dq, dk, dv = part(head, start, key_turned)
                out_ref[0, pl.ds(start, chunk), at : at + HEAD_DIM] = dq.astype(jnp.bfloat16)
                dk_ref[...] += dk
                dv_ref[...] += dv
                return 0

            lax.fori_loop(0, seq // chunk, step, 0, unroll=True)
            both = jnp.concatenate([dk_ref[...], dv_ref[...]], axis=1).astype(jnp.bfloat16)
            out_ref[0, :, at + HEAD_DIM : at + 3 * HEAD_DIM] = both
    else:

        def step(index, _):
            start = pl.multiple_of(index * chunk, chunk)
            outs = [t for head in range(heads) for t in part(head, start)]
            out_ref[0, pl.ds(start, chunk), :] = jnp.concatenate(outs, axis=1).astype(jnp.bfloat16)
            return 0

        lax.fori_loop(0, seq // chunk, step, 0, unroll=True)


def attend_back(projected, row, lse, grads, heads, chunk, groups, order):
    seq, width = projected.shape[1:]
    split = row == 0

    return call(
        functools.partial(attend_back_kernel, heads, chunk, groups, split),
        shape_of((1, seq, width), jnp.bfloat16),
        [
            pl.BlockSpec((1, seq, width), lambda i: (row, 0, 0)),
            pl.BlockSpec((1, heads, seq), lambda i: (0, 0, 0)),
            pl.BlockSpec((groups, 1, seq // groups, heads * HEAD_DIM), lambda i: (0, row, 0, 0)),
        ],
        pl.BlockSpec((1, seq, width), lambda i: (0, 0, 0)),
        grid=(1,),
        scratch=[pltpu.VMEM((seq, HEAD_DIM), jnp.float32)] * 2
        + [pltpu.VMEM((seq, heads * HEAD_DIM), jnp.bfloat16)],
        name="attend_back_split" if split else "attend_back_whole",
        micros=8 if split else 24,
        order=order,
    )(projected, lse, grads)


norm_eps = 1e-06
gelu_coeff = 0.7978845608028654
VMEM_BYTES = 58 * 1024 * 1024
UNIT_TILE = 384


def tn(left_side, right_side):
    return lax.dot_general(
        left_side, right_side, (((0,), (0,)), ((), ())), preferred_element_type=jnp.float32
    )


def row_norm(values):
    center = jnp.mean(values, axis=-1, keepdims=True)
    shifted = values - center
    spread = jnp.mean(shifted * shifted, axis=-1, keepdims=True)
    inverse = lax.rsqrt(spread + norm_eps)
    return (shifted * inverse, inverse)


def norm_back(normed, inverse, grad_normed):
    first_mean = jnp.mean(grad_normed, axis=-1, keepdims=True)
    second_mean = jnp.mean(grad_normed * normed, axis=-1, keepdims=True)
    return inverse * (grad_normed - first_mean - normed * second_mean)


def silu_act(values):
    return values / (1.0 + jnp.exp(-values))


def weight_of(micros):
    return pl.CostEstimate(flops=int(micros * 2.2e10), bytes_accessed=int(micros * 6.6e7), transcendentals=0)


def call(kernel, out_shape, in_specs, out_specs, grid=(), prefetch=0, scratch=(), name=None, micros=1, order=(), aliases={}):
    first = prefetch + len(in_specs)

    def ordered(*refs):
        kernel(*refs[:first], *refs[first + len(order) :])

    run = pl.pallas_call(
        ordered if order else kernel,
        grid_spec=pltpu.PrefetchScalarGridSpec(
            num_scalar_prefetch=prefetch,
            grid=grid,
            in_specs=list(in_specs) + [pl.BlockSpec(memory_space=pl.ANY)] * len(order),
            out_specs=out_specs,
            scratch_shapes=scratch,
        ),
        out_shape=out_shape,
        input_output_aliases=aliases,
        compiler_params=pltpu.CompilerParams(vmem_limit_bytes=VMEM_BYTES),
        cost_estimate=weight_of(micros),
        name=name,
    )
    return lambda *arrays: run(*arrays, *order)


def hold(values, *order, micros=0):
    run = pl.pallas_call(
        lambda *refs: None,
        in_specs=[pl.BlockSpec(memory_space=pl.ANY)] * (1 + len(order)),
        out_specs=pl.BlockSpec(memory_space=pl.ANY),
        out_shape=shape_of(values.shape, values.dtype),
        input_output_aliases={0: 0},
        cost_estimate=weight_of(micros),
        name="hold",
    )
    return run(values, *order)


def whole(shape):
    return pl.BlockSpec(shape, lambda *_: (0,) * len(shape))


SCALARS = pl.BlockSpec(memory_space=pltpu.SMEM)
shape_of = jax.ShapeDtypeStruct


class Links:
    def __init__(self, heads, batches):
        self.heads = heads
        self.batches = batches
        bits = batches.bit_length() - 1
        self.levels = bits - 1
        first = list(range(bits - 1, 0, -1))
        self.orders = (first, first[1:] + first[:1])

    def fetch(self, values, distance):
        count = self.heads
        return lax.ppermute(values, "head", [((i + distance) % count, i) for i in range(count)])

    def send(self, values, distance):
        count = self.heads
        return lax.ppermute(values, "head", [(i, (i + distance) % count) for i in range(count)])

    def head_swap(self, values, bit):
        return lax.ppermute(values, "head", [(i, i ^ (1 << bit)) for i in range(self.heads)])

    def head_cube(self, values, orders):
        for bit in range(self.heads.bit_length() - 1):
            more = self.head_swap(values, bit)
            if bit < len(orders):
                more = hold(more, orders[bit])
            values = jnp.concatenate([values, more], axis=0)
        return values

    def head_gather(self, values):
        return [values] + [self.fetch(values, distance) for distance in range(1, self.heads)]

    def by_head(self, pieces):
        values = pieces[0]
        rows = values.shape[0]
        held = jnp.zeros((self.heads * rows,) + values.shape[1:], values.dtype)
        for distance in range(self.heads):
            held = lax.dynamic_update_slice_in_dim(held, pieces[distance], self.at_head(distance) * rows, 0)
        return held

    def core_swap(self, values):
        return lax.ppermute(values, "batch", [(i, i ^ 1) for i in range(self.batches)])

    def link_swap(self, values, level):
        pairs = [(i, i ^ (1 << self.orders[i & 1][level])) for i in range(self.batches)]
        return lax.ppermute(values, "batch", pairs)

    def owner(self, spot):
        batch = lax.axis_index("batch")
        half = spot >> self.levels
        masks = [
            sum(1 << order[level] for level in range(self.levels) if spot >> level & 1)
            for order in self.orders
        ]
        mask = jnp.where(batch % 2 == half, masks[0], masks[1])
        return (batch ^ half) ^ mask

    def place(self, index):
        batch = lax.axis_index("batch")
        way = batch ^ index
        half = way & 1
        spots = [
            sum(((way >> order[level]) & 1) << level for level in range(self.levels))
            for order in self.orders
        ]
        return (half << self.levels) + jnp.where((batch & 1) == half, spots[0], spots[1])

    def gather_levels(self, values, order=()):
        pieces = [values]
        for level in range(self.levels):
            joined = pieces[0] if level == 0 else jnp.concatenate(pieces, axis=0)
            more = self.link_swap(joined, level)
            if level == 0 and order:
                more = hold(more, *order)
            pieces = [joined, more]
        return pieces

    def gather_batch(self, values):
        own = jnp.concatenate(self.gather_levels(values), axis=0)
        return jnp.concatenate([own, self.core_swap(own)], axis=0)

    def reduce_cores(self, pieces, *order):
        sums = []
        for mine, other in zip(pieces[:2], pieces[2:]):
            more = self.core_swap(other)
            if order:
                more = hold(more, *order)
            sums.append((mine.astype(jnp.float32) + more.astype(jnp.float32)).astype(jnp.bfloat16))
        return sums

    def reduce_first(self, kept, *order):
        more = self.link_swap(kept[1], self.levels - 1)
        if order:
            more = hold(more, *order)
        return (kept[0].astype(jnp.float32) + more.astype(jnp.float32)).astype(jnp.bfloat16)

    def reduce_rest(self, total, *order):
        for level in reversed(range(self.levels - 1)):
            half = total.shape[0] // 2
            more = self.link_swap(total[half:], level)
            if order:
                more = hold(more, *order)
                order = ()
            total = (total[:half].astype(jnp.float32) + more.astype(jnp.float32)).astype(jnp.bfloat16)
        return total

    def by_owner(self, values):
        return jnp.concatenate(
            [lax.dynamic_index_in_dim(values, self.owner(i), 0) for i in range(self.batches)]
        )

    def by_index(self, values):
        return jnp.concatenate(
            [lax.dynamic_index_in_dim(values, self.place(i), 0) for i in range(self.batches)]
        )

    def at_head(self, distance):
        return (lax.axis_index("head") + distance) % self.heads


def mod_kernel(quarter, units_here, seg_ref, item_ref, cond_ref, ada_ref, bias_ref, in_bias_ref, table_ref, info_ref):
    starts = [[seg_ref[row * SEQ + spot * quarter] for spot in range(4)] for row in range(2)]
    first_splits = starts[0][0] != starts[0][3]
    ids = [jnp.where(first_splits, starts[1][0], starts[0][0])] + [
        jnp.where(first_splits, starts[0][spot], starts[1][spot]) for spot in range(4)
    ]
    classes = [item_ref[one] for one in ids]
    info_ref[0] = jnp.where(first_splits, 0, 1)
    info_ref[1] = lax.axis_index("head")
    info_ref[2] = 0
    for spot in range(5):
        info_ref[3 + spot] = classes[spot]
    cond_low = silu_act(cond_ref[...].astype(jnp.float32)).astype(jnp.bfloat16)
    count = cond_low.shape[0]
    row_spot = lax.broadcasted_iota(jnp.int32, (8, count), 0)
    wanted = jnp.full((8, count), count, jnp.int32)
    for spot in range(5):
        wanted = jnp.where(row_spot == spot, classes[spot], wanted)
    hits = (lax.broadcasted_iota(jnp.int32, (8, count), 1) == wanted).astype(jnp.float32)
    rows = nn(hits.astype(jnp.bfloat16), cond_low).astype(jnp.bfloat16)
    table_ref[...] = nt(rows, ada_ref[...]) + bias_ref[...]
    table_ref[5:6, :units_here] = in_bias_ref[...]


def project_kernel(heads, quarter, info_ref, table_rel_ref, tokens_ref, weight_ref, bias_ref, attn_in_ref, projected_ref, table_ref):
    block = pl.program_id(0)
    width = tokens_ref.shape[1]
    columns = table_rel_ref.shape[2]

    @pl.when(block == 0)
    def _():
        for head in range(heads):
            spot = (head - lax.axis_index("head") + heads) % heads
            table_ref[:, head * columns : (head + 1) * columns] = table_rel_ref[spot]

    quarter_rows = tokens_ref.shape[0] // 2
    for half in range(2):
        here = slice(half * quarter_rows, (half + 1) * quarter_rows)
        spot = 2 * block + half
        row = jnp.where(spot < 4, 1 + spot % 4, 0)
        normed, _ = row_norm(tokens_ref[here, :].astype(jnp.float32))
        shift = table_ref[pl.ds(row, 1), :width]
        scale = table_ref[pl.ds(row, 1), width : 2 * width]
        attn_in = (normed * (1.0 + scale) + shift).astype(jnp.bfloat16)
        attn_in_ref[here, :] = attn_in
        projected_ref[here, :] = (nt(attn_in, weight_ref[...]) + bias_ref[...]).astype(jnp.bfloat16)


def home_row(info_ref, row, home, quarter):
    return jnp.where(row == 0, 1 + info_ref[1] * home // quarter, 0)


def enter_kernel(link, quarter, info_ref, table_ref, mixed_ref, proj_ref, tokens_ref, grad_ref, bias_ref,
                 attn_ref, stream_ref, mlp_in_ref, grad_mlp_ref, mixed_home_ref, proj_true_ref, grad_sum_ref):
    row = pl.program_id(0)
    heads = link.heads
    home, width = tokens_ref.shape[1:]
    share = width // heads
    slice_rows = proj_ref.shape[2]
    head = lax.axis_index("head")

    @pl.when(row == 0)
    def _():
        grad_sum_ref[...] = jnp.zeros_like(grad_sum_ref)
        for index in range(link.batches):
            first = index * slice_rows
            count = min(slice_rows, share - first)
            if count > 0:
                place = link.place(index)
                for spot in range(heads):
                    piece = proj_ref[place, (spot - head + heads) % heads]
                    at = spot * share + first
                    proj_true_ref[at : at + count, :] = piece[:count]

    for spot in range(heads):
        piece = mixed_ref[(spot - head + heads) % heads, 0]
        mixed_home_ref[0, :, spot * share : (spot + 1) * share] = piece
    spot = home_row(info_ref, row, home, quarter)

    def mod(group):
        return table_ref[pl.ds(spot, 1), group * width : (group + 1) * width]

    attn = nn(mixed_home_ref[0], proj_true_ref[...]) + bias_ref[...]
    attn_ref[0] = attn
    stream = tokens_ref[0].astype(jnp.float32) + mod(2) * attn
    stream_ref[0] = stream
    normed, _ = row_norm(stream.astype(jnp.bfloat16).astype(jnp.float32))
    mlp_in_ref[0] = (normed * (1.0 + mod(4)) + mod(3)).astype(jnp.bfloat16)
    grad_mlp = (grad_ref[0].astype(jnp.float32) * mod(5)).astype(jnp.bfloat16)
    grad_mlp_ref[0] = grad_mlp
    grad_sum_ref[...] += jnp.sum(grad_mlp.astype(jnp.float32), axis=0, keepdims=True)


def expand_kernel(steps, mlp_in_ref, bias_ref, *refs):
    pieces, (hidden_ref, slope_ref) = refs[:-2], refs[-2:]
    step = pl.program_id(0)
    for spot, piece_ref in enumerate(pieces):

        @pl.when(step // steps == spot)
        def _(piece_ref=piece_ref):
            pre = nt(mlp_in_ref[...], piece_ref[...]) + bias_ref[...]
            square = pre * pre
            bent = jnp.tanh(gelu_coeff * (pre + 0.044715 * square * pre))
            half = 0.5 * (1.0 + bent)
            hidden_ref[...] = (pre * half).astype(jnp.bfloat16)
            inner = gelu_coeff * (1.0 + (3.0 * 0.044715) * square)
            slope_ref[...] = (half + 0.5 * pre * (1.0 - bent * bent) * inner).astype(jnp.bfloat16)


def contract_kernel(link, quarter, info_ref, table_ref, grad_mlp_ref, out_bias_ref, hidden_ref, slope_ref,
                    tokens_grad_ref, stream_ref, attn_ref, proj_ref, *refs):
    count = 4
    ins, outs = refs[:count], refs[count : 2 * count]
    (grad_pre_ref, pre_sum_ref, block_ref, stream_grad_ref, grad_attn_ref, grad_mixed_ref, sums_ref, attn_sum_ref,
     mlp_acc, grad_acc, in_buf, out_buf, hidden_buf, slope_buf, pre_buf, tokens_buf, stream_buf, attn_buf, proj_buf,
     piece_sems, pre_sems, late_sems) = refs[2 * count :]
    heads = link.heads
    rows, home, width = stream_ref.shape
    share = width // heads
    units = ins[0].shape[0]
    tile = UNIT_TILE

    def piece_copies(piece):
        slot = piece % 2
        columns = pl.ds(piece * units, units)
        pairs = (
            (outs[piece], out_buf.at[slot]),
            (slope_ref.at[:, columns], slope_buf.at[slot]),
            (hidden_ref.at[:, columns], hidden_buf.at[slot]),
            (ins[piece], in_buf.at[slot]),
        )
        return [
            pltpu.make_async_copy(source, target, piece_sems.at[kind, slot])
            for kind, (source, target) in enumerate(pairs)
        ]

    def pre_copy(piece):
        slot = piece % 2
        return pltpu.make_async_copy(
            pre_buf.at[slot], grad_pre_ref.at[:, pl.ds(piece * units, units)], pre_sems.at[slot]
        )

    start = pl.multiple_of(info_ref[1] * home, 8)
    late = [
        pltpu.make_async_copy(tokens_grad_ref.at[:, pl.ds(start, home), :], tokens_buf, late_sems.at[0]),
        pltpu.make_async_copy(stream_ref, stream_buf, late_sems.at[1]),
        pltpu.make_async_copy(attn_ref, attn_buf, late_sems.at[2]),
        pltpu.make_async_copy(proj_ref, proj_buf, late_sems.at[3]),
    ]
    for piece in range(2):
        for copy in piece_copies(piece):
            copy.start()
    for copy in late:
        copy.start()
    for piece in range(count):
        slot = piece % 2
        copies = piece_copies(piece)
        copies[0].wait()
        copies[1].wait()
        if piece >= 2:
            pre_copy(piece - 2).wait()
        for at in range(0, units, tile):
            here = slice(at, at + tile)
            grad_pre = nt(grad_mlp_ref[...], out_buf[slot, here, :]) * slope_buf[slot, :, here].astype(jnp.float32)
            grad_pre = grad_pre.astype(jnp.bfloat16)
            pre_buf[slot, :, here] = grad_pre
            total = jnp.sum(grad_pre.astype(jnp.float32), axis=0, keepdims=True)
            pre_sum_ref[:, piece * units + at : piece * units + at + tile] = total
        pre_copy(piece).start()
        copies[2].wait()
        copies[3].wait()
        for at in range(0, width, tile):
            here = slice(at, at + tile)
            mlp = nn(hidden_buf[slot], out_buf[slot, :, here])
            grad = nn(pre_buf[slot], in_buf[slot, :, here])
            mlp_acc[:, here] = mlp if piece == 0 else mlp_acc[:, here] + mlp
            grad_acc[:, here] = grad if piece == 0 else grad_acc[:, here] + grad
        if piece + 2 < count:
            for copy in piece_copies(piece + 2):
                copy.start()
    for copy in late:
        copy.wait()
    head = lax.axis_index("head")
    attn_sum = jnp.zeros((1, width), jnp.float32)
    for row in range(rows):
        spot = home_row(info_ref, row, home, quarter)

        def mod(group):
            return table_ref[pl.ds(spot, 1), group * width : (group + 1) * width]

        here = slice(row * home, (row + 1) * home)
        grad_out = tokens_buf[row_at(row, info_ref)].astype(jnp.float32)
        stream = stream_buf[row]
        mlp = mlp_acc[here, :] + out_bias_ref[...]
        block = (stream + mod(5) * mlp).astype(jnp.bfloat16)
        for other in range(heads):
            block_ref[(other - head + heads) % heads, row] = block[:, other * share : (other + 1) * share]
        normed, inverse = row_norm(stream.astype(jnp.bfloat16).astype(jnp.float32))
        grad_in = grad_acc[here, :]
        sums_ref[row, 1:2] = jnp.sum(grad_in, axis=0, keepdims=True)
        sums_ref[row, 2:3] = jnp.sum(grad_in * normed, axis=0, keepdims=True)
        sums_ref[row, 3:4] = jnp.sum(grad_out * mlp, axis=0, keepdims=True)
        stream_grad = grad_out + norm_back(normed, inverse, grad_in * (1.0 + mod(4)))
        stream_grad_ref[row] = stream_grad
        rounded = stream_grad.astype(jnp.bfloat16).astype(jnp.float32)
        sums_ref[row, 0:1] = jnp.sum(rounded * attn_buf[row], axis=0, keepdims=True)
        grad_attn = (rounded * mod(2)).astype(jnp.bfloat16)
        grad_attn_ref[row] = grad_attn
        attn_sum += jnp.sum(grad_attn.astype(jnp.float32), axis=0, keepdims=True)
        grad_mixed = nt(grad_attn, proj_buf[...]).astype(jnp.bfloat16)
        for other in range(heads):
            grad_mixed_ref[(other - head + heads) % heads, row] = grad_mixed[:, other * share : (other + 1) * share]
    attn_sum_ref[...] = attn_sum
    for piece in range(count - 2, count):
        pre_copy(piece).wait()


def row_at(spot, info_ref):
    return jnp.where(spot == 0, info_ref[0], 1 - info_ref[0])


def leave_kernel(link, quarter, at_row, info_ref, table_ref, grad_ref, weight_ref, tokens_ref, stream_grad_ref,
                 shares_ref, sums_ref, term_ref):
    block = pl.program_id(0)
    heads = link.heads
    width = tokens_ref.shape[1]
    share = width // heads
    home = stream_grad_ref.shape[1]
    start = info_ref[1] * home
    for half in range(2):
        here = slice(half * quarter, (half + 1) * quarter)
        spot = 2 * block + half
        row = 1 + spot if at_row == 0 else 0
        scale = table_ref[pl.ds(row, 1), width : 2 * width]
        grad_in = nn(grad_ref[here, :], weight_ref[...])
        normed, inverse = row_norm(tokens_ref[here, :].astype(jnp.float32))
        sums_ref[half, 0:1] = jnp.sum(grad_in, axis=0, keepdims=True)
        sums_ref[half, 1:2] = jnp.sum(grad_in * normed, axis=0, keepdims=True)
        term_ref[here, :] = norm_back(normed, inverse, grad_in * (1.0 + scale))

    @pl.when(start // (2 * quarter) == block)
    def _():
        rows = pl.ds(pl.multiple_of(start % (2 * quarter), 8), home)
        term_ref[rows, :] += stream_grad_ref[0]

    for half in range(2):
        here = slice(half * quarter, (half + 1) * quarter)
        low = term_ref[here, :].astype(jnp.bfloat16)
        for head in range(heads):
            shares_ref[head, here, :] = low[:, head * share : (head + 1) * share]


def unit_grads_kernel(steps, left_ref, right_ref, *outs):
    for spot in range(4):

        @pl.when(pl.program_id(0) // steps == spot)
        def _(spot=spot):
            outs[spot][...] = tn(left_ref[...], right_ref[...]).astype(jnp.bfloat16)


def unit_grads(left, right, order=()):
    count, total = left.shape
    width = right.shape[1]
    piece = total // 4
    steps = piece // UNIT_TILE

    def spec(spot):
        return pl.BlockSpec((UNIT_TILE, width), lambda i: (jnp.clip(i - spot * steps, 0, steps - 1), 0))

    return call(
        functools.partial(unit_grads_kernel, steps),
        [shape_of((piece, width), jnp.bfloat16)] * 4,
        [pl.BlockSpec((count, UNIT_TILE), lambda i: (0, i)), whole((count, width))],
        [spec(i) for i in range(4)],
        grid=(4 * steps,),
        name="unit_grads", micros=14,
        order=order,
    )(left, right)


def place_rows_kernel(link, slices_ref, out_ref):
    rows = slices_ref.shape[1]
    for index in range(link.batches):
        count = min(rows, out_ref.shape[0] - index * rows)
        if count > 0:
            piece = slices_ref[link.place(index)].astype(jnp.float32)
            out_ref[index * rows : index * rows + count, :] = piece[:count]


def place_rows(link, slices, rows):
    width = slices.shape[2]
    tile = 384
    return call(
        functools.partial(place_rows_kernel, link),
        shape_of((rows, width), jnp.float32),
        [pl.BlockSpec(slices.shape[:2] + (tile,), lambda i: (0, 0, i))],
        pl.BlockSpec((rows, tile), lambda i: (0, i)),
        grid=(width // tile,),
        name="place_rows", micros=0,
    )(slices)


def place_columns_kernel(link, slices_ref, out_ref, rows_ref):
    rows = slices_ref.shape[1]
    for index in range(link.batches):
        rows_ref[index * rows : (index + 1) * rows, :] = slices_ref[link.place(index)].astype(jnp.float32)
    out_ref[...] = rows_ref[...].T


def place_columns(link, slices):
    batches, rows, width = slices.shape
    tile = 128
    return call(
        functools.partial(place_columns_kernel, link),
        shape_of((width, batches * rows), jnp.float32),
        [pl.BlockSpec((batches, rows, tile), lambda i: (0, 0, i))],
        pl.BlockSpec((tile, batches * rows), lambda i: (i, 0)),
        grid=(width // tile,),
        scratch=[pltpu.VMEM((batches * rows, tile), jnp.float32)],
        name="place_columns", micros=0,
    )(slices)


def lay_home_kernel(heads, info_ref, blocks_ref, out_ref):
    home = blocks_ref.shape[2]
    head = lax.axis_index("head")
    for spot in range(heads):
        for row in range(2):
            out_ref[row_at(row, info_ref), spot * home : (spot + 1) * home, :] = blocks_ref[(head - spot + heads) % heads, row]


def shards(
    tokens,
    segments,
    item_cond,
    condition,
    ada_weight,
    ada_bias,
    qkv_weight,
    qv_bias,
    proj_weight,
    proj_bias,
    in_weight,
    in_bias,
    out_weight,
    out_bias,
    cotangent,
):
    low = jnp.bfloat16
    full = jnp.float32
    heads, batches = lax.axis_size("head"), lax.axis_size("batch")
    link = Links(heads, batches)
    batch = lax.axis_index("batch")
    token_count, width = tokens.shape
    rows = token_count // SEQ
    quarter = SEQ // 4
    home = SEQ // heads
    home_count = rows * home
    share = width // heads
    heads_here = qv_bias.shape[0] // (2 * HEAD_DIM)
    qkv_here = 3 * heads_here * HEAD_DIM
    units_here = in_weight.shape[1]
    units = units_here // batches
    ada_here = ada_weight.shape[1]
    cond_count = condition.shape[0]

    ada_t = ada_weight.T
    qkv_t = qkv_weight.T
    table_part, info = call(
        functools.partial(mod_kernel, quarter, units_here),
        [shape_of((8, ada_here), full), shape_of((8,), jnp.int32)],
        [SCALARS, SCALARS] + [whole(s) for s in ((cond_count, width), (ada_here, width), (1, ada_here), (1, units_here))],
        [whole((8, ada_here)), SCALARS],
        name="modulation", micros=5,
    )(segments, item_cond, condition, ada_t, ada_bias.astype(full)[None], in_bias.astype(full)[None])
    table_rel = jnp.stack([table_part] + [link.fetch(table_part, j) for j in range(1, heads)])

    slice_rows = -(-share // (8 * batches)) * 8
    proj_pad = jnp.pad(proj_weight, ((0, slice_rows * batches - share), (0, 0)))
    in_slice = lax.dynamic_slice_in_dim(in_weight, batch * units, units, 1).T
    out_slice = lax.dynamic_slice_in_dim(out_weight, batch * units, units, 0)
    in_gathered = lax.all_gather(in_slice, "head", axis=0, tiled=True)
    out_gathered = lax.all_gather(out_slice, "head", axis=0, tiled=True)
    def tokens_block(i, info_ref):
        return (2 * row_at(i // 2, info_ref) + i % 2, 0)

    bias_pairs = qv_bias.astype(full).reshape(heads_here, 2, HEAD_DIM)
    full_bias = jnp.concatenate(
        [bias_pairs[:, :1], jnp.zeros((heads_here, 1, HEAD_DIM), full), bias_pairs[:, 1:]], axis=1
    ).reshape(1, -1)
    attn_in, projected, table = call(
        functools.partial(project_kernel, heads, quarter),
        [
            shape_of((token_count, width), low),
            shape_of((token_count, qkv_here), low),
            shape_of((8, 6 * width), full),
        ],
        [
            whole((heads, 8, ada_here)),
            pl.BlockSpec((2 * quarter, width), tokens_block),
            whole((qkv_here, width)),
            whole((1, qkv_here)),
        ],
        [
            pl.BlockSpec((2 * quarter, width), lambda i, _: (i, 0)),
            pl.BlockSpec((2 * quarter, qkv_here), lambda i, _: (i, 0)),
            whole((8, 6 * width)),
        ],
        grid=(2 * rows,),
        prefetch=1,
        name="project", micros=13,
    )(info, table_rel, tokens, qkv_t, full_bias)
    projected = projected.reshape(rows, SEQ, qkv_here)
    proj_slice = hold(lax.dynamic_slice_in_dim(proj_pad, batch * slice_rows, slice_rows, 0), table_rel)
    proj_rel = jnp.stack(
        [proj_slice] + [hold(link.fetch(proj_slice, j), projected) for j in range(1, heads)]
    )[None]
    mixed = None
    log_totals = []
    for row in range(rows):
        order = [in_gathered] if row == 1 else []
        mixed, log_total = attend(projected, row, mixed, heads_here, quarter, heads, order)
        log_totals.append(log_total)
        if row < link.levels:
            proj_rel = jnp.concatenate([proj_rel, hold(link.link_swap(proj_rel, row), log_total)], axis=0)
        if row == 0:
            in_gathered = hold(in_gathered, log_total)
    in_held = link.gather_levels(in_gathered, [log_totals[1]])
    for level in range(rows, link.levels):
        proj_rel = jnp.concatenate([proj_rel, link.link_swap(proj_rel, level)], axis=0)
    proj_all = jnp.concatenate([proj_rel, link.core_swap(proj_rel)], axis=0)
    out_gathered = hold(out_gathered, in_held[0])
    mixed = hold(mixed, out_gathered, proj_all, micros=20)
    mixed_all = jnp.stack([mixed[0]] + [link.fetch(mixed[j], j) for j in range(1, heads)])

    out_held = link.gather_levels(out_gathered)
    out_pieces = out_held + [link.core_swap(piece) for piece in out_held]
    tokens_rows = tokens.reshape(rows, SEQ, width)
    grad_rows = cotangent.reshape(rows, SEQ, width)
    home_spec = pl.BlockSpec((1, home, width), lambda i, info_ref: (row_at(i, info_ref), info_ref[1], 0))
    row_spec = pl.BlockSpec((1, home, width), lambda i, _: (i, 0, 0))
    attn, stream, mlp_in, grad_mlp, mixed_home, proj_true, grad_sum = call(
        functools.partial(enter_kernel, link, quarter),
        [
            shape_of((rows, home, width), full),
            shape_of((rows, home, width), full),
            shape_of((rows, home, width), low),
            shape_of((rows, home, width), low),
            shape_of((rows, home, width), low),
            shape_of((width, width), low),
            shape_of((1, width), full),
        ],
        [
            whole((8, 6 * width)),
            pl.BlockSpec((heads, 1, home, share), lambda i, _: (0, i, 0, 0)),
            whole(proj_all.shape),
            home_spec,
            home_spec,
            whole((1, width)),
        ],
        [row_spec] * 5 + [whole((width, width)), whole((1, width))],
        grid=(rows,),
        prefetch=1,
        name="enter", micros=9,
        order=[out_held[0]],
    )(info, table, mixed_all, proj_all, tokens_rows, grad_rows, proj_bias.astype(full)[None])

    in_held[1] = hold(in_held[1], mlp_in)
    in_pieces = in_held + [link.core_swap(piece) for piece in in_held]
    mlp_in = mlp_in.reshape(home_count, width)
    grad_mlp = grad_mlp.reshape(home_count, width)
    in_bias_all = table[5].reshape(heads, -1)[:, :units_here]
    in_bias_all = in_bias_all.reshape(heads, batches, units)
    in_bias_all = link.by_owner(in_bias_all.transpose(1, 0, 2)).reshape(1, -1)
    piece_rows = in_pieces[0].shape[0]
    unit_count = 4 * piece_rows
    steps = piece_rows // UNIT_TILE

    def piece_spec(spot):
        return pl.BlockSpec((UNIT_TILE, width), lambda i, *_: (jnp.clip(i - spot * steps, 0, steps - 1), 0))

    tile_spec = pl.BlockSpec((home_count, UNIT_TILE), lambda i, *_: (0, i))
    bias_spec = pl.BlockSpec((1, UNIT_TILE), lambda i, *_: (0, i))
    hidden, slope = call(
        functools.partial(expand_kernel, 1),
        [shape_of((home_count, unit_count), low)] * 2,
        [whole((home_count, width)), pl.BlockSpec((1, piece_rows), lambda i: (0, i))]
        + [whole((piece_rows, width))] * 4,
        [pl.BlockSpec((home_count, piece_rows), lambda i: (0, i))] * 2,
        grid=(4,),
        name="expand", micros=20,
        order=[out_held[0]],
    )(mlp_in, in_bias_all, *in_pieces)

    out_parts = unit_grads(hidden, grad_mlp, order=[out_pieces[2]])

    stay = pl.BlockSpec((rows, home, width), lambda *_: (0, 0, 0))
    by_head = whole((heads, rows, home, share))
    grad_pre, pre_sum, block_home, stream_grad, grad_attn, grad_mixed, home_sums, attn_sum = call(
        functools.partial(contract_kernel, link, quarter),
        [
            shape_of((home_count, unit_count), low),
            shape_of((1, unit_count), full),
            shape_of((heads, rows, home, share), low),
            shape_of((rows, home, width), full),
            shape_of((rows, home, width), low),
            shape_of((heads, rows, home, share), low),
            shape_of((rows, 4, width), full),
            shape_of((1, width), full),
        ],
        [SCALARS, whole((8, 6 * width)), whole((home_count, width)), whole((1, width))]
        + [pl.BlockSpec(memory_space=pl.ANY)] * 14,
        [
            pl.BlockSpec(memory_space=pl.ANY),
            whole((1, unit_count)),
            by_head,
            stay,
            stay,
            by_head,
            whole((rows, 4, width)),
            whole((1, width)),
        ],
        scratch=[
            pltpu.VMEM((home_count, width), full),
            pltpu.VMEM((home_count, width), full),
            pltpu.VMEM((2, piece_rows, width), low),
            pltpu.VMEM((2, piece_rows, width), low),
            pltpu.VMEM((2, home_count, piece_rows), low),
            pltpu.VMEM((2, home_count, piece_rows), low),
            pltpu.VMEM((2, home_count, piece_rows), low),
            pltpu.VMEM((rows, home, width), low),
            pltpu.VMEM((rows, home, width), full),
            pltpu.VMEM((rows, home, width), full),
            pltpu.VMEM((width, width), low),
            pltpu.SemaphoreType.DMA((4, 2)),
            pltpu.SemaphoreType.DMA((2,)),
            pltpu.SemaphoreType.DMA((4,)),
        ],
        name="contract", micros=44,
        order=[out_parts[0]],
    )(info, table, grad_mlp, out_bias.astype(full)[None], hidden, slope, grad_rows, stream, attn, proj_true,
      *in_pieces, *out_pieces)
    mixed_sends = [link.send(grad_mixed[j], j) for j in range(1, heads)]
    out_near = link.reduce_cores(out_parts, grad_pre)
    out_sum = link.reduce_first(out_near)
    in_parts = unit_grads(grad_pre, mlp_in, order=[out_near[1]])
    grad_mixed = jnp.stack([grad_mixed[0]] + [hold(piece, in_parts[0]) for piece in mixed_sends])
    out_slice = link.reduce_rest(out_sum)
    in_near = link.reduce_cores(in_parts, grad_mixed)
    proj_grad = tn(mixed_home.reshape(home_count, width), grad_attn.reshape(home_count, width)).astype(low)

    def head_sum(values):
        return lax.psum_scatter(values, "head", scatter_dimension=0, tiled=True)

    out_blocks = out_slice.reshape(heads, units, width)

    def out_block(distance):
        return lax.dynamic_index_in_dim(out_blocks, link.at_head(distance), 0, keepdims=False)

    out_more = [link.send(out_block(j), j) for j in range(1, heads)]
    grad_rows_low = []
    block_sums = []
    shares = None
    for row in range(rows):
        grad_row = attend_back(
            projected, row, log_totals[row], grad_mixed, heads_here, quarter, heads,
            [] if row == 0 else [sums_row, out_slice],
        )[0]
        order = list(in_near) + [out_sum]
        if row == 1:
            in_sum = link.reduce_first(in_near, grad_row)
            order = [in_sum]
        earlier = [] if shares is None else [shares]
        kernel = functools.partial(leave_kernel, link, quarter, row)
        shares, sums_row = call(
            kernel if row == 0 else lambda *refs: kernel(*refs[:6], *refs[7:]),
            [shape_of((heads, token_count, share), low), shape_of((4, 2, width), full)],
            [
                whole((8, 6 * width)),
                pl.BlockSpec((2 * quarter, qkv_here), lambda i, _: (i, 0)),
                whole((qkv_here, width)),
                pl.BlockSpec((2 * quarter, width), lambda i, info_ref, row=row: tokens_block(i + 2 * row, info_ref)),
                pl.BlockSpec((1, home, width), lambda i, _, row=row: (row, 0, 0)),
            ]
            + [pl.BlockSpec(memory_space=pl.ANY)] * len(earlier),
            [
                pl.BlockSpec((heads, 2 * quarter, share), lambda i, _, row=row: (0, i + 2 * row, 0)),
                pl.BlockSpec((2, 2, width), lambda i, _: (i, 0, 0)),
            ],
            grid=(2,),
            prefetch=1,
            scratch=[pltpu.VMEM((2 * quarter, width), full)],
            name="leave", micros=9,
            aliases={6: 0} if earlier else {},
            order=order,
        )(info, table, grad_row, qkv_t, tokens, stream_grad, *earlier)
        grad_rows_low.append(grad_row)
        block_sums.append(sums_row)
    in_slice = link.reduce_rest(in_sum, sums_row)
    out_slice_sum = out_block(0).astype(full)
    for more in out_more:
        out_slice_sum = out_slice_sum + hold(more, grad_rows_low[1]).astype(full)
    out_slice_sum = out_slice_sum.astype(low)
    grad_projected = hold(jnp.concatenate(grad_rows_low, axis=0), in_slice)

    in_slice_sum = head_sum(in_slice)
    shares = head_sum(hold(shares, in_slice_sum))[0]
    tokens_grad = jnp.where(
        info[0] == 0, shares, jnp.concatenate([shares[SEQ:], shares[:SEQ]], axis=0)
    )

    block_home = hold(block_home, grad_mixed)
    block_home = jnp.stack(
        [block_home[0]] + [hold(link.send(block_home[j], j), sums_row) for j in range(1, heads)]
    )
    block_out = call(
        functools.partial(lay_home_kernel, heads),
        shape_of((rows, SEQ, share), low),
        [whole((heads, rows, home, share))],
        whole((rows, SEQ, share)),
        prefetch=1,
        name="lay_home", micros=0,
        order=[sums_row],
    )(info, block_home).reshape(token_count, share)

    home_quarter = lax.axis_index("head") * home // quarter
    seg_spots = lax.broadcasted_iota(jnp.int32, (5, 1), 0)

    def seg_home(sums):
        placed = jnp.where(seg_spots == 1 + home_quarter, sums[0][None, :], 0.0)
        return jnp.where(seg_spots == 0, sums[1][None, :], placed)

    seg_blocks = jnp.concatenate([jnp.sum(block_sums[1], axis=0, keepdims=True), block_sums[0]], axis=0)
    seg_grads = jnp.concatenate(
        [seg_blocks[:, 0], seg_blocks[:, 1]] + [seg_home(home_sums[:, i]) for i in range(4)], axis=1
    )
    in_bias_part = link.by_index(pre_sum.reshape(batches, heads, units)).transpose(1, 0, 2)
    bias_grads = jnp.concatenate(
        [
            in_bias_part.reshape(heads, -1),
            grad_sum.reshape(heads, -1),
            attn_sum.reshape(heads, -1),
        ],
        axis=1,
    ).reshape(1, -1)
    sent = jnp.concatenate([seg_grads, bias_grads, jnp.zeros((2, 6 * width), full)], axis=0)
    sent = hold(sent, in_slice).reshape(8, heads, ada_here)

    def sent_block(distance):
        return lax.dynamic_index_in_dim(sent, link.at_head(distance), 1, keepdims=False)

    held = sent_block(0)
    for j in range(1, heads):
        held = held + link.send(sent_block(j), j)
    column_sums = jnp.sum(grad_projected.astype(full), axis=0).reshape(heads_here, 3, HEAD_DIM)
    qv_bias_part = jnp.concatenate([column_sums[:, :1], column_sums[:, 2:]], axis=1).reshape(-1)
    held = jnp.concatenate(
        [
            held[:6],
            jnp.pad(qv_bias_part, (0, ada_here - qv_bias_part.shape[0]))[None],
            jnp.pad(info[3:].astype(full), (0, ada_here - 5))[None],
        ],
        axis=0,
    )
    all_held = hold(link.gather_batch(held[None]), in_slice_sum)
    all_classes = (all_held[:, 7, :5] + 0.5).astype(jnp.int32).reshape(-1)
    class_hits = (
        lax.broadcasted_iota(jnp.int32, (cond_count, 1), 0) == all_classes[None, :]
    ).astype(full)
    mod_low = jnp.dot(
        class_hits,
        all_held[:, :5].reshape(-1, ada_here),
        precision=lax.Precision.HIGHEST,
        preferred_element_type=full,
    ).astype(low)
    bias_total = jnp.sum(all_held[:, 5], axis=0)
    qv_bias_grad = jnp.sum(all_held[:, 6, : qv_bias.shape[0]], axis=0)
    in_bias_grad = bias_total[:units_here]
    cond_f = condition.astype(full)
    ada_weight_grad = tn(mod_low, silu_act(cond_f).astype(low)).T
    ada_bias_grad = jnp.sum(mod_low.astype(full), axis=0)
    cond_part = nn(mod_low, ada_t)
    shared = jnp.pad(bias_total[units_here:], (0, width - 2 * share))
    last = jnp.concatenate([cond_part, shared[None], jnp.zeros((7, width), full)]).astype(low)
    last = jnp.stack([last] + [link.fetch(last, j) for j in range(1, heads)]).astype(full)
    cond_total = jnp.sum(last[:, :cond_count], axis=0)
    condition_grad = jax.vjp(silu_act, cond_f)[1](cond_total)[0]
    shared = last[:, cond_count]
    head = lax.axis_index("head")
    shared = jnp.concatenate(
        [lax.dynamic_index_in_dim(shared, (j - head + heads) % heads, 0) for j in range(heads)]
    )
    out_bias_grad = shared[:, :share].reshape(-1)
    proj_bias_grad = shared[:, share : 2 * share].reshape(-1)

    out_weight_grad = place_rows(link, link.gather_batch(out_slice_sum[None]), units_here)
    in_weight_grad = place_columns(link, link.gather_batch(in_slice_sum[None]))

    qkv_rows = -(-qkv_here // (16 * batches)) * 16
    qkv_grad = tn(grad_projected, attn_in.reshape(token_count, width)).astype(low)
    qkv_grad = jnp.pad(qkv_grad, ((0, qkv_rows * batches - qkv_here), (0, 0))).reshape(batches, qkv_rows, width)
    proj_grad = jnp.pad(
        proj_grad.reshape(heads, share, width), ((0, 0), (0, slice_rows * batches - share), (0, 0))
    ).reshape(heads, batches, slice_rows, width)
    proj_grad = proj_grad.transpose(1, 0, 2, 3).reshape(batches, heads * slice_rows, width)
    both = link.by_owner(jnp.concatenate([qkv_grad, proj_grad], axis=1))
    both = both.reshape(2, 2, -1, width)
    got = [link.core_swap(piece) for piece in both[1]]
    both = [(mine.astype(full) + more.astype(full)).astype(low) for mine, more in zip(both[0], got)]
    both = link.reduce_rest(link.reduce_first(both))
    proj_blocks = both[qkv_rows:].reshape(heads, slice_rows, width)

    def proj_block(distance):
        return lax.dynamic_index_in_dim(proj_blocks, link.at_head(distance), 0, keepdims=False)

    proj_sum = proj_block(0).astype(full)
    for j in range(1, heads):
        proj_sum = proj_sum + link.send(proj_block(j), j).astype(full)
    both = jnp.concatenate([both[:qkv_rows], proj_sum.astype(low)], axis=0)
    both = link.gather_batch(both[None])
    qkv_weight_grad = place_rows(link, both[:, :qkv_rows], qkv_here).T
    proj_weight_grad = place_rows(link, both[:, qkv_rows:], share)

    return (
        block_out,
        tokens_grad,
        condition_grad,
        ada_weight_grad,
        ada_bias_grad,
        qkv_weight_grad,
        qv_bias_grad,
        proj_weight_grad,
        proj_bias_grad,
        in_weight_grad,
        in_bias_grad,
        out_weight_grad,
        out_bias_grad,
    )


def solution(mesh):
    in_specs = (
        P("batch", None),
        P("batch"),
        P(),
        P(),
        P(None, "head"),
        P("head"),
        P(None, "head"),
        P("head"),
        P("head", None),
        P(),
        P(None, "head"),
        P("head"),
        P("head", None),
        P(),
        P("batch", None),
    )
    out_specs = (
        P("batch", "head"),
        P("batch", "head"),
        P(),
        P(None, "head"),
        P("head"),
        P(None, "head"),
        P("head"),
        P("head", None),
        P(),
        P(None, "head"),
        P("head"),
        P("head", None),
        P(),
    )
    return jax.shard_map(shards, mesh=mesh, in_specs=in_specs, out_specs=out_specs, check_vma=False)
```

```python
import functools
import math

import jax
import jax.numpy as jnp
from jax import lax
from jax.experimental import pallas as pl
from jax.experimental.pallas import tpu as pltpu
from jax.sharding import PartitionSpec as P

HEAD_DIM = 72
SEQ = 1024
LOG2E = 1.4426950408889634
KEY_SCALE = 1.0 / math.sqrt(HEAD_DIM)


def nt(a, b):
    return lax.dot_general(a, b, (((1,), (1,)), ((), ())), preferred_element_type=jnp.float32)


def nn(a, b):
    return lax.dot_general(a, b, (((1,), (0,)), ((), ())), preferred_element_type=jnp.float32)


def attend_kernel(heads, chunk, groups, split, proj_ref, mixed_ref, lse_ref):
    seq = proj_ref.shape[1]
    home = seq // groups
    group = lax.axis_index("head")
    width = 3 * HEAD_DIM
    key_count = chunk if split else seq

    def part(head, start):
        at = head * width
        rows = pl.ds(start, chunk)
        keys = pl.ds(start if split else 0, key_count)
        queries = proj_ref[0, rows, at : at + HEAD_DIM]
        key_rows = proj_ref[0, keys, at + HEAD_DIM : at + 2 * HEAD_DIM]
        value_rows = proj_ref[0, keys, at + 2 * HEAD_DIM : at + 3 * HEAD_DIM]
        scores = nt(key_rows, queries)
        peak = jnp.max(scores, axis=0, keepdims=True)
        weights = jnp.exp2((scores - peak) * (KEY_SCALE * LOG2E))
        total = jnp.sum(weights, axis=0, keepdims=True)
        mixed_t = nn(value_rows.T, weights.astype(jnp.bfloat16)) / total
        lse_ref[0, head : head + 1, rows] = peak * (KEY_SCALE * LOG2E) + jnp.log2(total)
        return mixed_t.T

    def step(index, _):
        start = pl.multiple_of(index * chunk, chunk)
        outs = [part(head, start) for head in range(heads)]
        outs = jnp.concatenate(outs, axis=1).astype(jnp.bfloat16)
        for spot in range(chunk // home):
            target = index * (chunk // home) + spot
            mixed_ref[(group - target + groups) % groups, 0] = outs[spot * home : (spot + 1) * home]
        return 0

    lax.fori_loop(0, seq // chunk, step, 0, unroll=True)


def attend(projected, row, mixed, heads, chunk, groups, order):
    seq, width = projected.shape[1:]
    split = row == 0
    kernel = functools.partial(attend_kernel, heads, chunk, groups, split)
    earlier = [] if mixed is None else [mixed]
    return call(
        kernel if mixed is None else lambda p, _, *refs: kernel(p, *refs),
        [
            shape_of((groups, 2, seq // groups, heads * HEAD_DIM), jnp.bfloat16),
            shape_of((1, heads, seq), jnp.float32),
        ],
        [pl.BlockSpec((1, seq, width), lambda i: (row, 0, 0))] + [pl.BlockSpec(memory_space=pl.ANY)] * len(earlier),
        [
            pl.BlockSpec((groups, 1, seq // groups, heads * HEAD_DIM), lambda i: (0, row, 0, 0)),
            pl.BlockSpec((1, heads, seq), lambda i: (0, 0, 0)),
        ],
        grid=(1,),
        name="attend_split" if split else "attend_whole",
        micros=6 if split else 16,
        order=order,
        aliases={} if mixed is None else {1: 0},
    )(projected, *earlier)


def attend_back_kernel(heads, chunk, groups, split, proj_ref, lse_ref, pieces_ref, out_ref, dk_ref, dv_ref, grad_ref):
    seq = proj_ref.shape[1]
    home = seq // groups
    group = lax.axis_index("head")
    width = 3 * HEAD_DIM
    key_count = chunk if split else seq
    for spot in range(groups):
        grad_ref[spot * home : (spot + 1) * home, :] = pieces_ref[(group - spot + groups) % groups, 0]

    def part(head, start, key_turned=None):
        at = head * width
        rows = pl.ds(start, chunk)
        keys = pl.ds(start if split else 0, key_count)
        queries = proj_ref[0, rows, at : at + HEAD_DIM]
        key_rows = proj_ref[0, keys, at + HEAD_DIM : at + 2 * HEAD_DIM]
        value_rows = proj_ref[0, keys, at + 2 * HEAD_DIM : at + 3 * HEAD_DIM]
        key_turned = key_rows.T if key_turned is None else key_turned
        grads = grad_ref[rows, head * HEAD_DIM : (head + 1) * HEAD_DIM]
        scores = nt(key_rows, queries)
        probs = jnp.exp2(scores * (KEY_SCALE * LOG2E) - lse_ref[0, head : head + 1, rows])
        grad_probs = nt(value_rows, grads)
        inner = jnp.sum(probs * grad_probs, axis=0, keepdims=True)
        grad_raw = (probs * (grad_probs - inner) * KEY_SCALE).astype(jnp.bfloat16)
        grad_values = nn(probs.astype(jnp.bfloat16), grads)
        grad_keys = nn(grad_raw, queries)
        grad_queries = nn(key_turned, grad_raw).T
        return grad_queries, grad_keys, grad_values

    if not split:
        for head in range(heads):
            at = head * width
            dk_ref[...] = jnp.zeros_like(dk_ref)
            dv_ref[...] = jnp.zeros_like(dv_ref)
            key_turned = proj_ref[0, :, at + HEAD_DIM : at + 2 * HEAD_DIM].T

            def step(index, _, head=head, at=at, key_turned=key_turned):
                start = pl.multiple_of(index * chunk, chunk)
                dq, dk, dv = part(head, start, key_turned)
                out_ref[0, pl.ds(start, chunk), at : at + HEAD_DIM] = dq.astype(jnp.bfloat16)
                dk_ref[...] += dk
                dv_ref[...] += dv
                return 0

            lax.fori_loop(0, seq // chunk, step, 0, unroll=True)
            both = jnp.concatenate([dk_ref[...], dv_ref[...]], axis=1).astype(jnp.bfloat16)
            out_ref[0, :, at + HEAD_DIM : at + 3 * HEAD_DIM] = both
    else:

        def step(index, _):
            start = pl.multiple_of(index * chunk, chunk)
            outs = [t for head in range(heads) for t in part(head, start)]
            out_ref[0, pl.ds(start, chunk), :] = jnp.concatenate(outs, axis=1).astype(jnp.bfloat16)
            return 0

        lax.fori_loop(0, seq // chunk, step, 0, unroll=True)


def attend_back(projected, row, lse, grads, heads, chunk, groups, order):
    seq, width = projected.shape[1:]
    split = row == 0

    return call(
        functools.partial(attend_back_kernel, heads, chunk, groups, split),
        shape_of((1, seq, width), jnp.bfloat16),
        [
            pl.BlockSpec((1, seq, width), lambda i: (row, 0, 0)),
            pl.BlockSpec((1, heads, seq), lambda i: (0, 0, 0)),
            pl.BlockSpec((groups, 1, seq // groups, heads * HEAD_DIM), lambda i: (0, row, 0, 0)),
        ],
        pl.BlockSpec((1, seq, width), lambda i: (0, 0, 0)),
        grid=(1,),
        scratch=[pltpu.VMEM((seq, HEAD_DIM), jnp.float32)] * 2
        + [pltpu.VMEM((seq, heads * HEAD_DIM), jnp.bfloat16)],
        name="attend_back_split" if split else "attend_back_whole",
        micros=8 if split else 24,
        order=order,
    )(projected, lse, grads)


norm_eps = 1e-06
gelu_coeff = 0.7978845608028654
VMEM_BYTES = 58 * 1024 * 1024
UNIT_TILE = 384


def tn(left_side, right_side):
    return lax.dot_general(
        left_side, right_side, (((0,), (0,)), ((), ())), preferred_element_type=jnp.float32
    )


def row_norm(values):
    center = jnp.mean(values, axis=-1, keepdims=True)
    shifted = values - center
    spread = jnp.mean(shifted * shifted, axis=-1, keepdims=True)
    inverse = lax.rsqrt(spread + norm_eps)
    return (shifted * inverse, inverse)


def norm_back(normed, inverse, grad_normed):
    first_mean = jnp.mean(grad_normed, axis=-1, keepdims=True)
    second_mean = jnp.mean(grad_normed * normed, axis=-1, keepdims=True)
    return inverse * (grad_normed - first_mean - normed * second_mean)


def silu_act(values):
    return values / (1.0 + jnp.exp(-values))


def weight_of(micros):
    return pl.CostEstimate(flops=int(micros * 2.2e10), bytes_accessed=int(micros * 6.6e7), transcendentals=0)


def call(kernel, out_shape, in_specs, out_specs, grid=(), prefetch=0, scratch=(), name=None, micros=1, order=(), aliases={}):
    first = prefetch + len(in_specs)

    def ordered(*refs):
        kernel(*refs[:first], *refs[first + len(order) :])

    run = pl.pallas_call(
        ordered if order else kernel,
        grid_spec=pltpu.PrefetchScalarGridSpec(
            num_scalar_prefetch=prefetch,
            grid=grid,
            in_specs=list(in_specs) + [pl.BlockSpec(memory_space=pl.ANY)] * len(order),
            out_specs=out_specs,
            scratch_shapes=scratch,
        ),
        out_shape=out_shape,
        input_output_aliases=aliases,
        compiler_params=pltpu.CompilerParams(vmem_limit_bytes=VMEM_BYTES),
        cost_estimate=weight_of(micros),
        name=name,
    )
    return lambda *arrays: run(*arrays, *order)


def hold(values, *order, micros=0):
    run = pl.pallas_call(
        lambda *refs: None,
        in_specs=[pl.BlockSpec(memory_space=pl.ANY)] * (1 + len(order)),
        out_specs=pl.BlockSpec(memory_space=pl.ANY),
        out_shape=shape_of(values.shape, values.dtype),
        input_output_aliases={0: 0},
        cost_estimate=weight_of(micros),
        name="hold",
    )
    return run(values, *order)


def whole(shape):
    return pl.BlockSpec(shape, lambda *_: (0,) * len(shape))


SCALARS = pl.BlockSpec(memory_space=pltpu.SMEM)
shape_of = jax.ShapeDtypeStruct


class Links:
    def __init__(self, heads, batches):
        self.heads = heads
        self.batches = batches
        bits = batches.bit_length() - 1
        self.levels = bits - 1
        first = list(range(bits - 1, 0, -1))
        self.orders = (first, first[1:] + first[:1])

    def fetch(self, values, distance):
        count = self.heads
        return lax.ppermute(values, "head", [((i + distance) % count, i) for i in range(count)])

    def send(self, values, distance):
        count = self.heads
        return lax.ppermute(values, "head", [(i, (i + distance) % count) for i in range(count)])

    def head_swap(self, values, bit):
        return lax.ppermute(values, "head", [(i, i ^ (1 << bit)) for i in range(self.heads)])

    def head_cube(self, values, orders):
        for bit in range(self.heads.bit_length() - 1):
            more = self.head_swap(values, bit)
            if bit < len(orders):
                more = hold(more, orders[bit])
            values = jnp.concatenate([values, more], axis=0)
        return values

    def head_gather(self, values):
        return [values] + [self.fetch(values, distance) for distance in range(1, self.heads)]

    def by_head(self, pieces):
        values = pieces[0]
        rows = values.shape[0]
        held = jnp.zeros((self.heads * rows,) + values.shape[1:], values.dtype)
        for distance in range(self.heads):
            held = lax.dynamic_update_slice_in_dim(held, pieces[distance], self.at_head(distance) * rows, 0)
        return held

    def core_swap(self, values):
        return lax.ppermute(values, "batch", [(i, i ^ 1) for i in range(self.batches)])

    def link_swap(self, values, level):
        pairs = [(i, i ^ (1 << self.orders[i & 1][level])) for i in range(self.batches)]
        return lax.ppermute(values, "batch", pairs)

    def owner(self, spot):
        batch = lax.axis_index("batch")
        half = spot >> self.levels
        masks = [
            sum(1 << order[level] for level in range(self.levels) if spot >> level & 1)
            for order in self.orders
        ]
        mask = jnp.where(batch % 2 == half, masks[0], masks[1])
        return (batch ^ half) ^ mask

    def place(self, index):
        batch = lax.axis_index("batch")
        way = batch ^ index
        half = way & 1
        spots = [
            sum(((way >> order[level]) & 1) << level for level in range(self.levels))
            for order in self.orders
        ]
        return (half << self.levels) + jnp.where((batch & 1) == half, spots[0], spots[1])

    def gather_levels(self, values, order=()):
        pieces = [values]
        for level in range(self.levels):
            joined = pieces[0] if level == 0 else jnp.concatenate(pieces, axis=0)
            more = self.link_swap(joined, level)
            if level == 0 and order:
                more = hold(more, *order)
            pieces = [joined, more]
        return pieces

    def gather_batch(self, values):
        own = jnp.concatenate(self.gather_levels(values), axis=0)
        return jnp.concatenate([own, self.core_swap(own)], axis=0)

    def reduce_cores(self, pieces, *order):
        sums = []
        for mine, other in zip(pieces[:2], pieces[2:]):
            more = self.core_swap(other)
            if order:
                more = hold(more, *order)
            sums.append((mine.astype(jnp.float32) + more.astype(jnp.float32)).astype(jnp.bfloat16))
        return sums

    def reduce_first(self, kept, *order):
        more = self.link_swap(kept[1], self.levels - 1)
        if order:
            more = hold(more, *order)
        return (kept[0].astype(jnp.float32) + more.astype(jnp.float32)).astype(jnp.bfloat16)

    def reduce_rest(self, total, *order):
        for level in reversed(range(self.levels - 1)):
            half = total.shape[0] // 2
            more = self.link_swap(total[half:], level)
            if order:
                more = hold(more, *order)
                order = ()
            total = (total[:half].astype(jnp.float32) + more.astype(jnp.float32)).astype(jnp.bfloat16)
        return total

    def by_owner(self, values):
        return jnp.concatenate(
            [lax.dynamic_index_in_dim(values, self.owner(i), 0) for i in range(self.batches)]
        )

    def by_index(self, values):
        return jnp.concatenate(
            [lax.dynamic_index_in_dim(values, self.place(i), 0) for i in range(self.batches)]
        )

    def at_head(self, distance):
        return (lax.axis_index("head") + distance) % self.heads


def mod_kernel(quarter, units_here, seg_ref, item_ref, cond_ref, ada_ref, bias_ref, in_bias_ref, table_ref, info_ref):
    starts = [[seg_ref[row * SEQ + spot * quarter] for spot in range(4)] for row in range(2)]
    first_splits = starts[0][0] != starts[0][3]
    ids = [jnp.where(first_splits, starts[1][0], starts[0][0])] + [
        jnp.where(first_splits, starts[0][spot], starts[1][spot]) for spot in range(4)
    ]
    classes = [item_ref[one] for one in ids]
    info_ref[0] = jnp.where(first_splits, 0, 1)
    info_ref[1] = lax.axis_index("head")
    info_ref[2] = 0
    for spot in range(5):
        info_ref[3 + spot] = classes[spot]
    cond_low = silu_act(cond_ref[...].astype(jnp.float32)).astype(jnp.bfloat16)
    count = cond_low.shape[0]
    row_spot = lax.broadcasted_iota(jnp.int32, (8, count), 0)
    wanted = jnp.full((8, count), count, jnp.int32)
    for spot in range(5):
        wanted = jnp.where(row_spot == spot, classes[spot], wanted)
    hits = (lax.broadcasted_iota(jnp.int32, (8, count), 1) == wanted).astype(jnp.float32)
    rows = nn(hits.astype(jnp.bfloat16), cond_low).astype(jnp.bfloat16)
    table_ref[...] = nt(rows, ada_ref[...]) + bias_ref[...]
    table_ref[5:6, :units_here] = in_bias_ref[...]


def project_kernel(heads, quarter, info_ref, table_rel_ref, tokens_ref, weight_ref, bias_ref, attn_in_ref, projected_ref, table_ref):
    block = pl.program_id(0)
    width = tokens_ref.shape[1]
    columns = table_rel_ref.shape[2]

    @pl.when(block == 0)
    def _():
        for head in range(heads):
            spot = (head - lax.axis_index("head") + heads) % heads
            table_ref[:, head * columns : (head + 1) * columns] = table_rel_ref[spot]

    quarter_rows = tokens_ref.shape[0] // 2
    for half in range(2):
        here = slice(half * quarter_rows, (half + 1) * quarter_rows)
        spot = 2 * block + half
        row = jnp.where(spot < 4, 1 + spot % 4, 0)
        normed, _ = row_norm(tokens_ref[here, :].astype(jnp.float32))
        shift = table_ref[pl.ds(row, 1), :width]
        scale = table_ref[pl.ds(row, 1), width : 2 * width]
        attn_in = (normed * (1.0 + scale) + shift).astype(jnp.bfloat16)
        attn_in_ref[here, :] = attn_in
        projected_ref[here, :] = (nt(attn_in, weight_ref[...]) + bias_ref[...]).astype(jnp.bfloat16)


def home_row(info_ref, row, home, quarter):
    return jnp.where(row == 0, 1 + info_ref[1] * home // quarter, 0)


def enter_kernel(link, quarter, info_ref, table_ref, mixed_ref, proj_ref, tokens_ref, grad_ref, bias_ref,
                 attn_ref, stream_ref, mlp_in_ref, grad_mlp_ref, mixed_home_ref, proj_true_ref, grad_sum_ref):
    row = pl.program_id(0)
    heads = link.heads
    home, width = tokens_ref.shape[1:]
    share = width // heads
    slice_rows = proj_ref.shape[2]
    head = lax.axis_index("head")

    @pl.when(row == 0)
    def _():
        grad_sum_ref[...] = jnp.zeros_like(grad_sum_ref)
        for index in range(link.batches):
            first = index * slice_rows
            count = min(slice_rows, share - first)
            if count > 0:
                place = link.place(index)
                for spot in range(heads):
                    piece = proj_ref[place, (spot - head + heads) % heads]
                    at = spot * share + first
                    proj_true_ref[at : at + count, :] = piece[:count]

    for spot in range(heads):
        piece = mixed_ref[(spot - head + heads) % heads, 0]
        mixed_home_ref[0, :, spot * share : (spot + 1) * share] = piece
    spot = home_row(info_ref, row, home, quarter)

    def mod(group):
        return table_ref[pl.ds(spot, 1), group * width : (group + 1) * width]

    attn = nn(mixed_home_ref[0], proj_true_ref[...]) + bias_ref[...]
    attn_ref[0] = attn
    stream = tokens_ref[0].astype(jnp.float32) + mod(2) * attn
    stream_ref[0] = stream
    normed, _ = row_norm(stream.astype(jnp.bfloat16).astype(jnp.float32))
    mlp_in_ref[0] = (normed * (1.0 + mod(4)) + mod(3)).astype(jnp.bfloat16)
    grad_mlp = (grad_ref[0].astype(jnp.float32) * mod(5)).astype(jnp.bfloat16)
    grad_mlp_ref[0] = grad_mlp
    grad_sum_ref[...] += jnp.sum(grad_mlp.astype(jnp.float32), axis=0, keepdims=True)


def expand_kernel(steps, mlp_in_ref, bias_ref, *refs):
    pieces, (hidden_ref, slope_ref) = refs[:-2], refs[-2:]
    step = pl.program_id(0)
    for spot, piece_ref in enumerate(pieces):

        @pl.when(step // steps == spot)
        def _(piece_ref=piece_ref):
            pre = nt(mlp_in_ref[...], piece_ref[...]) + bias_ref[...]
            square = pre * pre
            bent = jnp.tanh(gelu_coeff * (pre + 0.044715 * square * pre))
            half = 0.5 * (1.0 + bent)
            hidden_ref[...] = (pre * half).astype(jnp.bfloat16)
            inner = gelu_coeff * (1.0 + (3.0 * 0.044715) * square)
            slope_ref[...] = (half + 0.5 * pre * (1.0 - bent * bent) * inner).astype(jnp.bfloat16)


def contract_kernel(link, quarter, info_ref, table_ref, grad_mlp_ref, out_bias_ref, hidden_ref, slope_ref,
                    tokens_grad_ref, stream_ref, attn_ref, proj_ref, *refs):
    count = 4
    ins, outs = refs[:count], refs[count : 2 * count]
    (grad_pre_ref, pre_sum_ref, block_ref, stream_grad_ref, grad_attn_ref, grad_mixed_ref, sums_ref, attn_sum_ref,
     mlp_acc, grad_acc, in_buf, out_buf, hidden_buf, slope_buf, pre_buf, tokens_buf, stream_buf, attn_buf, proj_buf,
     piece_sems, pre_sems, late_sems) = refs[2 * count :]
    heads = link.heads
    rows, home, width = stream_ref.shape
    share = width // heads
    units = ins[0].shape[0]
    tile = UNIT_TILE

    def piece_copies(piece):
        slot = piece % 2
        columns = pl.ds(piece * units, units)
        pairs = (
            (outs[piece], out_buf.at[slot]),
            (slope_ref.at[:, columns], slope_buf.at[slot]),
            (hidden_ref.at[:, columns], hidden_buf.at[slot]),
            (ins[piece], in_buf.at[slot]),
        )
        return [
            pltpu.make_async_copy(source, target, piece_sems.at[kind, slot])
            for kind, (source, target) in enumerate(pairs)
        ]

    def pre_copy(piece):
        slot = piece % 2
        return pltpu.make_async_copy(
            pre_buf.at[slot], grad_pre_ref.at[:, pl.ds(piece * units, units)], pre_sems.at[slot]
        )

    start = pl.multiple_of(info_ref[1] * home, 8)
    late = [
        pltpu.make_async_copy(tokens_grad_ref.at[:, pl.ds(start, home), :], tokens_buf, late_sems.at[0]),
        pltpu.make_async_copy(stream_ref, stream_buf, late_sems.at[1]),
        pltpu.make_async_copy(attn_ref, attn_buf, late_sems.at[2]),
        pltpu.make_async_copy(proj_ref, proj_buf, late_sems.at[3]),
    ]
    for piece in range(2):
        for copy in piece_copies(piece):
            copy.start()
    for copy in late:
        copy.start()
    for piece in range(count):
        slot = piece % 2
        copies = piece_copies(piece)
        copies[0].wait()
        copies[1].wait()
        if piece >= 2:
            pre_copy(piece - 2).wait()
        for at in range(0, units, tile):
            here = slice(at, at + tile)
            grad_pre = nt(grad_mlp_ref[...], out_buf[slot, here, :]) * slope_buf[slot, :, here].astype(jnp.float32)
            grad_pre = grad_pre.astype(jnp.bfloat16)
            pre_buf[slot, :, here] = grad_pre
            total = jnp.sum(grad_pre.astype(jnp.float32), axis=0, keepdims=True)
            pre_sum_ref[:, piece * units + at : piece * units + at + tile] = total
        pre_copy(piece).start()
        copies[2].wait()
        copies[3].wait()
        for at in range(0, width, tile):
            here = slice(at, at + tile)
            mlp = nn(hidden_buf[slot], out_buf[slot, :, here])
            grad = nn(pre_buf[slot], in_buf[slot, :, here])
            mlp_acc[:, here] = mlp if piece == 0 else mlp_acc[:, here] + mlp
            grad_acc[:, here] = grad if piece == 0 else grad_acc[:, here] + grad
        if piece + 2 < count:
            for copy in piece_copies(piece + 2):
                copy.start()
    for copy in late:
        copy.wait()
    head = lax.axis_index("head")
    attn_sum = jnp.zeros((1, width), jnp.float32)
    for row in range(rows):
        spot = home_row(info_ref, row, home, quarter)

        def mod(group):
            return table_ref[pl.ds(spot, 1), group * width : (group + 1) * width]

        here = slice(row * home, (row + 1) * home)
        grad_out = tokens_buf[row_at(row, info_ref)].astype(jnp.float32)
        stream = stream_buf[row]
        mlp = mlp_acc[here, :] + out_bias_ref[...]
        block = (stream + mod(5) * mlp).astype(jnp.bfloat16)
        for other in range(heads):
            block_ref[(other - head + heads) % heads, row] = block[:, other * share : (other + 1) * share]
        normed, inverse = row_norm(stream.astype(jnp.bfloat16).astype(jnp.float32))
        grad_in = grad_acc[here, :]
        sums_ref[row, 1:2] = jnp.sum(grad_in, axis=0, keepdims=True)
        sums_ref[row, 2:3] = jnp.sum(grad_in * normed, axis=0, keepdims=True)
        sums_ref[row, 3:4] = jnp.sum(grad_out * mlp, axis=0, keepdims=True)
        stream_grad = grad_out + norm_back(normed, inverse, grad_in * (1.0 + mod(4)))
        stream_grad_ref[row] = stream_grad
        rounded = stream_grad.astype(jnp.bfloat16).astype(jnp.float32)
        sums_ref[row, 0:1] = jnp.sum(rounded * attn_buf[row], axis=0, keepdims=True)
        grad_attn = (rounded * mod(2)).astype(jnp.bfloat16)
        grad_attn_ref[row] = grad_attn
        attn_sum += jnp.sum(grad_attn.astype(jnp.float32), axis=0, keepdims=True)
        grad_mixed = nt(grad_attn, proj_buf[...]).astype(jnp.bfloat16)
        for other in range(heads):
            grad_mixed_ref[(other - head + heads) % heads, row] = grad_mixed[:, other * share : (other + 1) * share]
    attn_sum_ref[...] = attn_sum
    for piece in range(count - 2, count):
        pre_copy(piece).wait()


def row_at(spot, info_ref):
    return jnp.where(spot == 0, info_ref[0], 1 - info_ref[0])


def leave_kernel(link, quarter, at_row, info_ref, table_ref, grad_ref, weight_ref, tokens_ref, stream_grad_ref,
                 shares_ref, sums_ref, term_ref):
    block = pl.program_id(0)
    heads = link.heads
    width = tokens_ref.shape[1]
    share = width // heads
    home = stream_grad_ref.shape[1]
    start = info_ref[1] * home
    for half in range(2):
        here = slice(half * quarter, (half + 1) * quarter)
        spot = 2 * block + half
        row = 1 + spot if at_row == 0 else 0
        scale = table_ref[pl.ds(row, 1), width : 2 * width]
        grad_in = nn(grad_ref[here, :], weight_ref[...])
        normed, inverse = row_norm(tokens_ref[here, :].astype(jnp.float32))
        sums_ref[half, 0:1] = jnp.sum(grad_in, axis=0, keepdims=True)
        sums_ref[half, 1:2] = jnp.sum(grad_in * normed, axis=0, keepdims=True)
        term_ref[here, :] = norm_back(normed, inverse, grad_in * (1.0 + scale))

    @pl.when(start // (2 * quarter) == block)
    def _():
        rows = pl.ds(pl.multiple_of(start % (2 * quarter), 8), home)
        term_ref[rows, :] += stream_grad_ref[0]

    turned = term_ref[...].T
    for head in range(heads):
        shares_ref[head] = turned[head * share : (head + 1) * share, :].astype(jnp.bfloat16)


def unit_grads_kernel(steps, left_ref, right_ref, *outs):
    for spot in range(4):

        @pl.when(pl.program_id(0) // steps == spot)
        def _(spot=spot):
            outs[spot][...] = tn(left_ref[...], right_ref[...]).astype(jnp.bfloat16)


def unit_grads(left, right, order=()):
    count, total = left.shape
    width = right.shape[1]
    piece = total // 4
    steps = piece // UNIT_TILE

    def spec(spot):
        return pl.BlockSpec((UNIT_TILE, width), lambda i: (jnp.clip(i - spot * steps, 0, steps - 1), 0))

    return call(
        functools.partial(unit_grads_kernel, steps),
        [shape_of((piece, width), jnp.bfloat16)] * 4,
        [pl.BlockSpec((count, UNIT_TILE), lambda i: (0, i)), whole((count, width))],
        [spec(i) for i in range(4)],
        grid=(4 * steps,),
        name="unit_grads", micros=14,
        order=order,
    )(left, right)


def place_rows_kernel(link, slices_ref, out_ref):
    rows = slices_ref.shape[1]
    for index in range(link.batches):
        count = min(rows, out_ref.shape[0] - index * rows)
        if count > 0:
            piece = slices_ref[link.place(index)].astype(jnp.float32)
            out_ref[index * rows : index * rows + count, :] = piece[:count]


def place_rows(link, slices, rows):
    width = slices.shape[2]
    tile = 384
    return call(
        functools.partial(place_rows_kernel, link),
        shape_of((rows, width), jnp.float32),
        [pl.BlockSpec(slices.shape[:2] + (tile,), lambda i: (0, 0, i))],
        pl.BlockSpec((rows, tile), lambda i: (0, i)),
        grid=(width // tile,),
        name="place_rows", micros=0,
    )(slices)


def place_columns_kernel(link, slices_ref, out_ref, rows_ref):
    rows = slices_ref.shape[1]
    for index in range(link.batches):
        rows_ref[index * rows : (index + 1) * rows, :] = slices_ref[link.place(index)].astype(jnp.float32)
    out_ref[...] = rows_ref[...].T


def place_columns(link, slices):
    batches, rows, width = slices.shape
    tile = 128
    return call(
        functools.partial(place_columns_kernel, link),
        shape_of((width, batches * rows), jnp.float32),
        [pl.BlockSpec((batches, rows, tile), lambda i: (0, 0, i))],
        pl.BlockSpec((tile, batches * rows), lambda i: (i, 0)),
        grid=(width // tile,),
        scratch=[pltpu.VMEM((batches * rows, tile), jnp.float32)],
        name="place_columns", micros=0,
    )(slices)


def lay_home_kernel(heads, info_ref, blocks_ref, out_ref):
    home = blocks_ref.shape[2]
    head = lax.axis_index("head")
    for spot in range(heads):
        for row in range(2):
            out_ref[row_at(row, info_ref), spot * home : (spot + 1) * home, :] = blocks_ref[(head - spot + heads) % heads, row]


def shards(
    tokens,
    segments,
    item_cond,
    condition,
    ada_weight,
    ada_bias,
    qkv_weight,
    qv_bias,
    proj_weight,
    proj_bias,
    in_weight,
    in_bias,
    out_weight,
    out_bias,
    cotangent,
):
    low = jnp.bfloat16
    full = jnp.float32
    heads, batches = lax.axis_size("head"), lax.axis_size("batch")
    link = Links(heads, batches)
    batch = lax.axis_index("batch")
    token_count, width = tokens.shape
    rows = token_count // SEQ
    quarter = SEQ // 4
    home = SEQ // heads
    home_count = rows * home
    share = width // heads
    heads_here = qv_bias.shape[0] // (2 * HEAD_DIM)
    qkv_here = 3 * heads_here * HEAD_DIM
    units_here = in_weight.shape[1]
    units = units_here // batches
    ada_here = ada_weight.shape[1]
    cond_count = condition.shape[0]

    ada_t = ada_weight.T
    qkv_t = qkv_weight.T
    table_part, info = call(
        functools.partial(mod_kernel, quarter, units_here),
        [shape_of((8, ada_here), full), shape_of((8,), jnp.int32)],
        [SCALARS, SCALARS] + [whole(s) for s in ((cond_count, width), (ada_here, width), (1, ada_here), (1, units_here))],
        [whole((8, ada_here)), SCALARS],
        name="modulation", micros=5,
    )(segments, item_cond, condition, ada_t, ada_bias.astype(full)[None], in_bias.astype(full)[None])
    table_rel = jnp.stack([table_part] + [link.fetch(table_part, j) for j in range(1, heads)])

    slice_rows = -(-share // (8 * batches)) * 8
    proj_pad = jnp.pad(proj_weight, ((0, slice_rows * batches - share), (0, 0)))
    in_slice = lax.dynamic_slice_in_dim(in_weight, batch * units, units, 1).T
    out_slice = lax.dynamic_slice_in_dim(out_weight, batch * units, units, 0)
    in_gathered = lax.all_gather(in_slice, "head", axis=0, tiled=True)
    out_gathered = lax.all_gather(out_slice, "head", axis=0, tiled=True)
    def tokens_block(i, info_ref):
        return (2 * row_at(i // 2, info_ref) + i % 2, 0)

    bias_pairs = qv_bias.astype(full).reshape(heads_here, 2, HEAD_DIM)
    full_bias = jnp.concatenate(
        [bias_pairs[:, :1], jnp.zeros((heads_here, 1, HEAD_DIM), full), bias_pairs[:, 1:]], axis=1
    ).reshape(1, -1)
    attn_in, projected, table = call(
        functools.partial(project_kernel, heads, quarter),
        [
            shape_of((token_count, width), low),
            shape_of((token_count, qkv_here), low),
            shape_of((8, 6 * width), full),
        ],
        [
            whole((heads, 8, ada_here)),
            pl.BlockSpec((2 * quarter, width), tokens_block),
            whole((qkv_here, width)),
            whole((1, qkv_here)),
        ],
        [
            pl.BlockSpec((2 * quarter, width), lambda i, _: (i, 0)),
            pl.BlockSpec((2 * quarter, qkv_here), lambda i, _: (i, 0)),
            whole((8, 6 * width)),
        ],
        grid=(2 * rows,),
        prefetch=1,
        name="project", micros=13,
    )(info, table_rel, tokens, qkv_t, full_bias)
    projected = projected.reshape(rows, SEQ, qkv_here)
    proj_slice = hold(lax.dynamic_slice_in_dim(proj_pad, batch * slice_rows, slice_rows, 0), table_rel)
    proj_rel = jnp.stack(
        [proj_slice] + [hold(link.fetch(proj_slice, j), projected) for j in range(1, heads)]
    )[None]
    mixed = None
    log_totals = []
    for row in range(rows):
        order = [in_gathered] if row == 1 else []
        mixed, log_total = attend(projected, row, mixed, heads_here, quarter, heads, order)
        log_totals.append(log_total)
        if row < link.levels:
            proj_rel = jnp.concatenate([proj_rel, hold(link.link_swap(proj_rel, row), log_total)], axis=0)
        if row == 0:
            in_gathered = hold(in_gathered, log_total)
    in_held = link.gather_levels(in_gathered, [log_totals[1]])
    for level in range(rows, link.levels):
        proj_rel = jnp.concatenate([proj_rel, link.link_swap(proj_rel, level)], axis=0)
    proj_all = jnp.concatenate([proj_rel, link.core_swap(proj_rel)], axis=0)
    out_gathered = hold(out_gathered, in_held[0])
    mixed = hold(mixed, out_gathered, proj_all, micros=20)
    mixed_all = jnp.stack([mixed[0]] + [link.fetch(mixed[j], j) for j in range(1, heads)])

    out_held = link.gather_levels(out_gathered)
    out_pieces = out_held + [link.core_swap(piece) for piece in out_held]
    tokens_rows = tokens.reshape(rows, SEQ, width)
    grad_rows = cotangent.reshape(rows, SEQ, width)
    home_spec = pl.BlockSpec((1, home, width), lambda i, info_ref: (row_at(i, info_ref), info_ref[1], 0))
    row_spec = pl.BlockSpec((1, home, width), lambda i, _: (i, 0, 0))
    attn, stream, mlp_in, grad_mlp, mixed_home, proj_true, grad_sum = call(
        functools.partial(enter_kernel, link, quarter),
        [
            shape_of((rows, home, width), full),
            shape_of((rows, home, width), full),
            shape_of((rows, home, width), low),
            shape_of((rows, home, width), low),
            shape_of((rows, home, width), low),
            shape_of((width, width), low),
            shape_of((1, width), full),
        ],
        [
            whole((8, 6 * width)),
            pl.BlockSpec((heads, 1, home, share), lambda i, _: (0, i, 0, 0)),
            whole(proj_all.shape),
            home_spec,
            home_spec,
            whole((1, width)),
        ],
        [row_spec] * 5 + [whole((width, width)), whole((1, width))],
        grid=(rows,),
        prefetch=1,
        name="enter", micros=9,
        order=[out_held[0]],
    )(info, table, mixed_all, proj_all, tokens_rows, grad_rows, proj_bias.astype(full)[None])

    in_held[1] = hold(in_held[1], mlp_in)
    in_pieces = in_held + [link.core_swap(piece) for piece in in_held]
    mlp_in = mlp_in.reshape(home_count, width)
    grad_mlp = grad_mlp.reshape(home_count, width)
    in_bias_all = table[5].reshape(heads, -1)[:, :units_here]
    in_bias_all = in_bias_all.reshape(heads, batches, units)
    in_bias_all = link.by_owner(in_bias_all.transpose(1, 0, 2)).reshape(1, -1)
    piece_rows = in_pieces[0].shape[0]
    unit_count = 4 * piece_rows
    steps = piece_rows // UNIT_TILE

    def piece_spec(spot):
        return pl.BlockSpec((UNIT_TILE, width), lambda i, *_: (jnp.clip(i - spot * steps, 0, steps - 1), 0))

    tile_spec = pl.BlockSpec((home_count, UNIT_TILE), lambda i, *_: (0, i))
    bias_spec = pl.BlockSpec((1, UNIT_TILE), lambda i, *_: (0, i))
    hidden, slope = call(
        functools.partial(expand_kernel, 1),
        [shape_of((home_count, unit_count), low)] * 2,
        [whole((home_count, width)), pl.BlockSpec((1, piece_rows), lambda i: (0, i))]
        + [whole((piece_rows, width))] * 4,
        [pl.BlockSpec((home_count, piece_rows), lambda i: (0, i))] * 2,
        grid=(4,),
        name="expand", micros=20,
        order=[out_held[0]],
    )(mlp_in, in_bias_all, *in_pieces)

    out_parts = unit_grads(hidden, grad_mlp, order=[out_pieces[2]])

    stay = pl.BlockSpec((rows, home, width), lambda *_: (0, 0, 0))
    by_head = whole((heads, rows, home, share))
    grad_pre, pre_sum, block_home, stream_grad, grad_attn, grad_mixed, home_sums, attn_sum = call(
        functools.partial(contract_kernel, link, quarter),
        [
            shape_of((home_count, unit_count), low),
            shape_of((1, unit_count), full),
            shape_of((heads, rows, home, share), low),
            shape_of((rows, home, width), full),
            shape_of((rows, home, width), low),
            shape_of((heads, rows, home, share), low),
            shape_of((rows, 4, width), full),
            shape_of((1, width), full),
        ],
        [SCALARS, whole((8, 6 * width)), whole((home_count, width)), whole((1, width))]
        + [pl.BlockSpec(memory_space=pl.ANY)] * 14,
        [
            pl.BlockSpec(memory_space=pl.ANY),
            whole((1, unit_count)),
            by_head,
            stay,
            stay,
            by_head,
            whole((rows, 4, width)),
            whole((1, width)),
        ],
        scratch=[
            pltpu.VMEM((home_count, width), full),
            pltpu.VMEM((home_count, width), full),
            pltpu.VMEM((2, piece_rows, width), low),
            pltpu.VMEM((2, piece_rows, width), low),
            pltpu.VMEM((2, home_count, piece_rows), low),
            pltpu.VMEM((2, home_count, piece_rows), low),
            pltpu.VMEM((2, home_count, piece_rows), low),
            pltpu.VMEM((rows, home, width), low),
            pltpu.VMEM((rows, home, width), full),
            pltpu.VMEM((rows, home, width), full),
            pltpu.VMEM((width, width), low),
            pltpu.SemaphoreType.DMA((4, 2)),
            pltpu.SemaphoreType.DMA((2,)),
            pltpu.SemaphoreType.DMA((4,)),
        ],
        name="contract", micros=44,
        order=[out_parts[0]],
    )(info, table, grad_mlp, out_bias.astype(full)[None], hidden, slope, grad_rows, stream, attn, proj_true,
      *in_pieces, *out_pieces)
    mixed_sends = [link.send(grad_mixed[j], j) for j in range(1, heads)]
    out_near = link.reduce_cores(out_parts, grad_pre)
    out_sum = link.reduce_first(out_near)
    in_parts = unit_grads(grad_pre, mlp_in, order=[out_near[1]])
    grad_mixed = jnp.stack([grad_mixed[0]] + [hold(piece, in_parts[0]) for piece in mixed_sends])
    out_slice = link.reduce_rest(out_sum)
    in_near = link.reduce_cores(in_parts, grad_mixed)
    proj_grad = tn(mixed_home.reshape(home_count, width), grad_attn.reshape(home_count, width)).astype(low)

    def head_sum(values):
        return lax.psum_scatter(values, "head", scatter_dimension=0, tiled=True)

    out_blocks = out_slice.reshape(heads, units, width)

    def out_block(distance):
        return lax.dynamic_index_in_dim(out_blocks, link.at_head(distance), 0, keepdims=False)

    out_more = [link.send(out_block(j), j) for j in range(1, heads)]
    grad_rows_low = []
    block_sums = []
    shares = None
    for row in range(rows):
        grad_row = attend_back(
            projected, row, log_totals[row], grad_mixed, heads_here, quarter, heads,
            [] if row == 0 else [sums_row, out_slice],
        )[0]
        order = list(in_near) + [out_sum]
        if row == 1:
            in_sum = link.reduce_first(in_near, grad_row)
            order = [in_sum]
        earlier = [] if shares is None else [shares]
        kernel = functools.partial(leave_kernel, link, quarter, row)
        shares, sums_row = call(
            kernel if row == 0 else lambda *refs: kernel(*refs[:6], *refs[7:]),
            [shape_of((heads, share, token_count), low), shape_of((4, 2, width), full)],
            [
                whole((8, 6 * width)),
                pl.BlockSpec((2 * quarter, qkv_here), lambda i, _: (i, 0)),
                whole((qkv_here, width)),
                pl.BlockSpec((2 * quarter, width), lambda i, info_ref, row=row: tokens_block(i + 2 * row, info_ref)),
                pl.BlockSpec((1, home, width), lambda i, _, row=row: (row, 0, 0)),
            ]
            + [pl.BlockSpec(memory_space=pl.ANY)] * len(earlier),
            [
                pl.BlockSpec((heads, share, 2 * quarter), lambda i, _, row=row: (0, 0, i + 2 * row)),
                pl.BlockSpec((2, 2, width), lambda i, _: (i, 0, 0)),
            ],
            grid=(2,),
            prefetch=1,
            scratch=[pltpu.VMEM((2 * quarter, width), full)],
            name="leave", micros=9,
            aliases={6: 0} if earlier else {},
            order=order,
        )(info, table, grad_row, qkv_t, tokens, stream_grad, *earlier)
        grad_rows_low.append(grad_row)
        block_sums.append(sums_row)
    in_slice = link.reduce_rest(in_sum, sums_row)
    out_slice_sum = out_block(0).astype(full)
    for more in out_more:
        out_slice_sum = out_slice_sum + hold(more, grad_rows_low[1]).astype(full)
    out_slice_sum = out_slice_sum.astype(low)
    grad_projected = hold(jnp.concatenate(grad_rows_low, axis=0), in_slice)

    in_slice_sum = head_sum(in_slice)
    shares = head_sum(hold(shares, in_slice_sum))[0]
    tokens_grad = jnp.where(
        info[0] == 0, shares, jnp.concatenate([shares[:, SEQ:], shares[:, :SEQ]], axis=1)
    ).T

    block_home = hold(block_home, grad_mixed)
    block_home = jnp.stack(
        [block_home[0]] + [hold(link.send(block_home[j], j), sums_row) for j in range(1, heads)]
    )
    block_out = call(
        functools.partial(lay_home_kernel, heads),
        shape_of((rows, SEQ, share), low),
        [whole((heads, rows, home, share))],
        whole((rows, SEQ, share)),
        prefetch=1,
        name="lay_home", micros=0,
        order=[sums_row],
    )(info, block_home).reshape(token_count, share)

    home_quarter = lax.axis_index("head") * home // quarter
    seg_spots = lax.broadcasted_iota(jnp.int32, (5, 1), 0)

    def seg_home(sums):
        placed = jnp.where(seg_spots == 1 + home_quarter, sums[0][None, :], 0.0)
        return jnp.where(seg_spots == 0, sums[1][None, :], placed)

    seg_blocks = jnp.concatenate([jnp.sum(block_sums[1], axis=0, keepdims=True), block_sums[0]], axis=0)
    seg_grads = jnp.concatenate(
        [seg_blocks[:, 0], seg_blocks[:, 1]] + [seg_home(home_sums[:, i]) for i in range(4)], axis=1
    )
    in_bias_part = link.by_index(pre_sum.reshape(batches, heads, units)).transpose(1, 0, 2)
    bias_grads = jnp.concatenate(
        [
            in_bias_part.reshape(heads, -1),
            grad_sum.reshape(heads, -1),
            attn_sum.reshape(heads, -1),
        ],
        axis=1,
    ).reshape(1, -1)
    sent = jnp.concatenate([seg_grads, bias_grads, jnp.zeros((2, 6 * width), full)], axis=0)
    sent = hold(sent, in_slice).reshape(8, heads, ada_here)

    def sent_block(distance):
        return lax.dynamic_index_in_dim(sent, link.at_head(distance), 1, keepdims=False)

    held = sent_block(0)
    for j in range(1, heads):
        held = held + link.send(sent_block(j), j)
    column_sums = jnp.sum(grad_projected.astype(full), axis=0).reshape(heads_here, 3, HEAD_DIM)
    qv_bias_part = jnp.concatenate([column_sums[:, :1], column_sums[:, 2:]], axis=1).reshape(-1)
    held = jnp.concatenate(
        [
            held[:6],
            jnp.pad(qv_bias_part, (0, ada_here - qv_bias_part.shape[0]))[None],
            jnp.pad(info[3:].astype(full), (0, ada_here - 5))[None],
        ],
        axis=0,
    )
    all_held = hold(link.gather_batch(held[None]), in_slice_sum)
    all_classes = (all_held[:, 7, :5] + 0.5).astype(jnp.int32).reshape(-1)
    class_hits = (
        lax.broadcasted_iota(jnp.int32, (cond_count, 1), 0) == all_classes[None, :]
    ).astype(full)
    mod_low = jnp.dot(
        class_hits,
        all_held[:, :5].reshape(-1, ada_here),
        precision=lax.Precision.HIGHEST,
        preferred_element_type=full,
    ).astype(low)
    bias_total = jnp.sum(all_held[:, 5], axis=0)
    qv_bias_grad = jnp.sum(all_held[:, 6, : qv_bias.shape[0]], axis=0)
    in_bias_grad = bias_total[:units_here]
    cond_f = condition.astype(full)
    ada_weight_grad = tn(mod_low, silu_act(cond_f).astype(low)).T
    ada_bias_grad = jnp.sum(mod_low.astype(full), axis=0)
    cond_part = nn(mod_low, ada_t)
    shared = jnp.pad(bias_total[units_here:], (0, width - 2 * share))
    last = jnp.concatenate([cond_part, shared[None], jnp.zeros((7, width), full)]).astype(low)
    last = jnp.stack([last] + [link.fetch(last, j) for j in range(1, heads)]).astype(full)
    cond_total = jnp.sum(last[:, :cond_count], axis=0)
    condition_grad = jax.vjp(silu_act, cond_f)[1](cond_total)[0]
    shared = last[:, cond_count]
    head = lax.axis_index("head")
    shared = jnp.concatenate(
        [lax.dynamic_index_in_dim(shared, (j - head + heads) % heads, 0) for j in range(heads)]
    )
    out_bias_grad = shared[:, :share].reshape(-1)
    proj_bias_grad = shared[:, share : 2 * share].reshape(-1)

    out_weight_grad = place_rows(link, link.gather_batch(out_slice_sum[None]), units_here)
    in_weight_grad = place_columns(link, link.gather_batch(in_slice_sum[None]))

    qkv_rows = -(-qkv_here // (16 * batches)) * 16
    qkv_grad = tn(grad_projected, attn_in.reshape(token_count, width)).astype(low)
    qkv_grad = jnp.pad(qkv_grad, ((0, qkv_rows * batches - qkv_here), (0, 0))).reshape(batches, qkv_rows, width)
    proj_grad = jnp.pad(
        proj_grad.reshape(heads, share, width), ((0, 0), (0, slice_rows * batches - share), (0, 0))
    ).reshape(heads, batches, slice_rows, width)
    proj_grad = proj_grad.transpose(1, 0, 2, 3).reshape(batches, heads * slice_rows, width)
    both = link.by_owner(jnp.concatenate([qkv_grad, proj_grad], axis=1))
    both = both.reshape(2, 2, -1, width)
    got = [link.core_swap(piece) for piece in both[1]]
    both = [(mine.astype(full) + more.astype(full)).astype(low) for mine, more in zip(both[0], got)]
    both = link.reduce_rest(link.reduce_first(both))
    proj_blocks = both[qkv_rows:].reshape(heads, slice_rows, width)

    def proj_block(distance):
        return lax.dynamic_index_in_dim(proj_blocks, link.at_head(distance), 0, keepdims=False)

    proj_sum = proj_block(0).astype(full)
    for j in range(1, heads):
        proj_sum = proj_sum + link.send(proj_block(j), j).astype(full)
    both = jnp.concatenate([both[:qkv_rows], proj_sum.astype(low)], axis=0)
    both = link.gather_batch(both[None])
    qkv_weight_grad = place_rows(link, both[:, :qkv_rows], qkv_here).T
    proj_weight_grad = place_rows(link, both[:, qkv_rows:], share)

    return (
        block_out,
        tokens_grad,
        condition_grad,
        ada_weight_grad,
        ada_bias_grad,
        qkv_weight_grad,
        qv_bias_grad,
        proj_weight_grad,
        proj_bias_grad,
        in_weight_grad,
        in_bias_grad,
        out_weight_grad,
        out_bias_grad,
    )


def solution(mesh):
    in_specs = (
        P("batch", None),
        P("batch"),
        P(),
        P(),
        P(None, "head"),
        P("head"),
        P(None, "head"),
        P("head"),
        P("head", None),
        P(),
        P(None, "head"),
        P("head"),
        P("head", None),
        P(),
        P("batch", None),
    )
    out_specs = (
        P("batch", "head"),
        P("batch", "head"),
        P(),
        P(None, "head"),
        P("head"),
        P(None, "head"),
        P("head"),
        P("head", None),
        P(),
        P(None, "head"),
        P("head"),
        P("head", None),
        P(),
    )
    return jax.shard_map(shards, mesh=mesh, in_specs=in_specs, out_specs=out_specs, check_vma=False)
```

```python
import functools
import math

import jax
import jax.numpy as jnp
from jax import lax
from jax.experimental import pallas as pl
from jax.experimental.pallas import tpu as pltpu
from jax.sharding import PartitionSpec as P

HEAD_DIM = 72
SEQ = 1024
LOG2E = 1.4426950408889634
KEY_SCALE = 1.0 / math.sqrt(HEAD_DIM)


def nt(a, b):
    return lax.dot_general(a, b, (((1,), (1,)), ((), ())), preferred_element_type=jnp.float32)


def nn(a, b):
    return lax.dot_general(a, b, (((1,), (0,)), ((), ())), preferred_element_type=jnp.float32)


def attend_kernel(heads, chunk, groups, split, proj_ref, mixed_ref, lse_ref):
    seq = proj_ref.shape[1]
    home = seq // groups
    group = lax.axis_index("head")
    width = 3 * HEAD_DIM
    key_count = chunk if split else seq

    def part(head, start):
        at = head * width
        rows = pl.ds(start, chunk)
        keys = pl.ds(start if split else 0, key_count)
        queries = proj_ref[0, rows, at : at + HEAD_DIM]
        key_rows = proj_ref[0, keys, at + HEAD_DIM : at + 2 * HEAD_DIM]
        value_rows = proj_ref[0, keys, at + 2 * HEAD_DIM : at + 3 * HEAD_DIM]
        scores = nt(key_rows, queries)
        peak = jnp.max(scores, axis=0, keepdims=True)
        weights = jnp.exp2((scores - peak) * (KEY_SCALE * LOG2E))
        total = jnp.sum(weights, axis=0, keepdims=True)
        mixed_t = nn(value_rows.T, weights.astype(jnp.bfloat16)) / total
        lse_ref[0, head : head + 1, rows] = peak * (KEY_SCALE * LOG2E) + jnp.log2(total)
        return mixed_t

    def step(index, _):
        start = pl.multiple_of(index * chunk, chunk)
        outs = [part(head, start) for head in range(heads)]
        outs = jnp.concatenate(outs, axis=0).astype(jnp.bfloat16)
        for spot in range(chunk // home):
            target = index * (chunk // home) + spot
            mixed_ref[(group - target + groups) % groups, 0] = outs[:, spot * home : (spot + 1) * home]
        return 0

    lax.fori_loop(0, seq // chunk, step, 0, unroll=True)


def attend(projected, row, mixed, heads, chunk, groups, order):
    seq, width = projected.shape[1:]
    split = row == 0
    kernel = functools.partial(attend_kernel, heads, chunk, groups, split)
    earlier = [] if mixed is None else [mixed]
    return call(
        kernel if mixed is None else lambda p, _, *refs: kernel(p, *refs),
        [
            shape_of((groups, 2, heads * HEAD_DIM, seq // groups), jnp.bfloat16),
            shape_of((1, heads, seq), jnp.float32),
        ],
        [pl.BlockSpec((1, seq, width), lambda i: (row, 0, 0))] + [pl.BlockSpec(memory_space=pl.ANY)] * len(earlier),
        [
            pl.BlockSpec((groups, 1, heads * HEAD_DIM, seq // groups), lambda i: (0, row, 0, 0)),
            pl.BlockSpec((1, heads, seq), lambda i: (0, 0, 0)),
        ],
        grid=(1,),
        name="attend_split" if split else "attend_whole",
        micros=6 if split else 16,
        order=order,
        aliases={} if mixed is None else {1: 0},
    )(projected, *earlier)


def attend_back_kernel(heads, chunk, groups, split, proj_ref, lse_ref, pieces_ref, out_ref, dk_ref, dv_ref, grad_ref):
    seq = proj_ref.shape[1]
    home = seq // groups
    group = lax.axis_index("head")
    width = 3 * HEAD_DIM
    key_count = chunk if split else seq
    for spot in range(groups):
        piece = pieces_ref[(group - spot + groups) % groups, 0].astype(jnp.float32).T
        grad_ref[spot * home : (spot + 1) * home, :] = piece.astype(jnp.bfloat16)

    def part(head, start, key_turned=None):
        at = head * width
        rows = pl.ds(start, chunk)
        keys = pl.ds(start if split else 0, key_count)
        queries = proj_ref[0, rows, at : at + HEAD_DIM]
        key_rows = proj_ref[0, keys, at + HEAD_DIM : at + 2 * HEAD_DIM]
        value_rows = proj_ref[0, keys, at + 2 * HEAD_DIM : at + 3 * HEAD_DIM]
        key_turned = key_rows.T if key_turned is None else key_turned
        grads = grad_ref[rows, head * HEAD_DIM : (head + 1) * HEAD_DIM]
        scores = nt(key_rows, queries)
        probs = jnp.exp2(scores * (KEY_SCALE * LOG2E) - lse_ref[0, head : head + 1, rows])
        grad_probs = nt(value_rows, grads)
        inner = jnp.sum(probs * grad_probs, axis=0, keepdims=True)
        grad_raw = (probs * (grad_probs - inner) * KEY_SCALE).astype(jnp.bfloat16)
        grad_values = nn(probs.astype(jnp.bfloat16), grads)
        grad_keys = nn(grad_raw, queries)
        grad_queries = nn(key_turned, grad_raw).T
        return grad_queries, grad_keys, grad_values

    if not split:
        for head in range(heads):
            at = head * width
            dk_ref[...] = jnp.zeros_like(dk_ref)
            dv_ref[...] = jnp.zeros_like(dv_ref)
            key_turned = proj_ref[0, :, at + HEAD_DIM : at + 2 * HEAD_DIM].T

            def step(index, _, head=head, at=at, key_turned=key_turned):
                start = pl.multiple_of(index * chunk, chunk)
                dq, dk, dv = part(head, start, key_turned)
                out_ref[0, pl.ds(start, chunk), at : at + HEAD_DIM] = dq.astype(jnp.bfloat16)
                dk_ref[...] += dk
                dv_ref[...] += dv
                return 0

            lax.fori_loop(0, seq // chunk, step, 0, unroll=True)
            both = jnp.concatenate([dk_ref[...], dv_ref[...]], axis=1).astype(jnp.bfloat16)
            out_ref[0, :, at + HEAD_DIM : at + 3 * HEAD_DIM] = both
    else:

        def step(index, _):
            start = pl.multiple_of(index * chunk, chunk)
            outs = [t for head in range(heads) for t in part(head, start)]
            out_ref[0, pl.ds(start, chunk), :] = jnp.concatenate(outs, axis=1).astype(jnp.bfloat16)
            return 0

        lax.fori_loop(0, seq // chunk, step, 0, unroll=True)


def attend_back(projected, row, lse, grads, heads, chunk, groups, order):
    seq, width = projected.shape[1:]
    split = row == 0

    return call(
        functools.partial(attend_back_kernel, heads, chunk, groups, split),
        shape_of((1, seq, width), jnp.bfloat16),
        [
            pl.BlockSpec((1, seq, width), lambda i: (row, 0, 0)),
            pl.BlockSpec((1, heads, seq), lambda i: (0, 0, 0)),
            pl.BlockSpec((groups, 1, heads * HEAD_DIM, seq // groups), lambda i: (0, row, 0, 0)),
        ],
        pl.BlockSpec((1, seq, width), lambda i: (0, 0, 0)),
        grid=(1,),
        scratch=[pltpu.VMEM((seq, HEAD_DIM), jnp.float32)] * 2
        + [pltpu.VMEM((seq, heads * HEAD_DIM), jnp.bfloat16)],
        name="attend_back_split" if split else "attend_back_whole",
        micros=8 if split else 24,
        order=order,
    )(projected, lse, grads)


norm_eps = 1e-06
gelu_coeff = 0.7978845608028654
VMEM_BYTES = 58 * 1024 * 1024
UNIT_TILE = 384


def tn(left_side, right_side):
    return lax.dot_general(
        left_side, right_side, (((0,), (0,)), ((), ())), preferred_element_type=jnp.float32
    )


def row_norm(values):
    center = jnp.mean(values, axis=-1, keepdims=True)
    shifted = values - center
    spread = jnp.mean(shifted * shifted, axis=-1, keepdims=True)
    inverse = lax.rsqrt(spread + norm_eps)
    return (shifted * inverse, inverse)


def norm_back(normed, inverse, grad_normed):
    first_mean = jnp.mean(grad_normed, axis=-1, keepdims=True)
    second_mean = jnp.mean(grad_normed * normed, axis=-1, keepdims=True)
    return inverse * (grad_normed - first_mean - normed * second_mean)


def silu_act(values):
    return values / (1.0 + jnp.exp(-values))


def weight_of(micros):
    return pl.CostEstimate(flops=int(micros * 2.2e10), bytes_accessed=int(micros * 6.6e7), transcendentals=0)


def call(kernel, out_shape, in_specs, out_specs, grid=(), prefetch=0, scratch=(), name=None, micros=1, order=(), aliases={}):
    first = prefetch + len(in_specs)

    def ordered(*refs):
        kernel(*refs[:first], *refs[first + len(order) :])

    run = pl.pallas_call(
        ordered if order else kernel,
        grid_spec=pltpu.PrefetchScalarGridSpec(
            num_scalar_prefetch=prefetch,
            grid=grid,
            in_specs=list(in_specs) + [pl.BlockSpec(memory_space=pl.ANY)] * len(order),
            out_specs=out_specs,
            scratch_shapes=scratch,
        ),
        out_shape=out_shape,
        input_output_aliases=aliases,
        compiler_params=pltpu.CompilerParams(vmem_limit_bytes=VMEM_BYTES),
        cost_estimate=weight_of(micros),
        name=name,
    )
    return lambda *arrays: run(*arrays, *order)


def hold(values, *order, micros=0):
    run = pl.pallas_call(
        lambda *refs: None,
        in_specs=[pl.BlockSpec(memory_space=pl.ANY)] * (1 + len(order)),
        out_specs=pl.BlockSpec(memory_space=pl.ANY),
        out_shape=shape_of(values.shape, values.dtype),
        input_output_aliases={0: 0},
        cost_estimate=weight_of(micros),
        name="hold",
    )
    return run(values, *order)


def whole(shape):
    return pl.BlockSpec(shape, lambda *_: (0,) * len(shape))


SCALARS = pl.BlockSpec(memory_space=pltpu.SMEM)
shape_of = jax.ShapeDtypeStruct


class Links:
    def __init__(self, heads, batches):
        self.heads = heads
        self.batches = batches
        bits = batches.bit_length() - 1
        self.levels = bits - 1
        first = list(range(bits - 1, 0, -1))
        self.orders = (first, first[1:] + first[:1])

    def fetch(self, values, distance):
        count = self.heads
        return lax.ppermute(values, "head", [((i + distance) % count, i) for i in range(count)])

    def send(self, values, distance):
        count = self.heads
        return lax.ppermute(values, "head", [(i, (i + distance) % count) for i in range(count)])

    def head_swap(self, values, bit):
        return lax.ppermute(values, "head", [(i, i ^ (1 << bit)) for i in range(self.heads)])

    def head_cube(self, values, orders):
        for bit in range(self.heads.bit_length() - 1):
            more = self.head_swap(values, bit)
            if bit < len(orders):
                more = hold(more, orders[bit])
            values = jnp.concatenate([values, more], axis=0)
        return values

    def head_gather(self, values):
        return [values] + [self.fetch(values, distance) for distance in range(1, self.heads)]

    def by_head(self, pieces):
        values = pieces[0]
        rows = values.shape[0]
        held = jnp.zeros((self.heads * rows,) + values.shape[1:], values.dtype)
        for distance in range(self.heads):
            held = lax.dynamic_update_slice_in_dim(held, pieces[distance], self.at_head(distance) * rows, 0)
        return held

    def core_swap(self, values):
        return lax.ppermute(values, "batch", [(i, i ^ 1) for i in range(self.batches)])

    def link_swap(self, values, level):
        pairs = [(i, i ^ (1 << self.orders[i & 1][level])) for i in range(self.batches)]
        return lax.ppermute(values, "batch", pairs)

    def owner(self, spot):
        batch = lax.axis_index("batch")
        half = spot >> self.levels
        masks = [
            sum(1 << order[level] for level in range(self.levels) if spot >> level & 1)
            for order in self.orders
        ]
        mask = jnp.where(batch % 2 == half, masks[0], masks[1])
        return (batch ^ half) ^ mask

    def place(self, index):
        batch = lax.axis_index("batch")
        way = batch ^ index
        half = way & 1
        spots = [
            sum(((way >> order[level]) & 1) << level for level in range(self.levels))
            for order in self.orders
        ]
        return (half << self.levels) + jnp.where((batch & 1) == half, spots[0], spots[1])

    def gather_levels(self, values, order=()):
        pieces = [values]
        for level in range(self.levels):
            joined = pieces[0] if level == 0 else jnp.concatenate(pieces, axis=0)
            more = self.link_swap(joined, level)
            if level == 0 and order:
                more = hold(more, *order)
            pieces = [joined, more]
        return pieces

    def gather_batch(self, values):
        own = jnp.concatenate(self.gather_levels(values), axis=0)
        return jnp.concatenate([own, self.core_swap(own)], axis=0)

    def reduce_cores(self, pieces, *order):
        sums = []
        for mine, other in zip(pieces[:2], pieces[2:]):
            more = self.core_swap(other)
            if order:
                more = hold(more, *order)
            sums.append((mine.astype(jnp.float32) + more.astype(jnp.float32)).astype(jnp.bfloat16))
        return sums

    def reduce_first(self, kept, *order):
        more = self.link_swap(kept[1], self.levels - 1)
        if order:
            more = hold(more, *order)
        return (kept[0].astype(jnp.float32) + more.astype(jnp.float32)).astype(jnp.bfloat16)

    def reduce_rest(self, total, *order):
        for level in reversed(range(self.levels - 1)):
            half = total.shape[0] // 2
            more = self.link_swap(total[half:], level)
            if order:
                more = hold(more, *order)
                order = ()
            total = (total[:half].astype(jnp.float32) + more.astype(jnp.float32)).astype(jnp.bfloat16)
        return total

    def by_owner(self, values):
        return jnp.concatenate(
            [lax.dynamic_index_in_dim(values, self.owner(i), 0) for i in range(self.batches)]
        )

    def by_index(self, values):
        return jnp.concatenate(
            [lax.dynamic_index_in_dim(values, self.place(i), 0) for i in range(self.batches)]
        )

    def at_head(self, distance):
        return (lax.axis_index("head") + distance) % self.heads


def mod_kernel(quarter, units_here, seg_ref, item_ref, cond_ref, ada_ref, bias_ref, in_bias_ref, table_ref, info_ref):
    starts = [[seg_ref[row * SEQ + spot * quarter] for spot in range(4)] for row in range(2)]
    first_splits = starts[0][0] != starts[0][3]
    ids = [jnp.where(first_splits, starts[1][0], starts[0][0])] + [
        jnp.where(first_splits, starts[0][spot], starts[1][spot]) for spot in range(4)
    ]
    classes = [item_ref[one] for one in ids]
    info_ref[0] = jnp.where(first_splits, 0, 1)
    info_ref[1] = lax.axis_index("head")
    info_ref[2] = 0
    for spot in range(5):
        info_ref[3 + spot] = classes[spot]
    cond_low = silu_act(cond_ref[...].astype(jnp.float32)).astype(jnp.bfloat16)
    count = cond_low.shape[0]
    row_spot = lax.broadcasted_iota(jnp.int32, (8, count), 0)
    wanted = jnp.full((8, count), count, jnp.int32)
    for spot in range(5):
        wanted = jnp.where(row_spot == spot, classes[spot], wanted)
    hits = (lax.broadcasted_iota(jnp.int32, (8, count), 1) == wanted).astype(jnp.float32)
    rows = nn(hits.astype(jnp.bfloat16), cond_low).astype(jnp.bfloat16)
    table_ref[...] = nt(rows, ada_ref[...]) + bias_ref[...]
    table_ref[5:6, :units_here] = in_bias_ref[...]


def project_kernel(heads, quarter, info_ref, table_rel_ref, tokens_ref, weight_ref, bias_ref, attn_in_ref, projected_ref, table_ref):
    block = pl.program_id(0)
    width = tokens_ref.shape[1]
    columns = table_rel_ref.shape[2]

    @pl.when(block == 0)
    def _():
        for head in range(heads):
            spot = (head - lax.axis_index("head") + heads) % heads
            table_ref[:, head * columns : (head + 1) * columns] = table_rel_ref[spot]

    quarter_rows = tokens_ref.shape[0] // 2
    for half in range(2):
        here = slice(half * quarter_rows, (half + 1) * quarter_rows)
        spot = 2 * block + half
        row = jnp.where(spot < 4, 1 + spot % 4, 0)
        normed, _ = row_norm(tokens_ref[here, :].astype(jnp.float32))
        shift = table_ref[pl.ds(row, 1), :width]
        scale = table_ref[pl.ds(row, 1), width : 2 * width]
        attn_in = (normed * (1.0 + scale) + shift).astype(jnp.bfloat16)
        attn_in_ref[here, :] = attn_in
        projected_ref[here, :] = (nt(attn_in, weight_ref[...]) + bias_ref[...]).astype(jnp.bfloat16)


def home_row(info_ref, row, home, quarter):
    return jnp.where(row == 0, 1 + info_ref[1] * home // quarter, 0)


def enter_kernel(link, quarter, info_ref, table_ref, mixed_ref, proj_ref, tokens_ref, grad_ref, bias_ref,
                 attn_ref, stream_ref, mlp_in_ref, grad_mlp_ref, mixed_home_ref, proj_true_ref, grad_sum_ref):
    row = pl.program_id(0)
    heads = link.heads
    home, width = tokens_ref.shape[1:]
    share = width // heads
    slice_rows = proj_ref.shape[2]
    head = lax.axis_index("head")

    @pl.when(row == 0)
    def _():
        grad_sum_ref[...] = jnp.zeros_like(grad_sum_ref)
        for index in range(link.batches):
            first = index * slice_rows
            count = min(slice_rows, share - first)
            if count > 0:
                place = link.place(index)
                for spot in range(heads):
                    piece = proj_ref[place, (spot - head + heads) % heads]
                    at = spot * share + first
                    proj_true_ref[at : at + count, :] = piece[:count]

    for spot in range(heads):
        piece = mixed_ref[(spot - head + heads) % heads, 0].astype(jnp.float32).T
        mixed_home_ref[0, :, spot * share : (spot + 1) * share] = piece.astype(jnp.bfloat16)
    spot = home_row(info_ref, row, home, quarter)

    def mod(group):
        return table_ref[pl.ds(spot, 1), group * width : (group + 1) * width]

    attn = nn(mixed_home_ref[0], proj_true_ref[...]) + bias_ref[...]
    attn_ref[0] = attn
    stream = tokens_ref[0].astype(jnp.float32) + mod(2) * attn
    stream_ref[0] = stream
    normed, _ = row_norm(stream.astype(jnp.bfloat16).astype(jnp.float32))
    mlp_in_ref[0] = (normed * (1.0 + mod(4)) + mod(3)).astype(jnp.bfloat16)
    grad_mlp = (grad_ref[0].astype(jnp.float32) * mod(5)).astype(jnp.bfloat16)
    grad_mlp_ref[0] = grad_mlp
    grad_sum_ref[...] += jnp.sum(grad_mlp.astype(jnp.float32), axis=0, keepdims=True)


def expand_kernel(steps, mlp_in_ref, bias_ref, *refs):
    pieces, (hidden_ref, slope_ref) = refs[:-2], refs[-2:]
    step = pl.program_id(0)
    for spot, piece_ref in enumerate(pieces):

        @pl.when(step // steps == spot)
        def _(piece_ref=piece_ref):
            pre = nt(mlp_in_ref[...], piece_ref[...]) + bias_ref[...]
            square = pre * pre
            bent = jnp.tanh(gelu_coeff * (pre + 0.044715 * square * pre))
            half = 0.5 * (1.0 + bent)
            hidden_ref[...] = (pre * half).astype(jnp.bfloat16)
            inner = gelu_coeff * (1.0 + (3.0 * 0.044715) * square)
            slope_ref[...] = (half + 0.5 * pre * (1.0 - bent * bent) * inner).astype(jnp.bfloat16)


def contract_kernel(link, quarter, info_ref, table_ref, grad_mlp_ref, out_bias_ref, hidden_ref, slope_ref,
                    tokens_grad_ref, stream_ref, attn_ref, proj_ref, *refs):
    count = 4
    ins, outs = refs[:count], refs[count : 2 * count]
    (grad_pre_ref, pre_sum_ref, block_ref, stream_grad_ref, grad_attn_ref, grad_mixed_ref, sums_ref, attn_sum_ref,
     mlp_acc, grad_acc, in_buf, out_buf, hidden_buf, slope_buf, pre_buf, tokens_buf, stream_buf, attn_buf, proj_buf,
     piece_sems, pre_sems, late_sems) = refs[2 * count :]
    heads = link.heads
    rows, home, width = stream_ref.shape
    share = width // heads
    units = ins[0].shape[0]
    tile = UNIT_TILE

    def piece_copies(piece):
        slot = piece % 2
        columns = pl.ds(piece * units, units)
        pairs = (
            (outs[piece], out_buf.at[slot]),
            (slope_ref.at[:, columns], slope_buf.at[slot]),
            (hidden_ref.at[:, columns], hidden_buf.at[slot]),
            (ins[piece], in_buf.at[slot]),
        )
        return [
            pltpu.make_async_copy(source, target, piece_sems.at[kind, slot])
            for kind, (source, target) in enumerate(pairs)
        ]

    def pre_copy(piece):
        slot = piece % 2
        return pltpu.make_async_copy(
            pre_buf.at[slot], grad_pre_ref.at[:, pl.ds(piece * units, units)], pre_sems.at[slot]
        )

    start = pl.multiple_of(info_ref[1] * home, 8)
    late = [
        pltpu.make_async_copy(tokens_grad_ref.at[:, pl.ds(start, home), :], tokens_buf, late_sems.at[0]),
        pltpu.make_async_copy(stream_ref, stream_buf, late_sems.at[1]),
        pltpu.make_async_copy(attn_ref, attn_buf, late_sems.at[2]),
        pltpu.make_async_copy(proj_ref, proj_buf, late_sems.at[3]),
    ]
    for piece in range(2):
        for copy in piece_copies(piece):
            copy.start()
    for copy in late:
        copy.start()
    for piece in range(count):
        slot = piece % 2
        copies = piece_copies(piece)
        copies[0].wait()
        copies[1].wait()
        if piece >= 2:
            pre_copy(piece - 2).wait()
        for at in range(0, units, tile):
            here = slice(at, at + tile)
            grad_pre = nt(grad_mlp_ref[...], out_buf[slot, here, :]) * slope_buf[slot, :, here].astype(jnp.float32)
            grad_pre = grad_pre.astype(jnp.bfloat16)
            pre_buf[slot, :, here] = grad_pre
            total = jnp.sum(grad_pre.astype(jnp.float32), axis=0, keepdims=True)
            pre_sum_ref[:, piece * units + at : piece * units + at + tile] = total
        pre_copy(piece).start()
        copies[2].wait()
        copies[3].wait()
        for at in range(0, width, tile):
            here = slice(at, at + tile)
            mlp = nn(hidden_buf[slot], out_buf[slot, :, here])
            grad = nn(pre_buf[slot], in_buf[slot, :, here])
            mlp_acc[:, here] = mlp if piece == 0 else mlp_acc[:, here] + mlp
            grad_acc[:, here] = grad if piece == 0 else grad_acc[:, here] + grad
        if piece + 2 < count:
            for copy in piece_copies(piece + 2):
                copy.start()
    for copy in late:
        copy.wait()
    head = lax.axis_index("head")
    attn_sum = jnp.zeros((1, width), jnp.float32)
    for row in range(rows):
        spot = home_row(info_ref, row, home, quarter)

        def mod(group):
            return table_ref[pl.ds(spot, 1), group * width : (group + 1) * width]

        here = slice(row * home, (row + 1) * home)
        grad_out = tokens_buf[row_at(row, info_ref)].astype(jnp.float32)
        stream = stream_buf[row]
        mlp = mlp_acc[here, :] + out_bias_ref[...]
        block = (stream + mod(5) * mlp).astype(jnp.bfloat16)
        for other in range(heads):
            block_ref[(other - head + heads) % heads, row] = block[:, other * share : (other + 1) * share]
        normed, inverse = row_norm(stream.astype(jnp.bfloat16).astype(jnp.float32))
        grad_in = grad_acc[here, :]
        sums_ref[row, 1:2] = jnp.sum(grad_in, axis=0, keepdims=True)
        sums_ref[row, 2:3] = jnp.sum(grad_in * normed, axis=0, keepdims=True)
        sums_ref[row, 3:4] = jnp.sum(grad_out * mlp, axis=0, keepdims=True)
        stream_grad = grad_out + norm_back(normed, inverse, grad_in * (1.0 + mod(4)))
        stream_grad_ref[row] = stream_grad
        rounded = stream_grad.astype(jnp.bfloat16).astype(jnp.float32)
        sums_ref[row, 0:1] = jnp.sum(rounded * attn_buf[row], axis=0, keepdims=True)
        grad_attn = (rounded * mod(2)).astype(jnp.bfloat16)
        grad_attn_ref[row] = grad_attn
        attn_sum += jnp.sum(grad_attn.astype(jnp.float32), axis=0, keepdims=True)
        grad_mixed = nt(proj_buf[...], grad_attn).astype(jnp.bfloat16)
        for other in range(heads):
            grad_mixed_ref[(other - head + heads) % heads, row] = grad_mixed[other * share : (other + 1) * share]
    attn_sum_ref[...] = attn_sum
    for piece in range(count - 2, count):
        pre_copy(piece).wait()


def row_at(spot, info_ref):
    return jnp.where(spot == 0, info_ref[0], 1 - info_ref[0])


def leave_kernel(link, quarter, at_row, info_ref, table_ref, grad_ref, weight_ref, tokens_ref, stream_grad_ref,
                 shares_ref, sums_ref, term_ref):
    block = pl.program_id(0)
    heads = link.heads
    width = tokens_ref.shape[1]
    share = width // heads
    home = stream_grad_ref.shape[1]
    start = info_ref[1] * home
    for half in range(2):
        here = slice(half * quarter, (half + 1) * quarter)
        spot = 2 * block + half
        row = 1 + spot if at_row == 0 else 0
        scale = table_ref[pl.ds(row, 1), width : 2 * width]
        grad_in = nn(grad_ref[here, :], weight_ref[...])
        normed, inverse = row_norm(tokens_ref[here, :].astype(jnp.float32))
        sums_ref[half, 0:1] = jnp.sum(grad_in, axis=0, keepdims=True)
        sums_ref[half, 1:2] = jnp.sum(grad_in * normed, axis=0, keepdims=True)
        term_ref[here, :] = norm_back(normed, inverse, grad_in * (1.0 + scale))

    @pl.when(start // (2 * quarter) == block)
    def _():
        rows = pl.ds(pl.multiple_of(start % (2 * quarter), 8), home)
        term_ref[rows, :] += stream_grad_ref[0]

    turned = term_ref[...].T
    for head in range(heads):
        shares_ref[head] = turned[head * share : (head + 1) * share, :].astype(jnp.bfloat16)


def unit_grads_kernel(steps, left_ref, right_ref, *outs):
    for spot in range(4):

        @pl.when(pl.program_id(0) // steps == spot)
        def _(spot=spot):
            outs[spot][...] = tn(left_ref[...], right_ref[...]).astype(jnp.bfloat16)


def unit_grads(left, right, order=()):
    count, total = left.shape
    width = right.shape[1]
    piece = total // 4
    steps = piece // UNIT_TILE

    def spec(spot):
        return pl.BlockSpec((UNIT_TILE, width), lambda i: (jnp.clip(i - spot * steps, 0, steps - 1), 0))

    return call(
        functools.partial(unit_grads_kernel, steps),
        [shape_of((piece, width), jnp.bfloat16)] * 4,
        [pl.BlockSpec((count, UNIT_TILE), lambda i: (0, i)), whole((count, width))],
        [spec(i) for i in range(4)],
        grid=(4 * steps,),
        name="unit_grads", micros=14,
        order=order,
    )(left, right)


def place_rows_kernel(link, slices_ref, out_ref):
    rows = slices_ref.shape[1]
    for index in range(link.batches):
        count = min(rows, out_ref.shape[0] - index * rows)
        if count > 0:
            piece = slices_ref[link.place(index)].astype(jnp.float32)
            out_ref[index * rows : index * rows + count, :] = piece[:count]


def place_rows(link, slices, rows):
    width = slices.shape[2]
    tile = 384
    return call(
        functools.partial(place_rows_kernel, link),
        shape_of((rows, width), jnp.float32),
        [pl.BlockSpec(slices.shape[:2] + (tile,), lambda i: (0, 0, i))],
        pl.BlockSpec((rows, tile), lambda i: (0, i)),
        grid=(width // tile,),
        name="place_rows", micros=0,
    )(slices)


def place_columns_kernel(link, slices_ref, out_ref, rows_ref):
    rows = slices_ref.shape[1]
    for index in range(link.batches):
        rows_ref[index * rows : (index + 1) * rows, :] = slices_ref[link.place(index)].astype(jnp.float32)
    out_ref[...] = rows_ref[...].T


def place_columns(link, slices):
    batches, rows, width = slices.shape
    tile = 128
    return call(
        functools.partial(place_columns_kernel, link),
        shape_of((width, batches * rows), jnp.float32),
        [pl.BlockSpec((batches, rows, tile), lambda i: (0, 0, i))],
        pl.BlockSpec((tile, batches * rows), lambda i: (i, 0)),
        grid=(width // tile,),
        scratch=[pltpu.VMEM((batches * rows, tile), jnp.float32)],
        name="place_columns", micros=0,
    )(slices)


def lay_home_kernel(heads, info_ref, blocks_ref, out_ref):
    home = blocks_ref.shape[2]
    head = lax.axis_index("head")
    for spot in range(heads):
        for row in range(2):
            out_ref[row_at(row, info_ref), spot * home : (spot + 1) * home, :] = blocks_ref[(head - spot + heads) % heads, row]


def shards(
    tokens,
    segments,
    item_cond,
    condition,
    ada_weight,
    ada_bias,
    qkv_weight,
    qv_bias,
    proj_weight,
    proj_bias,
    in_weight,
    in_bias,
    out_weight,
    out_bias,
    cotangent,
):
    low = jnp.bfloat16
    full = jnp.float32
    heads, batches = lax.axis_size("head"), lax.axis_size("batch")
    link = Links(heads, batches)
    batch = lax.axis_index("batch")
    token_count, width = tokens.shape
    rows = token_count // SEQ
    quarter = SEQ // 4
    home = SEQ // heads
    home_count = rows * home
    share = width // heads
    heads_here = qv_bias.shape[0] // (2 * HEAD_DIM)
    qkv_here = 3 * heads_here * HEAD_DIM
    units_here = in_weight.shape[1]
    units = units_here // batches
    ada_here = ada_weight.shape[1]
    cond_count = condition.shape[0]

    ada_t = ada_weight.T
    qkv_t = qkv_weight.T
    table_part, info = call(
        functools.partial(mod_kernel, quarter, units_here),
        [shape_of((8, ada_here), full), shape_of((8,), jnp.int32)],
        [SCALARS, SCALARS] + [whole(s) for s in ((cond_count, width), (ada_here, width), (1, ada_here), (1, units_here))],
        [whole((8, ada_here)), SCALARS],
        name="modulation", micros=5,
    )(segments, item_cond, condition, ada_t, ada_bias.astype(full)[None], in_bias.astype(full)[None])
    table_rel = jnp.stack([table_part] + [link.fetch(table_part, j) for j in range(1, heads)])

    slice_rows = -(-share // (8 * batches)) * 8
    proj_pad = jnp.pad(proj_weight, ((0, slice_rows * batches - share), (0, 0)))
    in_slice = lax.dynamic_slice_in_dim(in_weight, batch * units, units, 1).T
    out_slice = lax.dynamic_slice_in_dim(out_weight, batch * units, units, 0)
    in_gathered = lax.all_gather(in_slice, "head", axis=0, tiled=True)
    out_gathered = lax.all_gather(out_slice, "head", axis=0, tiled=True)
    def tokens_block(i, info_ref):
        return (2 * row_at(i // 2, info_ref) + i % 2, 0)

    bias_pairs = qv_bias.astype(full).reshape(heads_here, 2, HEAD_DIM)
    full_bias = jnp.concatenate(
        [bias_pairs[:, :1], jnp.zeros((heads_here, 1, HEAD_DIM), full), bias_pairs[:, 1:]], axis=1
    ).reshape(1, -1)
    attn_in, projected, table = call(
        functools.partial(project_kernel, heads, quarter),
        [
            shape_of((token_count, width), low),
            shape_of((token_count, qkv_here), low),
            shape_of((8, 6 * width), full),
        ],
        [
            whole((heads, 8, ada_here)),
            pl.BlockSpec((2 * quarter, width), tokens_block),
            whole((qkv_here, width)),
            whole((1, qkv_here)),
        ],
        [
            pl.BlockSpec((2 * quarter, width), lambda i, _: (i, 0)),
            pl.BlockSpec((2 * quarter, qkv_here), lambda i, _: (i, 0)),
            whole((8, 6 * width)),
        ],
        grid=(2 * rows,),
        prefetch=1,
        name="project", micros=13,
    )(info, table_rel, tokens, qkv_t, full_bias)
    projected = projected.reshape(rows, SEQ, qkv_here)
    proj_slice = hold(lax.dynamic_slice_in_dim(proj_pad, batch * slice_rows, slice_rows, 0), table_rel)
    proj_rel = jnp.stack(
        [proj_slice] + [hold(link.fetch(proj_slice, j), projected) for j in range(1, heads)]
    )[None]
    mixed = None
    log_totals = []
    for row in range(rows):
        order = [in_gathered] if row == 1 else []
        mixed, log_total = attend(projected, row, mixed, heads_here, quarter, heads, order)
        log_totals.append(log_total)
        if row < link.levels:
            proj_rel = jnp.concatenate([proj_rel, hold(link.link_swap(proj_rel, row), log_total)], axis=0)
        if row == 0:
            in_gathered = hold(in_gathered, log_total)
    in_held = link.gather_levels(in_gathered, [log_totals[1]])
    for level in range(rows, link.levels):
        proj_rel = jnp.concatenate([proj_rel, link.link_swap(proj_rel, level)], axis=0)
    proj_all = jnp.concatenate([proj_rel, link.core_swap(proj_rel)], axis=0)
    out_gathered = hold(out_gathered, in_held[0])
    mixed = hold(mixed, out_gathered, proj_all, micros=20)
    mixed_all = jnp.stack([mixed[0]] + [link.fetch(mixed[j], j) for j in range(1, heads)])

    out_held = link.gather_levels(out_gathered)
    out_pieces = out_held + [link.core_swap(piece) for piece in out_held]
    tokens_rows = tokens.reshape(rows, SEQ, width)
    grad_rows = cotangent.reshape(rows, SEQ, width)
    home_spec = pl.BlockSpec((1, home, width), lambda i, info_ref: (row_at(i, info_ref), info_ref[1], 0))
    row_spec = pl.BlockSpec((1, home, width), lambda i, _: (i, 0, 0))
    attn, stream, mlp_in, grad_mlp, mixed_home, proj_true, grad_sum = call(
        functools.partial(enter_kernel, link, quarter),
        [
            shape_of((rows, home, width), full),
            shape_of((rows, home, width), full),
            shape_of((rows, home, width), low),
            shape_of((rows, home, width), low),
            shape_of((rows, home, width), low),
            shape_of((width, width), low),
            shape_of((1, width), full),
        ],
        [
            whole((8, 6 * width)),
            pl.BlockSpec((heads, 1, share, home), lambda i, _: (0, i, 0, 0)),
            whole(proj_all.shape),
            home_spec,
            home_spec,
            whole((1, width)),
        ],
        [row_spec] * 5 + [whole((width, width)), whole((1, width))],
        grid=(rows,),
        prefetch=1,
        name="enter", micros=9,
        order=[out_held[0]],
    )(info, table, mixed_all, proj_all, tokens_rows, grad_rows, proj_bias.astype(full)[None])

    in_held[1] = hold(in_held[1], mlp_in)
    in_pieces = in_held + [link.core_swap(piece) for piece in in_held]
    mlp_in = mlp_in.reshape(home_count, width)
    grad_mlp = grad_mlp.reshape(home_count, width)
    in_bias_all = table[5].reshape(heads, -1)[:, :units_here]
    in_bias_all = in_bias_all.reshape(heads, batches, units)
    in_bias_all = link.by_owner(in_bias_all.transpose(1, 0, 2)).reshape(1, -1)
    piece_rows = in_pieces[0].shape[0]
    unit_count = 4 * piece_rows
    steps = piece_rows // UNIT_TILE

    def piece_spec(spot):
        return pl.BlockSpec((UNIT_TILE, width), lambda i, *_: (jnp.clip(i - spot * steps, 0, steps - 1), 0))

    tile_spec = pl.BlockSpec((home_count, UNIT_TILE), lambda i, *_: (0, i))
    bias_spec = pl.BlockSpec((1, UNIT_TILE), lambda i, *_: (0, i))
    hidden, slope = call(
        functools.partial(expand_kernel, 1),
        [shape_of((home_count, unit_count), low)] * 2,
        [whole((home_count, width)), pl.BlockSpec((1, piece_rows), lambda i: (0, i))]
        + [whole((piece_rows, width))] * 4,
        [pl.BlockSpec((home_count, piece_rows), lambda i: (0, i))] * 2,
        grid=(4,),
        name="expand", micros=20,
        order=[out_held[0]],
    )(mlp_in, in_bias_all, *in_pieces)

    out_parts = unit_grads(hidden, grad_mlp, order=[out_pieces[2]])

    stay = pl.BlockSpec((rows, home, width), lambda *_: (0, 0, 0))
    by_head = whole((heads, rows, home, share))
    grad_pre, pre_sum, block_home, stream_grad, grad_attn, grad_mixed, home_sums, attn_sum = call(
        functools.partial(contract_kernel, link, quarter),
        [
            shape_of((home_count, unit_count), low),
            shape_of((1, unit_count), full),
            shape_of((heads, rows, home, share), low),
            shape_of((rows, home, width), full),
            shape_of((rows, home, width), low),
            shape_of((heads, rows, share, home), low),
            shape_of((rows, 4, width), full),
            shape_of((1, width), full),
        ],
        [SCALARS, whole((8, 6 * width)), whole((home_count, width)), whole((1, width))]
        + [pl.BlockSpec(memory_space=pl.ANY)] * 14,
        [
            pl.BlockSpec(memory_space=pl.ANY),
            whole((1, unit_count)),
            by_head,
            stay,
            stay,
            whole((heads, rows, share, home)),
            whole((rows, 4, width)),
            whole((1, width)),
        ],
        scratch=[
            pltpu.VMEM((home_count, width), full),
            pltpu.VMEM((home_count, width), full),
            pltpu.VMEM((2, piece_rows, width), low),
            pltpu.VMEM((2, piece_rows, width), low),
            pltpu.VMEM((2, home_count, piece_rows), low),
            pltpu.VMEM((2, home_count, piece_rows), low),
            pltpu.VMEM((2, home_count, piece_rows), low),
            pltpu.VMEM((rows, home, width), low),
            pltpu.VMEM((rows, home, width), full),
            pltpu.VMEM((rows, home, width), full),
            pltpu.VMEM((width, width), low),
            pltpu.SemaphoreType.DMA((4, 2)),
            pltpu.SemaphoreType.DMA((2,)),
            pltpu.SemaphoreType.DMA((4,)),
        ],
        name="contract", micros=44,
        order=[out_parts[0]],
    )(info, table, grad_mlp, out_bias.astype(full)[None], hidden, slope, grad_rows, stream, attn, proj_true,
      *in_pieces, *out_pieces)
    mixed_sends = [link.send(grad_mixed[j], j) for j in range(1, heads)]
    out_near = link.reduce_cores(out_parts, grad_pre)
    out_sum = link.reduce_first(out_near)
    in_parts = unit_grads(grad_pre, mlp_in, order=[out_near[1]])
    grad_mixed = jnp.stack([grad_mixed[0]] + [hold(piece, in_parts[0]) for piece in mixed_sends])
    out_slice = link.reduce_rest(out_sum)
    in_near = link.reduce_cores(in_parts, grad_mixed)
    proj_grad = tn(mixed_home.reshape(home_count, width), grad_attn.reshape(home_count, width)).astype(low)

    def head_sum(values):
        return lax.psum_scatter(values, "head", scatter_dimension=0, tiled=True)

    out_blocks = out_slice.reshape(heads, units, width)

    def out_block(distance):
        return lax.dynamic_index_in_dim(out_blocks, link.at_head(distance), 0, keepdims=False)

    out_more = [link.send(out_block(j), j) for j in range(1, heads)]
    grad_rows_low = []
    block_sums = []
    shares = None
    for row in range(rows):
        grad_row = attend_back(
            projected, row, log_totals[row], grad_mixed, heads_here, quarter, heads,
            [] if row == 0 else [sums_row, out_slice],
        )[0]
        order = list(in_near) + [out_sum]
        if row == 1:
            in_sum = link.reduce_first(in_near, grad_row)
            order = [in_sum]
        earlier = [] if shares is None else [shares]
        kernel = functools.partial(leave_kernel, link, quarter, row)
        shares, sums_row = call(
            kernel if row == 0 else lambda *refs: kernel(*refs[:6], *refs[7:]),
            [shape_of((heads, share, token_count), low), shape_of((4, 2, width), full)],
            [
                whole((8, 6 * width)),
                pl.BlockSpec((2 * quarter, qkv_here), lambda i, _: (i, 0)),
                whole((qkv_here, width)),
                pl.BlockSpec((2 * quarter, width), lambda i, info_ref, row=row: tokens_block(i + 2 * row, info_ref)),
                pl.BlockSpec((1, home, width), lambda i, _, row=row: (row, 0, 0)),
            ]
            + [pl.BlockSpec(memory_space=pl.ANY)] * len(earlier),
            [
                pl.BlockSpec((heads, share, 2 * quarter), lambda i, _, row=row: (0, 0, i + 2 * row)),
                pl.BlockSpec((2, 2, width), lambda i, _: (i, 0, 0)),
            ],
            grid=(2,),
            prefetch=1,
            scratch=[pltpu.VMEM((2 * quarter, width), full)],
            name="leave", micros=9,
            aliases={6: 0} if earlier else {},
            order=order,
        )(info, table, grad_row, qkv_t, tokens, stream_grad, *earlier)
        grad_rows_low.append(grad_row)
        block_sums.append(sums_row)
    in_slice = link.reduce_rest(in_sum, sums_row)
    out_slice_sum = out_block(0).astype(full)
    for more in out_more:
        out_slice_sum = out_slice_sum + hold(more, grad_rows_low[1]).astype(full)
    out_slice_sum = out_slice_sum.astype(low)
    grad_projected = hold(jnp.concatenate(grad_rows_low, axis=0), in_slice)

    in_slice_sum = head_sum(in_slice)
    shares = head_sum(hold(shares, in_slice_sum))[0]
    tokens_grad = jnp.where(
        info[0] == 0, shares, jnp.concatenate([shares[:, SEQ:], shares[:, :SEQ]], axis=1)
    ).T

    block_home = hold(block_home, grad_mixed)
    block_home = jnp.stack(
        [block_home[0]] + [hold(link.send(block_home[j], j), sums_row) for j in range(1, heads)]
    )
    block_out = call(
        functools.partial(lay_home_kernel, heads),
        shape_of((rows, SEQ, share), low),
        [whole((heads, rows, home, share))],
        whole((rows, SEQ, share)),
        prefetch=1,
        name="lay_home", micros=0,
        order=[sums_row],
    )(info, block_home).reshape(token_count, share)

    home_quarter = lax.axis_index("head") * home // quarter
    seg_spots = lax.broadcasted_iota(jnp.int32, (5, 1), 0)

    def seg_home(sums):
        placed = jnp.where(seg_spots == 1 + home_quarter, sums[0][None, :], 0.0)
        return jnp.where(seg_spots == 0, sums[1][None, :], placed)

    seg_blocks = jnp.concatenate([jnp.sum(block_sums[1], axis=0, keepdims=True), block_sums[0]], axis=0)
    seg_grads = jnp.concatenate(
        [seg_blocks[:, 0], seg_blocks[:, 1]] + [seg_home(home_sums[:, i]) for i in range(4)], axis=1
    )
    in_bias_part = link.by_index(pre_sum.reshape(batches, heads, units)).transpose(1, 0, 2)
    bias_grads = jnp.concatenate(
        [
            in_bias_part.reshape(heads, -1),
            grad_sum.reshape(heads, -1),
            attn_sum.reshape(heads, -1),
        ],
        axis=1,
    ).reshape(1, -1)
    sent = jnp.concatenate([seg_grads, bias_grads, jnp.zeros((2, 6 * width), full)], axis=0)
    sent = hold(sent, in_slice).reshape(8, heads, ada_here)

    def sent_block(distance):
        return lax.dynamic_index_in_dim(sent, link.at_head(distance), 1, keepdims=False)

    held = sent_block(0)
    for j in range(1, heads):
        held = held + link.send(sent_block(j), j)
    column_sums = jnp.sum(grad_projected.astype(full), axis=0).reshape(heads_here, 3, HEAD_DIM)
    qv_bias_part = jnp.concatenate([column_sums[:, :1], column_sums[:, 2:]], axis=1).reshape(-1)
    held = jnp.concatenate(
        [
            held[:6],
            jnp.pad(qv_bias_part, (0, ada_here - qv_bias_part.shape[0]))[None],
            jnp.pad(info[3:].astype(full), (0, ada_here - 5))[None],
        ],
        axis=0,
    )
    all_held = hold(link.gather_batch(held[None]), in_slice_sum)
    all_classes = (all_held[:, 7, :5] + 0.5).astype(jnp.int32).reshape(-1)
    class_hits = (
        lax.broadcasted_iota(jnp.int32, (cond_count, 1), 0) == all_classes[None, :]
    ).astype(full)
    mod_low = jnp.dot(
        class_hits,
        all_held[:, :5].reshape(-1, ada_here),
        precision=lax.Precision.HIGHEST,
        preferred_element_type=full,
    ).astype(low)
    bias_total = jnp.sum(all_held[:, 5], axis=0)
    qv_bias_grad = jnp.sum(all_held[:, 6, : qv_bias.shape[0]], axis=0)
    in_bias_grad = bias_total[:units_here]
    cond_f = condition.astype(full)
    ada_weight_grad = tn(mod_low, silu_act(cond_f).astype(low)).T
    ada_bias_grad = jnp.sum(mod_low.astype(full), axis=0)
    cond_part = nn(mod_low, ada_t)
    shared = jnp.pad(bias_total[units_here:], (0, width - 2 * share))
    last = jnp.concatenate([cond_part, shared[None], jnp.zeros((7, width), full)]).astype(low)
    last = jnp.stack([last] + [link.fetch(last, j) for j in range(1, heads)]).astype(full)
    cond_total = jnp.sum(last[:, :cond_count], axis=0)
    condition_grad = jax.vjp(silu_act, cond_f)[1](cond_total)[0]
    shared = last[:, cond_count]
    head = lax.axis_index("head")
    shared = jnp.concatenate(
        [lax.dynamic_index_in_dim(shared, (j - head + heads) % heads, 0) for j in range(heads)]
    )
    out_bias_grad = shared[:, :share].reshape(-1)
    proj_bias_grad = shared[:, share : 2 * share].reshape(-1)

    out_weight_grad = place_rows(link, link.gather_batch(out_slice_sum[None]), units_here)
    in_weight_grad = place_columns(link, link.gather_batch(in_slice_sum[None]))

    qkv_rows = -(-qkv_here // (16 * batches)) * 16
    qkv_grad = tn(grad_projected, attn_in.reshape(token_count, width)).astype(low)
    qkv_grad = jnp.pad(qkv_grad, ((0, qkv_rows * batches - qkv_here), (0, 0))).reshape(batches, qkv_rows, width)
    proj_grad = jnp.pad(
        proj_grad.reshape(heads, share, width), ((0, 0), (0, slice_rows * batches - share), (0, 0))
    ).reshape(heads, batches, slice_rows, width)
    proj_grad = proj_grad.transpose(1, 0, 2, 3).reshape(batches, heads * slice_rows, width)
    both = link.by_owner(jnp.concatenate([qkv_grad, proj_grad], axis=1))
    both = both.reshape(2, 2, -1, width)
    got = [link.core_swap(piece) for piece in both[1]]
    both = [(mine.astype(full) + more.astype(full)).astype(low) for mine, more in zip(both[0], got)]
    both = link.reduce_rest(link.reduce_first(both))
    proj_blocks = both[qkv_rows:].reshape(heads, slice_rows, width)

    def proj_block(distance):
        return lax.dynamic_index_in_dim(proj_blocks, link.at_head(distance), 0, keepdims=False)

    proj_sum = proj_block(0).astype(full)
    for j in range(1, heads):
        proj_sum = proj_sum + link.send(proj_block(j), j).astype(full)
    both = jnp.concatenate([both[:qkv_rows], proj_sum.astype(low)], axis=0)
    both = link.gather_batch(both[None])
    qkv_weight_grad = place_rows(link, both[:, :qkv_rows], qkv_here).T
    proj_weight_grad = place_rows(link, both[:, qkv_rows:], share)

    return (
        block_out,
        tokens_grad,
        condition_grad,
        ada_weight_grad,
        ada_bias_grad,
        qkv_weight_grad,
        qv_bias_grad,
        proj_weight_grad,
        proj_bias_grad,
        in_weight_grad,
        in_bias_grad,
        out_weight_grad,
        out_bias_grad,
    )


def solution(mesh):
    in_specs = (
        P("batch", None),
        P("batch"),
        P(),
        P(),
        P(None, "head"),
        P("head"),
        P(None, "head"),
        P("head"),
        P("head", None),
        P(),
        P(None, "head"),
        P("head"),
        P("head", None),
        P(),
        P("batch", None),
    )
    out_specs = (
        P("batch", "head"),
        P("batch", "head"),
        P(),
        P(None, "head"),
        P("head"),
        P(None, "head"),
        P("head"),
        P("head", None),
        P(),
        P(None, "head"),
        P("head"),
        P("head", None),
        P(),
    )
    return jax.shard_map(shards, mesh=mesh, in_specs=in_specs, out_specs=out_specs, check_vma=False)
```

```python
import functools
import math

import jax
import jax.numpy as jnp
from jax import lax
from jax.experimental import pallas as pl
from jax.experimental.pallas import tpu as pltpu
from jax.sharding import PartitionSpec as P

HEAD_DIM = 72
SEQ = 1024
LOG2E = 1.4426950408889634
KEY_SCALE = 1.0 / math.sqrt(HEAD_DIM)


def nt(a, b):
    return lax.dot_general(a, b, (((1,), (1,)), ((), ())), preferred_element_type=jnp.float32)


def nn(a, b):
    return lax.dot_general(a, b, (((1,), (0,)), ((), ())), preferred_element_type=jnp.float32)


def attend_kernel(heads, chunk, groups, split, proj_ref, mixed_ref, lse_ref):
    seq = proj_ref.shape[1]
    home = seq // groups
    group = lax.axis_index("head")
    width = 3 * HEAD_DIM
    key_count = chunk if split else seq

    def part(head, start):
        at = head * width
        rows = pl.ds(start, chunk)
        keys = pl.ds(start if split else 0, key_count)
        queries = proj_ref[0, rows, at : at + HEAD_DIM]
        key_rows = proj_ref[0, keys, at + HEAD_DIM : at + 2 * HEAD_DIM]
        value_rows = proj_ref[0, keys, at + 2 * HEAD_DIM : at + 3 * HEAD_DIM]
        scores = nt(key_rows, queries)
        peak = jnp.max(scores, axis=0, keepdims=True)
        weights = jnp.exp2((scores - peak) * (KEY_SCALE * LOG2E))
        total = jnp.sum(weights, axis=0, keepdims=True)
        mixed_t = nn(value_rows.T, weights.astype(jnp.bfloat16)) / total
        lse_ref[0, head : head + 1, rows] = peak * (KEY_SCALE * LOG2E) + jnp.log2(total)
        return mixed_t

    def step(index, _):
        start = pl.multiple_of(index * chunk, chunk)
        outs = [part(head, start) for head in range(heads)]
        outs = jnp.concatenate(outs, axis=0).astype(jnp.bfloat16)
        for spot in range(chunk // home):
            target = index * (chunk // home) + spot
            mixed_ref[(group - target + groups) % groups, 0] = outs[:, spot * home : (spot + 1) * home]
        return 0

    lax.fori_loop(0, seq // chunk, step, 0, unroll=True)


def attend(projected, row, mixed, heads, chunk, groups, order):
    seq, width = projected.shape[1:]
    split = row == 0
    kernel = functools.partial(attend_kernel, heads, chunk, groups, split)
    earlier = [] if mixed is None else [mixed]
    return call(
        kernel if mixed is None else lambda p, _, *refs: kernel(p, *refs),
        [
            shape_of((groups, 2, heads * HEAD_DIM, seq // groups), jnp.bfloat16),
            shape_of((1, heads, seq), jnp.float32),
        ],
        [pl.BlockSpec((1, seq, width), lambda i: (row, 0, 0))] + [pl.BlockSpec(memory_space=pl.ANY)] * len(earlier),
        [
            pl.BlockSpec((groups, 1, heads * HEAD_DIM, seq // groups), lambda i: (0, row, 0, 0)),
            pl.BlockSpec((1, heads, seq), lambda i: (0, 0, 0)),
        ],
        grid=(1,),
        name="attend_split" if split else "attend_whole",
        micros=6 if split else 16,
        order=order,
        aliases={} if mixed is None else {1: 0},
    )(projected, *earlier)


def attend_back_kernel(heads, chunk, groups, split, proj_ref, lse_ref, pieces_ref, out_ref, dk_ref, dv_ref, grad_ref):
    seq = proj_ref.shape[1]
    home = seq // groups
    group = lax.axis_index("head")
    width = 3 * HEAD_DIM
    key_count = chunk if split else seq
    for spot in range(groups):
        piece = pieces_ref[(group - spot + groups) % groups, 0].astype(jnp.float32).T
        grad_ref[spot * home : (spot + 1) * home, :] = piece.astype(jnp.bfloat16)

    def part(head, start, key_turned=None):
        at = head * width
        rows = pl.ds(start, chunk)
        keys = pl.ds(start if split else 0, key_count)
        queries = proj_ref[0, rows, at : at + HEAD_DIM]
        key_rows = proj_ref[0, keys, at + HEAD_DIM : at + 2 * HEAD_DIM]
        value_rows = proj_ref[0, keys, at + 2 * HEAD_DIM : at + 3 * HEAD_DIM]
        key_turned = key_rows.T if key_turned is None else key_turned
        grads = grad_ref[rows, head * HEAD_DIM : (head + 1) * HEAD_DIM]
        scores = nt(key_rows, queries)
        probs = jnp.exp2(scores * (KEY_SCALE * LOG2E) - lse_ref[0, head : head + 1, rows])
        grad_probs = nt(value_rows, grads)
        inner = jnp.sum(probs * grad_probs, axis=0, keepdims=True)
        grad_raw = (probs * (grad_probs - inner) * KEY_SCALE).astype(jnp.bfloat16)
        grad_values = nn(probs.astype(jnp.bfloat16), grads)
        grad_keys = nn(grad_raw, queries)
        grad_queries = nn(key_turned, grad_raw).T
        return grad_queries, grad_keys, grad_values

    if not split:
        for head in range(heads):
            at = head * width
            dk_ref[...] = jnp.zeros_like(dk_ref)
            dv_ref[...] = jnp.zeros_like(dv_ref)
            key_turned = proj_ref[0, :, at + HEAD_DIM : at + 2 * HEAD_DIM].T

            def step(index, _, head=head, at=at, key_turned=key_turned):
                start = pl.multiple_of(index * chunk, chunk)
                dq, dk, dv = part(head, start, key_turned)
                out_ref[0, pl.ds(start, chunk), at : at + HEAD_DIM] = dq.astype(jnp.bfloat16)
                dk_ref[...] += dk
                dv_ref[...] += dv
                return 0

            lax.fori_loop(0, seq // chunk, step, 0, unroll=True)
            both = jnp.concatenate([dk_ref[...], dv_ref[...]], axis=1).astype(jnp.bfloat16)
            out_ref[0, :, at + HEAD_DIM : at + 3 * HEAD_DIM] = both
    else:

        def step(index, _):
            start = pl.multiple_of(index * chunk, chunk)
            outs = [t for head in range(heads) for t in part(head, start)]
            out_ref[0, pl.ds(start, chunk), :] = jnp.concatenate(outs, axis=1).astype(jnp.bfloat16)
            return 0

        lax.fori_loop(0, seq // chunk, step, 0, unroll=True)


def attend_back(projected, row, lse, grads, heads, chunk, groups, order):
    seq, width = projected.shape[1:]
    split = row == 0

    return call(
        functools.partial(attend_back_kernel, heads, chunk, groups, split),
        shape_of((1, seq, width), jnp.bfloat16),
        [
            pl.BlockSpec((1, seq, width), lambda i: (row, 0, 0)),
            pl.BlockSpec((1, heads, seq), lambda i: (0, 0, 0)),
            pl.BlockSpec((groups, 1, heads * HEAD_DIM, seq // groups), lambda i: (0, row, 0, 0)),
        ],
        pl.BlockSpec((1, seq, width), lambda i: (0, 0, 0)),
        grid=(1,),
        scratch=[pltpu.VMEM((seq, HEAD_DIM), jnp.float32)] * 2
        + [pltpu.VMEM((seq, heads * HEAD_DIM), jnp.bfloat16)],
        name="attend_back_split" if split else "attend_back_whole",
        micros=8 if split else 24,
        order=order,
    )(projected, lse, grads)


norm_eps = 1e-06
gelu_coeff = 0.7978845608028654
VMEM_BYTES = 58 * 1024 * 1024
UNIT_TILE = 384


def tn(left_side, right_side):
    return lax.dot_general(
        left_side, right_side, (((0,), (0,)), ((), ())), preferred_element_type=jnp.float32
    )


def row_norm(values):
    center = jnp.mean(values, axis=-1, keepdims=True)
    shifted = values - center
    spread = jnp.mean(shifted * shifted, axis=-1, keepdims=True)
    inverse = lax.rsqrt(spread + norm_eps)
    return (shifted * inverse, inverse)


def norm_back(normed, inverse, grad_normed):
    first_mean = jnp.mean(grad_normed, axis=-1, keepdims=True)
    second_mean = jnp.mean(grad_normed * normed, axis=-1, keepdims=True)
    return inverse * (grad_normed - first_mean - normed * second_mean)


def silu_act(values):
    return values / (1.0 + jnp.exp(-values))


def weight_of(micros):
    return pl.CostEstimate(flops=int(micros * 2.2e10), bytes_accessed=int(micros * 6.6e7), transcendentals=0)


def call(kernel, out_shape, in_specs, out_specs, grid=(), prefetch=0, scratch=(), name=None, micros=1, order=(), aliases={}):
    first = prefetch + len(in_specs)

    def ordered(*refs):
        kernel(*refs[:first], *refs[first + len(order) :])

    run = pl.pallas_call(
        ordered if order else kernel,
        grid_spec=pltpu.PrefetchScalarGridSpec(
            num_scalar_prefetch=prefetch,
            grid=grid,
            in_specs=list(in_specs) + [pl.BlockSpec(memory_space=pl.ANY)] * len(order),
            out_specs=out_specs,
            scratch_shapes=scratch,
        ),
        out_shape=out_shape,
        input_output_aliases=aliases,
        compiler_params=pltpu.CompilerParams(vmem_limit_bytes=VMEM_BYTES),
        cost_estimate=weight_of(micros),
        name=name,
    )
    return lambda *arrays: run(*arrays, *order)


def hold(values, *order, micros=0):
    run = pl.pallas_call(
        lambda *refs: None,
        in_specs=[pl.BlockSpec(memory_space=pl.ANY)] * (1 + len(order)),
        out_specs=pl.BlockSpec(memory_space=pl.ANY),
        out_shape=shape_of(values.shape, values.dtype),
        input_output_aliases={0: 0},
        cost_estimate=weight_of(micros),
        name="hold",
    )
    return run(values, *order)


def whole(shape):
    return pl.BlockSpec(shape, lambda *_: (0,) * len(shape))


SCALARS = pl.BlockSpec(memory_space=pltpu.SMEM)
shape_of = jax.ShapeDtypeStruct


class Links:
    def __init__(self, heads, batches):
        self.heads = heads
        self.batches = batches
        bits = batches.bit_length() - 1
        self.levels = bits - 1
        first = list(range(bits - 1, 0, -1))
        self.orders = (first, first[1:] + first[:1])

    def fetch(self, values, distance):
        count = self.heads
        return lax.ppermute(values, "head", [((i + distance) % count, i) for i in range(count)])

    def send(self, values, distance):
        count = self.heads
        return lax.ppermute(values, "head", [(i, (i + distance) % count) for i in range(count)])

    def head_swap(self, values, bit):
        return lax.ppermute(values, "head", [(i, i ^ (1 << bit)) for i in range(self.heads)])

    def head_cube(self, values, orders):
        for bit in range(self.heads.bit_length() - 1):
            more = self.head_swap(values, bit)
            if bit < len(orders):
                more = hold(more, orders[bit])
            values = jnp.concatenate([values, more], axis=0)
        return values

    def head_gather(self, values):
        return [values] + [self.fetch(values, distance) for distance in range(1, self.heads)]

    def by_head(self, pieces):
        values = pieces[0]
        rows = values.shape[0]
        held = jnp.zeros((self.heads * rows,) + values.shape[1:], values.dtype)
        for distance in range(self.heads):
            held = lax.dynamic_update_slice_in_dim(held, pieces[distance], self.at_head(distance) * rows, 0)
        return held

    def core_swap(self, values):
        return lax.ppermute(values, "batch", [(i, i ^ 1) for i in range(self.batches)])

    def link_swap(self, values, level):
        pairs = [(i, i ^ (1 << self.orders[i & 1][level])) for i in range(self.batches)]
        return lax.ppermute(values, "batch", pairs)

    def owner(self, spot):
        batch = lax.axis_index("batch")
        half = spot >> self.levels
        masks = [
            sum(1 << order[level] for level in range(self.levels) if spot >> level & 1)
            for order in self.orders
        ]
        mask = jnp.where(batch % 2 == half, masks[0], masks[1])
        return (batch ^ half) ^ mask

    def place(self, index):
        batch = lax.axis_index("batch")
        way = batch ^ index
        half = way & 1
        spots = [
            sum(((way >> order[level]) & 1) << level for level in range(self.levels))
            for order in self.orders
        ]
        return (half << self.levels) + jnp.where((batch & 1) == half, spots[0], spots[1])

    def gather_levels(self, values, order=()):
        pieces = [values]
        for level in range(self.levels):
            joined = pieces[0] if level == 0 else jnp.concatenate(pieces, axis=0)
            more = self.link_swap(joined, level)
            if level == 0 and order:
                more = hold(more, *order)
            pieces = [joined, more]
        return pieces

    def gather_batch(self, values):
        own = jnp.concatenate(self.gather_levels(values), axis=0)
        return jnp.concatenate([own, self.core_swap(own)], axis=0)

    def reduce_cores(self, pieces, *order):
        sums = []
        for mine, other in zip(pieces[:2], pieces[2:]):
            more = self.core_swap(other)
            if order:
                more = hold(more, *order)
            sums.append((mine.astype(jnp.float32) + more.astype(jnp.float32)).astype(jnp.bfloat16))
        return sums

    def reduce_first(self, kept, *order):
        more = self.link_swap(kept[1], self.levels - 1)
        if order:
            more = hold(more, *order)
        return (kept[0].astype(jnp.float32) + more.astype(jnp.float32)).astype(jnp.bfloat16)

    def reduce_rest(self, total, *order):
        for level in reversed(range(self.levels - 1)):
            half = total.shape[0] // 2
            more = self.link_swap(total[half:], level)
            if order:
                more = hold(more, *order)
                order = ()
            total = (total[:half].astype(jnp.float32) + more.astype(jnp.float32)).astype(jnp.bfloat16)
        return total

    def by_owner(self, values):
        return jnp.concatenate(
            [lax.dynamic_index_in_dim(values, self.owner(i), 0) for i in range(self.batches)]
        )

    def by_index(self, values):
        return jnp.concatenate(
            [lax.dynamic_index_in_dim(values, self.place(i), 0) for i in range(self.batches)]
        )

    def at_head(self, distance):
        return (lax.axis_index("head") + distance) % self.heads


def mod_kernel(quarter, units_here, seg_ref, item_ref, cond_ref, ada_ref, bias_ref, in_bias_ref, table_ref, info_ref):
    starts = [[seg_ref[row * SEQ + spot * quarter] for spot in range(4)] for row in range(2)]
    first_splits = starts[0][0] != starts[0][3]
    ids = [jnp.where(first_splits, starts[1][0], starts[0][0])] + [
        jnp.where(first_splits, starts[0][spot], starts[1][spot]) for spot in range(4)
    ]
    classes = [item_ref[one] for one in ids]
    info_ref[0] = jnp.where(first_splits, 0, 1)
    info_ref[1] = lax.axis_index("head")
    info_ref[2] = 0
    for spot in range(5):
        info_ref[3 + spot] = classes[spot]
    cond_low = silu_act(cond_ref[...].astype(jnp.float32)).astype(jnp.bfloat16)
    count = cond_low.shape[0]
    row_spot = lax.broadcasted_iota(jnp.int32, (8, count), 0)
    wanted = jnp.full((8, count), count, jnp.int32)
    for spot in range(5):
        wanted = jnp.where(row_spot == spot, classes[spot], wanted)
    hits = (lax.broadcasted_iota(jnp.int32, (8, count), 1) == wanted).astype(jnp.float32)
    rows = nn(hits.astype(jnp.bfloat16), cond_low).astype(jnp.bfloat16)
    table_ref[...] = nt(rows, ada_ref[...]) + bias_ref[...]
    table_ref[5:6, :units_here] = in_bias_ref[...]


def project_kernel(heads, quarter, info_ref, table_rel_ref, tokens_ref, weight_ref, bias_ref, attn_in_ref, projected_ref, table_ref):
    block = pl.program_id(0)
    width = tokens_ref.shape[1]
    columns = table_rel_ref.shape[2]

    @pl.when(block == 0)
    def _():
        for head in range(heads):
            spot = (head - lax.axis_index("head") + heads) % heads
            table_ref[:, head * columns : (head + 1) * columns] = table_rel_ref[spot]

    quarter_rows = tokens_ref.shape[0] // 2
    for half in range(2):
        here = slice(half * quarter_rows, (half + 1) * quarter_rows)
        spot = 2 * block + half
        row = jnp.where(spot < 4, 1 + spot % 4, 0)
        normed, _ = row_norm(tokens_ref[here, :].astype(jnp.float32))
        shift = table_ref[pl.ds(row, 1), :width]
        scale = table_ref[pl.ds(row, 1), width : 2 * width]
        attn_in = (normed * (1.0 + scale) + shift).astype(jnp.bfloat16)
        attn_in_ref[here, :] = attn_in
        projected_ref[here, :] = (nt(attn_in, weight_ref[...]) + bias_ref[...]).astype(jnp.bfloat16)


def home_row(info_ref, row, home, quarter):
    return jnp.where(row == 0, 1 + info_ref[1] * home // quarter, 0)


def enter_kernel(link, quarter, info_ref, table_ref, mixed_ref, proj_ref, tokens_ref, grad_ref, bias_ref,
                 attn_ref, stream_ref, mlp_in_ref, grad_mlp_ref, mixed_home_ref, proj_true_ref, grad_sum_ref):
    row = pl.program_id(0)
    heads = link.heads
    home, width = tokens_ref.shape[1:]
    share = width // heads
    slice_rows = proj_ref.shape[2]
    head = lax.axis_index("head")

    @pl.when(row == 0)
    def _():
        grad_sum_ref[...] = jnp.zeros_like(grad_sum_ref)
        for index in range(link.batches):
            first = index * slice_rows
            count = min(slice_rows, share - first)
            if count > 0:
                place = link.place(index)
                for spot in range(heads):
                    piece = proj_ref[place, (spot - head + heads) % heads]
                    at = spot * share + first
                    proj_true_ref[at : at + count, :] = piece[:count]

    for spot in range(heads):
        piece = mixed_ref[(spot - head + heads) % heads, 0].astype(jnp.float32).T
        mixed_home_ref[0, :, spot * share : (spot + 1) * share] = piece.astype(jnp.bfloat16)
    spot = home_row(info_ref, row, home, quarter)

    def mod(group):
        return table_ref[pl.ds(spot, 1), group * width : (group + 1) * width]

    attn = nn(mixed_home_ref[0], proj_true_ref[...]) + bias_ref[...]
    attn_ref[0] = attn
    stream = tokens_ref[0].astype(jnp.float32) + mod(2) * attn
    stream_ref[0] = stream
    normed, _ = row_norm(stream.astype(jnp.bfloat16).astype(jnp.float32))
    mlp_in_ref[0] = (normed * (1.0 + mod(4)) + mod(3)).astype(jnp.bfloat16)
    grad_mlp = (grad_ref[0].astype(jnp.float32) * mod(5)).astype(jnp.bfloat16)
    grad_mlp_ref[0] = grad_mlp
    grad_sum_ref[...] += jnp.sum(grad_mlp.astype(jnp.float32), axis=0, keepdims=True)


def expand_kernel(steps, mlp_in_ref, bias_ref, *refs):
    pieces, (hidden_ref, slope_ref) = refs[:-2], refs[-2:]
    step = pl.program_id(0)
    for spot, piece_ref in enumerate(pieces):

        @pl.when(step // steps == spot)
        def _(piece_ref=piece_ref):
            pre = nt(mlp_in_ref[...], piece_ref[...]) + bias_ref[...]
            square = pre * pre
            bent = jnp.tanh(gelu_coeff * (pre + 0.044715 * square * pre))
            half = 0.5 * (1.0 + bent)
            hidden_ref[...] = (pre * half).astype(jnp.bfloat16)
            inner = gelu_coeff * (1.0 + (3.0 * 0.044715) * square)
            slope_ref[...] = (half + 0.5 * pre * (1.0 - bent * bent) * inner).astype(jnp.bfloat16)


def contract_kernel(link, quarter, info_ref, table_ref, grad_mlp_ref, out_bias_ref, hidden_ref, slope_ref,
                    tokens_grad_ref, stream_ref, attn_ref, proj_ref, *refs):
    count = 4
    ins, outs = refs[:count], refs[count : 2 * count]
    (grad_pre_ref, pre_sum_ref, block_ref, stream_grad_ref, grad_attn_ref, grad_mixed_ref, sums_ref, attn_sum_ref,
     mlp_acc, grad_acc, in_buf, out_buf, hidden_buf, slope_buf, pre_buf, tokens_buf, stream_buf, attn_buf, proj_buf,
     piece_sems, pre_sems, late_sems) = refs[2 * count :]
    heads = link.heads
    rows, home, width = stream_ref.shape
    share = width // heads
    units = ins[0].shape[0]
    tile = UNIT_TILE

    def piece_copies(piece):
        slot = piece % 2
        columns = pl.ds(piece * units, units)
        pairs = (
            (outs[piece], out_buf.at[slot]),
            (slope_ref.at[:, columns], slope_buf.at[slot]),
            (hidden_ref.at[:, columns], hidden_buf.at[slot]),
            (ins[piece], in_buf.at[slot]),
        )
        return [
            pltpu.make_async_copy(source, target, piece_sems.at[kind, slot])
            for kind, (source, target) in enumerate(pairs)
        ]

    def pre_copy(piece):
        slot = piece % 2
        return pltpu.make_async_copy(
            pre_buf.at[slot], grad_pre_ref.at[:, pl.ds(piece * units, units)], pre_sems.at[slot]
        )

    start = pl.multiple_of(info_ref[1] * home, 8)
    late = [
        pltpu.make_async_copy(tokens_grad_ref.at[:, pl.ds(start, home), :], tokens_buf, late_sems.at[0]),
        pltpu.make_async_copy(stream_ref, stream_buf, late_sems.at[1]),
        pltpu.make_async_copy(attn_ref, attn_buf, late_sems.at[2]),
        pltpu.make_async_copy(proj_ref, proj_buf, late_sems.at[3]),
    ]
    for piece in range(2):
        for copy in piece_copies(piece):
            copy.start()
    for copy in late:
        copy.start()
    for piece in range(count):
        slot = piece % 2
        copies = piece_copies(piece)
        copies[0].wait()
        copies[1].wait()
        if piece >= 2:
            pre_copy(piece - 2).wait()
        for at in range(0, units, tile):
            here = slice(at, at + tile)
            grad_pre = nt(grad_mlp_ref[...], out_buf[slot, here, :]) * slope_buf[slot, :, here].astype(jnp.float32)
            grad_pre = grad_pre.astype(jnp.bfloat16)
            pre_buf[slot, :, here] = grad_pre
            total = jnp.sum(grad_pre.astype(jnp.float32), axis=0, keepdims=True)
            pre_sum_ref[:, piece * units + at : piece * units + at + tile] = total
        pre_copy(piece).start()
        copies[2].wait()
        copies[3].wait()
        for at in range(0, width, tile):
            here = slice(at, at + tile)
            mlp = nn(hidden_buf[slot], out_buf[slot, :, here])
            grad = nn(pre_buf[slot], in_buf[slot, :, here])
            mlp_acc[:, here] = mlp if piece == 0 else mlp_acc[:, here] + mlp
            grad_acc[:, here] = grad if piece == 0 else grad_acc[:, here] + grad
        if piece + 2 < count:
            for copy in piece_copies(piece + 2):
                copy.start()
    for copy in late:
        copy.wait()
    head = lax.axis_index("head")
    attn_sum = jnp.zeros((1, width), jnp.float32)
    for row in range(rows):
        spot = home_row(info_ref, row, home, quarter)

        def mod(group):
            return table_ref[pl.ds(spot, 1), group * width : (group + 1) * width]

        here = slice(row * home, (row + 1) * home)
        grad_out = tokens_buf[row_at(row, info_ref)].astype(jnp.float32)
        stream = stream_buf[row]
        mlp = mlp_acc[here, :] + out_bias_ref[...]
        block = (stream + mod(5) * mlp).T.astype(jnp.bfloat16)
        for other in range(heads):
            block_ref[(other - head + heads) % heads, row] = block[other * share : (other + 1) * share]
        normed, inverse = row_norm(stream.astype(jnp.bfloat16).astype(jnp.float32))
        grad_in = grad_acc[here, :]
        sums_ref[row, 1:2] = jnp.sum(grad_in, axis=0, keepdims=True)
        sums_ref[row, 2:3] = jnp.sum(grad_in * normed, axis=0, keepdims=True)
        sums_ref[row, 3:4] = jnp.sum(grad_out * mlp, axis=0, keepdims=True)
        stream_grad = grad_out + norm_back(normed, inverse, grad_in * (1.0 + mod(4)))
        stream_grad_ref[row] = stream_grad
        rounded = stream_grad.astype(jnp.bfloat16).astype(jnp.float32)
        sums_ref[row, 0:1] = jnp.sum(rounded * attn_buf[row], axis=0, keepdims=True)
        grad_attn = (rounded * mod(2)).astype(jnp.bfloat16)
        grad_attn_ref[row] = grad_attn
        attn_sum += jnp.sum(grad_attn.astype(jnp.float32), axis=0, keepdims=True)
        grad_mixed = nt(proj_buf[...], grad_attn).astype(jnp.bfloat16)
        for other in range(heads):
            grad_mixed_ref[(other - head + heads) % heads, row] = grad_mixed[other * share : (other + 1) * share]
    attn_sum_ref[...] = attn_sum
    for piece in range(count - 2, count):
        pre_copy(piece).wait()


def row_at(spot, info_ref):
    return jnp.where(spot == 0, info_ref[0], 1 - info_ref[0])


def leave_kernel(link, quarter, at_row, info_ref, table_ref, grad_ref, weight_ref, tokens_ref, stream_grad_ref,
                 shares_ref, sums_ref, term_ref):
    block = pl.program_id(0)
    heads = link.heads
    width = tokens_ref.shape[1]
    share = width // heads
    home = stream_grad_ref.shape[1]
    start = info_ref[1] * home
    for half in range(2):
        here = slice(half * quarter, (half + 1) * quarter)
        spot = 2 * block + half
        row = 1 + spot if at_row == 0 else 0
        scale = table_ref[pl.ds(row, 1), width : 2 * width]
        grad_in = nn(grad_ref[here, :], weight_ref[...])
        normed, inverse = row_norm(tokens_ref[here, :].astype(jnp.float32))
        sums_ref[half, 0:1] = jnp.sum(grad_in, axis=0, keepdims=True)
        sums_ref[half, 1:2] = jnp.sum(grad_in * normed, axis=0, keepdims=True)
        term_ref[here, :] = norm_back(normed, inverse, grad_in * (1.0 + scale))

    @pl.when(start // (2 * quarter) == block)
    def _():
        rows = pl.ds(pl.multiple_of(start % (2 * quarter), 8), home)
        term_ref[rows, :] += stream_grad_ref[0]

    turned = term_ref[...].T
    for head in range(heads):
        shares_ref[head] = turned[head * share : (head + 1) * share, :].astype(jnp.bfloat16)


def unit_grads_kernel(steps, left_ref, right_ref, *outs):
    for spot in range(4):

        @pl.when(pl.program_id(0) // steps == spot)
        def _(spot=spot):
            outs[spot][...] = tn(left_ref[...], right_ref[...]).astype(jnp.bfloat16)


def unit_grads(left, right, order=()):
    count, total = left.shape
    width = right.shape[1]
    piece = total // 4
    steps = piece // UNIT_TILE

    def spec(spot):
        return pl.BlockSpec((UNIT_TILE, width), lambda i: (jnp.clip(i - spot * steps, 0, steps - 1), 0))

    return call(
        functools.partial(unit_grads_kernel, steps),
        [shape_of((piece, width), jnp.bfloat16)] * 4,
        [pl.BlockSpec((count, UNIT_TILE), lambda i: (0, i)), whole((count, width))],
        [spec(i) for i in range(4)],
        grid=(4 * steps,),
        name="unit_grads", micros=14,
        order=order,
    )(left, right)


def place_rows_kernel(link, slices_ref, out_ref):
    rows = slices_ref.shape[1]
    for index in range(link.batches):
        count = min(rows, out_ref.shape[0] - index * rows)
        if count > 0:
            piece = slices_ref[link.place(index)].astype(jnp.float32)
            out_ref[index * rows : index * rows + count, :] = piece[:count]


def place_rows(link, slices, rows):
    width = slices.shape[2]
    tile = 384
    return call(
        functools.partial(place_rows_kernel, link),
        shape_of((rows, width), jnp.float32),
        [pl.BlockSpec(slices.shape[:2] + (tile,), lambda i: (0, 0, i))],
        pl.BlockSpec((rows, tile), lambda i: (0, i)),
        grid=(width // tile,),
        name="place_rows", micros=0,
    )(slices)


def place_columns_kernel(link, slices_ref, out_ref, rows_ref):
    rows = slices_ref.shape[1]
    for index in range(link.batches):
        rows_ref[index * rows : (index + 1) * rows, :] = slices_ref[link.place(index)].astype(jnp.float32)
    out_ref[...] = rows_ref[...].T


def place_columns(link, slices):
    batches, rows, width = slices.shape
    tile = 128
    return call(
        functools.partial(place_columns_kernel, link),
        shape_of((width, batches * rows), jnp.float32),
        [pl.BlockSpec((batches, rows, tile), lambda i: (0, 0, i))],
        pl.BlockSpec((tile, batches * rows), lambda i: (i, 0)),
        grid=(width // tile,),
        scratch=[pltpu.VMEM((batches * rows, tile), jnp.float32)],
        name="place_columns", micros=0,
    )(slices)


def lay_home_kernel(heads, info_ref, blocks_ref, out_ref):
    home = blocks_ref.shape[3]
    head = lax.axis_index("head")
    for split_row in range(2):

        @pl.when(info_ref[0] == split_row)
        def _(split_row=split_row):
            for spot in range(heads):
                for row in range(2):
                    at = (split_row ^ row) * SEQ + spot * home
                    out_ref[:, at : at + home] = blocks_ref[(head - spot + heads) % heads, row]


def shards(
    tokens,
    segments,
    item_cond,
    condition,
    ada_weight,
    ada_bias,
    qkv_weight,
    qv_bias,
    proj_weight,
    proj_bias,
    in_weight,
    in_bias,
    out_weight,
    out_bias,
    cotangent,
):
    low = jnp.bfloat16
    full = jnp.float32
    heads, batches = lax.axis_size("head"), lax.axis_size("batch")
    link = Links(heads, batches)
    batch = lax.axis_index("batch")
    token_count, width = tokens.shape
    rows = token_count // SEQ
    quarter = SEQ // 4
    home = SEQ // heads
    home_count = rows * home
    share = width // heads
    heads_here = qv_bias.shape[0] // (2 * HEAD_DIM)
    qkv_here = 3 * heads_here * HEAD_DIM
    units_here = in_weight.shape[1]
    units = units_here // batches
    ada_here = ada_weight.shape[1]
    cond_count = condition.shape[0]

    ada_t = ada_weight.T
    qkv_t = qkv_weight.T
    table_part, info = call(
        functools.partial(mod_kernel, quarter, units_here),
        [shape_of((8, ada_here), full), shape_of((8,), jnp.int32)],
        [SCALARS, SCALARS] + [whole(s) for s in ((cond_count, width), (ada_here, width), (1, ada_here), (1, units_here))],
        [whole((8, ada_here)), SCALARS],
        name="modulation", micros=5,
    )(segments, item_cond, condition, ada_t, ada_bias.astype(full)[None], in_bias.astype(full)[None])
    table_rel = jnp.stack([table_part] + [link.fetch(table_part, j) for j in range(1, heads)])

    slice_rows = -(-share // (8 * batches)) * 8
    proj_pad = jnp.pad(proj_weight, ((0, slice_rows * batches - share), (0, 0)))
    in_slice = lax.dynamic_slice_in_dim(in_weight, batch * units, units, 1).T
    out_slice = lax.dynamic_slice_in_dim(out_weight, batch * units, units, 0)
    in_gathered = lax.all_gather(in_slice, "head", axis=0, tiled=True)
    out_gathered = lax.all_gather(out_slice, "head", axis=0, tiled=True)
    def tokens_block(i, info_ref):
        return (2 * row_at(i // 2, info_ref) + i % 2, 0)

    bias_pairs = qv_bias.astype(full).reshape(heads_here, 2, HEAD_DIM)
    full_bias = jnp.concatenate(
        [bias_pairs[:, :1], jnp.zeros((heads_here, 1, HEAD_DIM), full), bias_pairs[:, 1:]], axis=1
    ).reshape(1, -1)
    attn_in, projected, table = call(
        functools.partial(project_kernel, heads, quarter),
        [
            shape_of((token_count, width), low),
            shape_of((token_count, qkv_here), low),
            shape_of((8, 6 * width), full),
        ],
        [
            whole((heads, 8, ada_here)),
            pl.BlockSpec((2 * quarter, width), tokens_block),
            whole((qkv_here, width)),
            whole((1, qkv_here)),
        ],
        [
            pl.BlockSpec((2 * quarter, width), lambda i, _: (i, 0)),
            pl.BlockSpec((2 * quarter, qkv_here), lambda i, _: (i, 0)),
            whole((8, 6 * width)),
        ],
        grid=(2 * rows,),
        prefetch=1,
        name="project", micros=13,
    )(info, table_rel, tokens, qkv_t, full_bias)
    projected = projected.reshape(rows, SEQ, qkv_here)
    proj_slice = hold(lax.dynamic_slice_in_dim(proj_pad, batch * slice_rows, slice_rows, 0), table_rel)
    proj_rel = jnp.stack(
        [proj_slice] + [hold(link.fetch(proj_slice, j), projected) for j in range(1, heads)]
    )[None]
    mixed = None
    log_totals = []
    for row in range(rows):
        order = [in_gathered] if row == 1 else []
        mixed, log_total = attend(projected, row, mixed, heads_here, quarter, heads, order)
        log_totals.append(log_total)
        if row < link.levels:
            proj_rel = jnp.concatenate([proj_rel, hold(link.link_swap(proj_rel, row), log_total)], axis=0)
        if row == 0:
            in_gathered = hold(in_gathered, log_total)
    in_held = link.gather_levels(in_gathered, [log_totals[1]])
    for level in range(rows, link.levels):
        proj_rel = jnp.concatenate([proj_rel, link.link_swap(proj_rel, level)], axis=0)
    proj_all = jnp.concatenate([proj_rel, link.core_swap(proj_rel)], axis=0)
    out_gathered = hold(out_gathered, in_held[0])
    mixed = hold(mixed, out_gathered, proj_all, micros=20)
    mixed_all = jnp.stack([mixed[0]] + [link.fetch(mixed[j], j) for j in range(1, heads)])

    out_held = link.gather_levels(out_gathered)
    out_pieces = out_held + [link.core_swap(piece) for piece in out_held]
    tokens_rows = tokens.reshape(rows, SEQ, width)
    grad_rows = cotangent.reshape(rows, SEQ, width)
    home_spec = pl.BlockSpec((1, home, width), lambda i, info_ref: (row_at(i, info_ref), info_ref[1], 0))
    row_spec = pl.BlockSpec((1, home, width), lambda i, _: (i, 0, 0))
    attn, stream, mlp_in, grad_mlp, mixed_home, proj_true, grad_sum = call(
        functools.partial(enter_kernel, link, quarter),
        [
            shape_of((rows, home, width), full),
            shape_of((rows, home, width), full),
            shape_of((rows, home, width), low),
            shape_of((rows, home, width), low),
            shape_of((rows, home, width), low),
            shape_of((width, width), low),
            shape_of((1, width), full),
        ],
        [
            whole((8, 6 * width)),
            pl.BlockSpec((heads, 1, share, home), lambda i, _: (0, i, 0, 0)),
            whole(proj_all.shape),
            home_spec,
            home_spec,
            whole((1, width)),
        ],
        [row_spec] * 5 + [whole((width, width)), whole((1, width))],
        grid=(rows,),
        prefetch=1,
        name="enter", micros=9,
        order=[out_held[0]],
    )(info, table, mixed_all, proj_all, tokens_rows, grad_rows, proj_bias.astype(full)[None])

    in_held[1] = hold(in_held[1], mlp_in)
    in_pieces = in_held + [link.core_swap(piece) for piece in in_held]
    mlp_in = mlp_in.reshape(home_count, width)
    grad_mlp = grad_mlp.reshape(home_count, width)
    in_bias_all = table[5].reshape(heads, -1)[:, :units_here]
    in_bias_all = in_bias_all.reshape(heads, batches, units)
    in_bias_all = link.by_owner(in_bias_all.transpose(1, 0, 2)).reshape(1, -1)
    piece_rows = in_pieces[0].shape[0]
    unit_count = 4 * piece_rows
    steps = piece_rows // UNIT_TILE

    def piece_spec(spot):
        return pl.BlockSpec((UNIT_TILE, width), lambda i, *_: (jnp.clip(i - spot * steps, 0, steps - 1), 0))

    tile_spec = pl.BlockSpec((home_count, UNIT_TILE), lambda i, *_: (0, i))
    bias_spec = pl.BlockSpec((1, UNIT_TILE), lambda i, *_: (0, i))
    hidden, slope = call(
        functools.partial(expand_kernel, 1),
        [shape_of((home_count, unit_count), low)] * 2,
        [whole((home_count, width)), pl.BlockSpec((1, piece_rows), lambda i: (0, i))]
        + [whole((piece_rows, width))] * 4,
        [pl.BlockSpec((home_count, piece_rows), lambda i: (0, i))] * 2,
        grid=(4,),
        name="expand", micros=20,
        order=[out_held[0]],
    )(mlp_in, in_bias_all, *in_pieces)

    out_parts = unit_grads(hidden, grad_mlp, order=[out_pieces[2]])

    stay = pl.BlockSpec((rows, home, width), lambda *_: (0, 0, 0))
    by_head = whole((heads, rows, home, share))
    grad_pre, pre_sum, block_home, stream_grad, grad_attn, grad_mixed, home_sums, attn_sum = call(
        functools.partial(contract_kernel, link, quarter),
        [
            shape_of((home_count, unit_count), low),
            shape_of((1, unit_count), full),
            shape_of((heads, rows, share, home), low),
            shape_of((rows, home, width), full),
            shape_of((rows, home, width), low),
            shape_of((heads, rows, share, home), low),
            shape_of((rows, 4, width), full),
            shape_of((1, width), full),
        ],
        [SCALARS, whole((8, 6 * width)), whole((home_count, width)), whole((1, width))]
        + [pl.BlockSpec(memory_space=pl.ANY)] * 14,
        [
            pl.BlockSpec(memory_space=pl.ANY),
            whole((1, unit_count)),
            whole((heads, rows, share, home)),
            stay,
            stay,
            whole((heads, rows, share, home)),
            whole((rows, 4, width)),
            whole((1, width)),
        ],
        scratch=[
            pltpu.VMEM((home_count, width), full),
            pltpu.VMEM((home_count, width), full),
            pltpu.VMEM((2, piece_rows, width), low),
            pltpu.VMEM((2, piece_rows, width), low),
            pltpu.VMEM((2, home_count, piece_rows), low),
            pltpu.VMEM((2, home_count, piece_rows), low),
            pltpu.VMEM((2, home_count, piece_rows), low),
            pltpu.VMEM((rows, home, width), low),
            pltpu.VMEM((rows, home, width), full),
            pltpu.VMEM((rows, home, width), full),
            pltpu.VMEM((width, width), low),
            pltpu.SemaphoreType.DMA((4, 2)),
            pltpu.SemaphoreType.DMA((2,)),
            pltpu.SemaphoreType.DMA((4,)),
        ],
        name="contract", micros=44,
        order=[out_parts[0]],
    )(info, table, grad_mlp, out_bias.astype(full)[None], hidden, slope, grad_rows, stream, attn, proj_true,
      *in_pieces, *out_pieces)
    mixed_sends = [link.send(grad_mixed[j], j) for j in range(1, heads)]
    out_near = link.reduce_cores(out_parts, grad_pre)
    out_sum = link.reduce_first(out_near)
    in_parts = unit_grads(grad_pre, mlp_in, order=[out_near[1]])
    grad_mixed = jnp.stack([grad_mixed[0]] + [hold(piece, in_parts[0]) for piece in mixed_sends])
    out_slice = link.reduce_rest(out_sum)
    in_near = link.reduce_cores(in_parts, grad_mixed)
    proj_grad = tn(mixed_home.reshape(home_count, width), grad_attn.reshape(home_count, width)).astype(low)

    def head_sum(values):
        return lax.psum_scatter(values, "head", scatter_dimension=0, tiled=True)

    out_blocks = out_slice.reshape(heads, units, width)

    def out_block(distance):
        return lax.dynamic_index_in_dim(out_blocks, link.at_head(distance), 0, keepdims=False)

    out_more = [link.send(out_block(j), j) for j in range(1, heads)]
    grad_rows_low = []
    block_sums = []
    shares = None
    for row in range(rows):
        grad_row = attend_back(
            projected, row, log_totals[row], grad_mixed, heads_here, quarter, heads,
            [] if row == 0 else [sums_row, out_slice],
        )[0]
        order = list(in_near) + [out_sum]
        if row == 1:
            in_sum = link.reduce_first(in_near, grad_row)
            order = [in_sum]
        earlier = [] if shares is None else [shares]
        kernel = functools.partial(leave_kernel, link, quarter, row)
        shares, sums_row = call(
            kernel if row == 0 else lambda *refs: kernel(*refs[:6], *refs[7:]),
            [shape_of((heads, share, token_count), low), shape_of((4, 2, width), full)],
            [
                whole((8, 6 * width)),
                pl.BlockSpec((2 * quarter, qkv_here), lambda i, _: (i, 0)),
                whole((qkv_here, width)),
                pl.BlockSpec((2 * quarter, width), lambda i, info_ref, row=row: tokens_block(i + 2 * row, info_ref)),
                pl.BlockSpec((1, home, width), lambda i, _, row=row: (row, 0, 0)),
            ]
            + [pl.BlockSpec(memory_space=pl.ANY)] * len(earlier),
            [
                pl.BlockSpec((heads, share, 2 * quarter), lambda i, _, row=row: (0, 0, i + 2 * row)),
                pl.BlockSpec((2, 2, width), lambda i, _: (i, 0, 0)),
            ],
            grid=(2,),
            prefetch=1,
            scratch=[pltpu.VMEM((2 * quarter, width), full)],
            name="leave", micros=9,
            aliases={6: 0} if earlier else {},
            order=order,
        )(info, table, grad_row, qkv_t, tokens, stream_grad, *earlier)
        grad_rows_low.append(grad_row)
        block_sums.append(sums_row)
    in_slice = link.reduce_rest(in_sum, sums_row)
    out_slice_sum = out_block(0).astype(full)
    for more in out_more:
        out_slice_sum = out_slice_sum + hold(more, grad_rows_low[1]).astype(full)
    out_slice_sum = out_slice_sum.astype(low)
    grad_projected = hold(jnp.concatenate(grad_rows_low, axis=0), in_slice)

    in_slice_sum = head_sum(in_slice)
    shares = head_sum(hold(shares, in_slice_sum))[0]
    tokens_grad = jnp.where(
        info[0] == 0, shares, jnp.concatenate([shares[:, SEQ:], shares[:, :SEQ]], axis=1)
    ).T

    block_home = hold(block_home, grad_mixed)
    block_home = jnp.stack(
        [block_home[0]] + [hold(link.send(block_home[j], j), sums_row) for j in range(1, heads)]
    )
    block_out = call(
        functools.partial(lay_home_kernel, heads),
        shape_of((share, token_count), low),
        [whole((heads, rows, share, home))],
        whole((share, token_count)),
        prefetch=1,
        name="lay_home", micros=0,
        order=[sums_row],
    )(info, block_home).T

    home_quarter = lax.axis_index("head") * home // quarter
    seg_spots = lax.broadcasted_iota(jnp.int32, (5, 1), 0)

    def seg_home(sums):
        placed = jnp.where(seg_spots == 1 + home_quarter, sums[0][None, :], 0.0)
        return jnp.where(seg_spots == 0, sums[1][None, :], placed)

    seg_blocks = jnp.concatenate([jnp.sum(block_sums[1], axis=0, keepdims=True), block_sums[0]], axis=0)
    seg_grads = jnp.concatenate(
        [seg_blocks[:, 0], seg_blocks[:, 1]] + [seg_home(home_sums[:, i]) for i in range(4)], axis=1
    )
    in_bias_part = link.by_index(pre_sum.reshape(batches, heads, units)).transpose(1, 0, 2)
    bias_grads = jnp.concatenate(
        [
            in_bias_part.reshape(heads, -1),
            grad_sum.reshape(heads, -1),
            attn_sum.reshape(heads, -1),
        ],
        axis=1,
    ).reshape(1, -1)
    sent = jnp.concatenate([seg_grads, bias_grads, jnp.zeros((2, 6 * width), full)], axis=0)
    sent = hold(sent, in_slice).reshape(8, heads, ada_here)

    def sent_block(distance):
        return lax.dynamic_index_in_dim(sent, link.at_head(distance), 1, keepdims=False)

    held = sent_block(0)
    for j in range(1, heads):
        held = held + link.send(sent_block(j), j)
    column_sums = jnp.sum(grad_projected.astype(full), axis=0).reshape(heads_here, 3, HEAD_DIM)
    qv_bias_part = jnp.concatenate([column_sums[:, :1], column_sums[:, 2:]], axis=1).reshape(-1)
    held = jnp.concatenate(
        [
            held[:6],
            jnp.pad(qv_bias_part, (0, ada_here - qv_bias_part.shape[0]))[None],
            jnp.pad(info[3:].astype(full), (0, ada_here - 5))[None],
        ],
        axis=0,
    )
    all_held = hold(link.gather_batch(held[None]), in_slice_sum)
    all_classes = (all_held[:, 7, :5] + 0.5).astype(jnp.int32).reshape(-1)
    class_hits = (
        lax.broadcasted_iota(jnp.int32, (cond_count, 1), 0) == all_classes[None, :]
    ).astype(full)
    mod_low = jnp.dot(
        class_hits,
        all_held[:, :5].reshape(-1, ada_here),
        precision=lax.Precision.HIGHEST,
        preferred_element_type=full,
    ).astype(low)
    bias_total = jnp.sum(all_held[:, 5], axis=0)
    qv_bias_grad = jnp.sum(all_held[:, 6, : qv_bias.shape[0]], axis=0)
    in_bias_grad = bias_total[:units_here]
    cond_f = condition.astype(full)
    ada_weight_grad = tn(mod_low, silu_act(cond_f).astype(low)).T
    ada_bias_grad = jnp.sum(mod_low.astype(full), axis=0)
    cond_part = nn(mod_low, ada_t)
    shared = jnp.pad(bias_total[units_here:], (0, width - 2 * share))
    last = jnp.concatenate([cond_part, shared[None], jnp.zeros((7, width), full)]).astype(low)
    last = jnp.stack([last] + [link.fetch(last, j) for j in range(1, heads)]).astype(full)
    cond_total = jnp.sum(last[:, :cond_count], axis=0)
    condition_grad = jax.vjp(silu_act, cond_f)[1](cond_total)[0]
    shared = last[:, cond_count]
    head = lax.axis_index("head")
    shared = jnp.concatenate(
        [lax.dynamic_index_in_dim(shared, (j - head + heads) % heads, 0) for j in range(heads)]
    )
    out_bias_grad = shared[:, :share].reshape(-1)
    proj_bias_grad = shared[:, share : 2 * share].reshape(-1)

    out_weight_grad = place_rows(link, link.gather_batch(out_slice_sum[None]), units_here)
    in_weight_grad = place_columns(link, link.gather_batch(in_slice_sum[None]))

    qkv_rows = -(-qkv_here // (16 * batches)) * 16
    qkv_grad = tn(grad_projected, attn_in.reshape(token_count, width)).astype(low)
    qkv_grad = jnp.pad(qkv_grad, ((0, qkv_rows * batches - qkv_here), (0, 0))).reshape(batches, qkv_rows, width)
    proj_grad = jnp.pad(
        proj_grad.reshape(heads, share, width), ((0, 0), (0, slice_rows * batches - share), (0, 0))
    ).reshape(heads, batches, slice_rows, width)
    proj_grad = proj_grad.transpose(1, 0, 2, 3).reshape(batches, heads * slice_rows, width)
    both = link.by_owner(jnp.concatenate([qkv_grad, proj_grad], axis=1))
    both = both.reshape(2, 2, -1, width)
    got = [link.core_swap(piece) for piece in both[1]]
    both = [(mine.astype(full) + more.astype(full)).astype(low) for mine, more in zip(both[0], got)]
    both = link.reduce_rest(link.reduce_first(both))
    proj_blocks = both[qkv_rows:].reshape(heads, slice_rows, width)

    def proj_block(distance):
        return lax.dynamic_index_in_dim(proj_blocks, link.at_head(distance), 0, keepdims=False)

    proj_sum = proj_block(0).astype(full)
    for j in range(1, heads):
        proj_sum = proj_sum + link.send(proj_block(j), j).astype(full)
    both = jnp.concatenate([both[:qkv_rows], proj_sum.astype(low)], axis=0)
    both = link.gather_batch(both[None])
    qkv_weight_grad = place_rows(link, both[:, :qkv_rows], qkv_here).T
    proj_weight_grad = place_rows(link, both[:, qkv_rows:], share)

    return (
        block_out,
        tokens_grad,
        condition_grad,
        ada_weight_grad,
        ada_bias_grad,
        qkv_weight_grad,
        qv_bias_grad,
        proj_weight_grad,
        proj_bias_grad,
        in_weight_grad,
        in_bias_grad,
        out_weight_grad,
        out_bias_grad,
    )


def solution(mesh):
    in_specs = (
        P("batch", None),
        P("batch"),
        P(),
        P(),
        P(None, "head"),
        P("head"),
        P(None, "head"),
        P("head"),
        P("head", None),
        P(),
        P(None, "head"),
        P("head"),
        P("head", None),
        P(),
        P("batch", None),
    )
    out_specs = (
        P("batch", "head"),
        P("batch", "head"),
        P(),
        P(None, "head"),
        P("head"),
        P(None, "head"),
        P("head"),
        P("head", None),
        P(),
        P(None, "head"),
        P("head"),
        P("head", None),
        P(),
    )
    return jax.shard_map(shards, mesh=mesh, in_specs=in_specs, out_specs=out_specs, check_vma=False)
```
